32 devices in a mesh: dp: 32 (over z, y, x, core).
Axes of the slice: x: 2, y: 2, z: 4, core: 2. Of those that a mesh axis runs over, the one named last changes fastest.
Arguments:
- tokens: bfloat16 [32768, 576], P('dp'), may hold values from -6 to 6
- positions: int32 [32768], P('dp'), may hold values from 0 to 1023, as said below
- cotangent: bfloat16 [32768, 576], P('dp'), may hold values from -6 to 6
- w_query: float32 [331776], P('dp'), may hold values from -0.5 to 0.5
- w_key: float32 [110592], P('dp'), may hold values from -0.25 to 0.25
- w_value: float32 [110592], P('dp'), may hold values from -0.25 to 0.25
- w_out: float32 [331776], P('dp'), may hold values from -1.5 to 1.5
- w_gate: float32 [884736], P('dp'), may hold values from -0.25 to 0.25
- w_up: float32 [884736], P('dp'), may hold values from -0.25 to 0.25
- w_down: float32 [884736], P('dp'), may hold values from -0.15625 to 0.15625
- gains: float32 [1152], P('dp'), may hold values from 0.5 to 1.5
- m_query: float32 [331776], P('dp'), may hold values from -512 to 512
- m_key: float32 [110592], P('dp'), may hold values from -512 to 512
- m_value: float32 [110592], P('dp'), may hold values from -512 to 512
- m_out: float32 [331776], P('dp'), may hold values from -512 to 512
- m_gate: float32 [884736], P('dp'), may hold values from -512 to 512
- m_up: float32 [884736], P('dp'), may hold values from -512 to 512
- m_down: float32 [884736], P('dp'), may hold values from -512 to 512
- m_gains: float32 [1152], P('dp'), may hold values from -512 to 512
Outputs:
- block_out: float32 [32768, 576], P('dp')
- input_grad: float32 [32768, 576], P('dp')
- new_m_query: float32 [331776], P('dp')
- new_m_key: float32 [110592], P('dp')
- new_m_value: float32 [110592], P('dp')
- new_m_out: float32 [331776], P('dp')
- new_m_gate: float32 [884736], P('dp')
- new_m_up: float32 [884736], P('dp')
- new_m_down: float32 [884736], P('dp')
- new_m_gains: float32 [1152], P('dp')
- new_query: float32 [331776], P('dp')
- new_key: float32 [110592], P('dp')
- new_value: float32 [110592], P('dp')
- new_out: float32 [331776], P('dp')
- new_gate: float32 [884736], P('dp')
- new_up: float32 [884736], P('dp')
- new_down: float32 [884736], P('dp')
- new_gains: float32 [1152], P('dp')
- grad_query: float32 [331776], P('dp')
- grad_key: float32 [110592], P('dp')
- grad_value: float32 [110592], P('dp')
- grad_out: float32 [331776], P('dp')
- grad_gate: float32 [884736], P('dp')
- grad_up: float32 [884736], P('dp')
- grad_down: float32 [884736], P('dp')
- grad_gains: float32 [1152], P('dp')
The draws below stay inside these ranges and needn't reach their ends.
Inputs may be any that keep to these rules, and one draw needn't show every extreme that they name: `positions`: each sequence of 1024 tokens is one or more documents laid end to end; a token's position counts from the start of its document; in every draw some sequence is a single document.
All inputs are finite; a program needn't handle non-finite values.
Results may differ from the reference program's by a relative error of at most 0.013.
The reference program's roundings to bfloat16 on the way count: a program that leaves them out, or rounds other values in their place, can miss the bound.
Values may be sent and summed in bfloat16 or wider, within the bound.
A program may use at most 192 MiB of HBM per device.

```python
import math
import jax
import jax.numpy as jnp
from jax import lax

HEADS = 9
KV_HEADS = 3
HEAD_DIM = 64
D = 576
KVD = 192
FF = 1536
SEQ = 1024
NS_ITERS = 5
TOKENS = 32768


def draw_positions(key, part):
    key = jax.random.fold_in(key, 11)
    count = TOKENS // SEQ
    breaks = jax.random.randint(jax.random.fold_in(key, 1), (count, SEQ), 0, max(SEQ // 16, 2)) == 0
    single = jax.random.randint(jax.random.fold_in(key, 2), (), 0, count)
    rows = jnp.arange(count, dtype=jnp.int32)[:, None]
    index = jnp.broadcast_to(jnp.arange(SEQ, dtype=jnp.int32)[None, :], (count, SEQ))
    breaks = jnp.logical_and(breaks, rows != single)
    breaks = jnp.logical_or(breaks, index == 0)
    marks = jnp.where(breaks, index, 0)
    last = lax.cummax(marks, axis=1)
    return (index - last).reshape(-1).astype(jnp.int32)


def shard_levels(key, extent, cuts, smallest, top_value):
    loudness = 1.0
    for position, shards_of in cuts:
        draws = jax.random.uniform(jax.random.fold_in(jax.random.fold_in(key, 6), position), (shards_of,), jnp.float32, smallest / len(cuts), top_value / len(cuts))
        loudness = loudness * jnp.repeat(jnp.exp(draws), extent[position] // shards_of).reshape((-1,) + (1,) * (len(extent) - 1 - position))
    return loudness


def scatter_about(rng, extent, spread, most, cuts=(), held_as=jnp.bfloat16):
    drawn = jax.random.normal(rng, extent, jnp.float32) * spread
    if len(cuts) > 0:
        drawn = shard_levels(rng, extent, cuts, -0.22, 0.18) * drawn
    return jnp.clip(drawn, min=-most, max=most).astype(held_as)


def setup_inputs(seed: int = 0) -> dict:
    keys = jax.random.split(jax.random.key(seed), 20)
    return {
        "tokens": scatter_about(keys[0], (TOKENS, D), 1.0, 6.0, ((0, 32),)),
        "positions": draw_positions(jax.random.fold_in(keys[19], 71), 0),
        "cotangent": scatter_about(keys[2], (TOKENS, D), 1.0, 6.0, ((0, 32),)),
        "w_query": scatter_about(keys[3], (D * D,), (D // 4) ** -0.5, 0.5, ((0, 32),), jnp.float32),
        "w_key": scatter_about(keys[4], (D * KVD,), D ** -0.5, 0.25, ((0, 32),), jnp.float32),
        "w_value": scatter_about(keys[5], (D * KVD,), D ** -0.5, 0.25, ((0, 32),), jnp.float32),
        "w_out": scatter_about(keys[6], (D * D,), (D // 32) ** -0.5, 1.5, ((0, 32),), jnp.float32),
        "w_gate": scatter_about(keys[7], (D * FF,), D ** -0.5, 0.25, ((0, 32),), jnp.float32),
        "w_up": scatter_about(keys[8], (D * FF,), D ** -0.5, 0.25, ((0, 32),), jnp.float32),
        "w_down": scatter_about(keys[9], (FF * D,), FF ** -0.5, 0.15625, ((0, 32),), jnp.float32),
        "gains": jnp.clip(1.0 + 0.1 * jax.random.normal(keys[10], (2 * D,), jnp.float32), 0.5, 1.5),
        "m_query": scatter_about(keys[11], (D * D,), (0.5 * TOKENS ** 0.5), 512.0, ((0, 32),), jnp.float32),
        "m_key": scatter_about(keys[12], (D * KVD,), (0.5 * TOKENS ** 0.5), 512.0, ((0, 32),), jnp.float32),
        "m_value": scatter_about(keys[13], (D * KVD,), (0.5 * TOKENS ** 0.5), 512.0, ((0, 32),), jnp.float32),
        "m_out": scatter_about(keys[14], (D * D,), (0.5 * TOKENS ** 0.5), 512.0, ((0, 32),), jnp.float32),
        "m_gate": scatter_about(keys[15], (D * FF,), (0.5 * TOKENS ** 0.5), 512.0, ((0, 32),), jnp.float32),
        "m_up": scatter_about(keys[16], (D * FF,), (0.5 * TOKENS ** 0.5), 512.0, ((0, 32),), jnp.float32),
        "m_down": scatter_about(keys[17], (FF * D,), (0.5 * TOKENS ** 0.5), 512.0, ((0, 32),), jnp.float32),
        "m_gains": scatter_about(keys[18], (2 * D,), (0.5 * TOKENS ** 0.5), 512.0, ((0, 32),), jnp.float32),
    }


eps_norm = 1e-05
rope_base = 100000.0
momentum_decay = 0.95
matrix_rate = 0.1
weight_decay = 0.1
gain_rate = 0.25
coef_one = 3.4445
coef_two = -4.775
coef_three = 2.0315
precise = lax.Precision.HIGHEST

@jax.custom_vjp
def low(v):
    return lax.optimization_barrier(v.astype(jnp.bfloat16)).astype(jnp.float32)

@jax.custom_vjp
def low_back(v):
    return v

def low_keep(v):
    return (low(v), None)

def low_pass(kept, grad):
    return (grad,)

def back_keep(v):
    return (v, None)

def back_low(kept, grad):
    return (low(grad),)
low.defvjp(low_keep, low_pass)
low_back.defvjp(back_keep, back_low)

def product(left, right):
    return jnp.dot(left, right, precision=precise, preferred_element_type=jnp.float32)

def normalize(values, gain):
    scale = lax.rsqrt(lax.optimization_barrier(jnp.mean(values * values, axis=-1, keepdims=True)) + eps_norm)
    return values * scale * gain

def rotate(values, positions, heads):
    count = values.shape[0]
    half = HEAD_DIM // 2
    freqs = rope_base ** (-jnp.arange(half, dtype=jnp.float32) * 2.0 / HEAD_DIM)
    angle = positions.astype(jnp.float32)[:, None] * freqs[None, :]
    cosine = jnp.cos(angle)[:, None, :]
    sine = jnp.sin(angle)[:, None, :]
    shaped = values.reshape(count, heads, HEAD_DIM)
    first = shaped[..., :half]
    second = shaped[..., half:]
    turned = jnp.concatenate([first * cosine - second * sine, second * cosine + first * sine], axis=-1)
    return turned.reshape(count, heads * HEAD_DIM)

def attend(block):
    query, key, value = block
    group = HEADS // KV_HEADS
    query = query.reshape(SEQ, KV_HEADS, group, HEAD_DIM)
    scores = jnp.einsum('qkgd,skd->kgqs', query, key, precision=precise) * HEAD_DIM ** (-0.5)
    scores = low_back(scores)
    rows = lax.broadcasted_iota(jnp.int32, (SEQ, SEQ), 0)
    cols = lax.broadcasted_iota(jnp.int32, (SEQ, SEQ), 1)
    scores = jnp.where(rows >= cols, scores, -1e+30)
    top = lax.optimization_barrier(jnp.max(scores, axis=-1, keepdims=True))
    weights = jnp.exp(scores - top)
    probs = low(weights / lax.optimization_barrier(jnp.sum(weights, axis=-1, keepdims=True)))
    output = jnp.einsum('kgqs,skd->qkgd', probs, value, precision=precise)
    return output.reshape(SEQ, HEADS * HEAD_DIM)

def layer(inputs, query_w, key_w, value_w, out_w, gate_w, up_w, down_w, gain_pair, positions):
    first_gain = low(gain_pair[:D])
    second_gain = low(gain_pair[D:])
    count = inputs.shape[0] // SEQ
    normed = low(normalize(inputs, first_gain))
    query = low(rotate(low_back(product(normed, low(query_w.reshape(D, D)))), positions, HEADS))
    key = low(rotate(low_back(product(normed, low(key_w.reshape(D, KVD)))), positions, KV_HEADS))
    value = low(low_back(product(normed, low(value_w.reshape(D, KVD)))))
    blocks = (query.reshape(count, SEQ, HEADS, HEAD_DIM), key.reshape(count, SEQ, KV_HEADS, HEAD_DIM), value.reshape(count, SEQ, KV_HEADS, HEAD_DIM))
    mixed = lax.map(jax.checkpoint(attend), blocks).reshape(count * SEQ, D)
    mixed = low(low_back(mixed))
    middle = inputs + low_back(product(mixed, low(out_w.reshape(D, D))))
    hidden_in = low(normalize(middle, second_gain))
    gate = low_back(product(hidden_in, low(gate_w.reshape(D, FF))))
    upper = low_back(product(hidden_in, low(up_w.reshape(D, FF))))
    hidden = low(jax.nn.silu(gate) * upper)
    return middle + low_back(product(hidden, low(down_w.reshape(FF, D))))

def orthogonal(matrix):
    rows, cols = matrix.shape
    wide = matrix.T if rows > cols else matrix
    state = wide / (jnp.sqrt(jnp.sum(wide * wide)) + 1e-07)
    for turn in range(NS_ITERS):
        gram = jnp.dot(state, state.T, precision=precise)
        poly = coef_two * gram + coef_three * jnp.dot(gram, gram, precision=precise)
        state = coef_one * state + jnp.dot(poly, state, precision=precise)
    return state.T if rows > cols else state

def matrix_step(weight, moment, grad, shape):
    fresh = momentum_decay * moment + grad
    direction = orthogonal(fresh.reshape(shape)).reshape(-1)
    scale = 0.2 * math.sqrt(max(shape[0], shape[1]))
    return (fresh, weight - matrix_rate * (weight_decay * weight + scale * direction))

def reference(tokens, positions, cotangent, w_query, w_key, w_value, w_out, w_gate, w_up, w_down, gains, m_query, m_key, m_value, m_out, m_gate, m_up, m_down, m_gains):

    def forward(inputs, query_w, key_w, value_w, out_w, gate_w, up_w, down_w, gain_pair):
        return layer(inputs, query_w, key_w, value_w, out_w, gate_w, up_w, down_w, gain_pair, positions)
    block_out, pull = jax.vjp(forward, tokens.astype(jnp.float32), w_query, w_key, w_value, w_out, w_gate, w_up, w_down, gains)
    grads = pull(cotangent.astype(jnp.float32))
    mq, nq = matrix_step(w_query, m_query, grads[1], (D, D))
    mk, nk = matrix_step(w_key, m_key, grads[2], (D, KVD))
    mv, nv = matrix_step(w_value, m_value, grads[3], (D, KVD))
    mo, no = matrix_step(w_out, m_out, grads[4], (D, D))
    mg, ng = matrix_step(w_gate, m_gate, grads[5], (D, FF))
    mu, nu = matrix_step(w_up, m_up, grads[6], (D, FF))
    md, nd = matrix_step(w_down, m_down, grads[7], (FF, D))
    gain_moment = momentum_decay * m_gains + grads[8]
    halves = gain_moment.reshape(2, D)
    gain_dir = halves * lax.rsqrt(lax.optimization_barrier(jnp.mean(halves * halves, axis=1, keepdims=True)) + 1e-06)
    new_gains = gains - gain_rate * gain_dir.reshape(-1)
    return (block_out, grads[0], mq, mk, mv, mo, mg, mu, md, gain_moment, nq, nk, nv, no, ng, nu, nd, new_gains, grads[1], grads[2], grads[3], grads[4], grads[5], grads[6], grads[7], grads[8])
```

```python
from functools import partial
import math

import jax
import jax.numpy as jnp
import ml_dtypes
import numpy as np
from jax import lax
from jax.experimental import pallas as pl
from jax.experimental.pallas import tpu as pltpu
from jax.sharding import PartitionSpec as P

HEADS = 9
KV_HEADS = 3
HEAD_DIM = 64
D = 576
KVD = 192
FF = 1536
SEQ = 1024
NS_ITERS = 5


eps_norm = 1e-05
rope_base = 100000.0
momentum_decay = 0.95
matrix_rate = 0.1
weight_decay = 0.1
gain_rate = 0.25
coef_one = 3.4445
coef_two = -4.775
coef_three = 2.0315
precise = lax.Precision.HIGHEST


def matrix_shapes():
    return ((D, D), (D, KVD), (D, KVD), (D, D), (D, FF), (D, FF), (FF, D))


def normalize(values):
    scale = lax.rsqrt(jnp.mean(values * values, axis=-1, keepdims=True) + eps_norm)
    return (values * scale, scale)


def norm_back(grad_normed, normed, scale, gain):
    scaled = grad_normed * gain
    return scale * (scaled - normed * jnp.mean(scaled * normed, axis=-1, keepdims=True))


def angles(positions):
    half = HEAD_DIM // 2
    freqs = rope_base ** (-jnp.arange(half, dtype=jnp.float32) * 2.0 / HEAD_DIM)
    angle = positions.astype(jnp.float32)[:, None] * freqs[None, :]
    return (jnp.cos(angle)[:, None, :], jnp.sin(angle)[:, None, :])


def rotate(values, cosine, sine, heads, inverse):
    count = values.shape[0]
    half = HEAD_DIM // 2
    shaped = values.reshape(count, heads, HEAD_DIM)
    first = shaped[..., :half]
    second = shaped[..., half:]
    if inverse:
        turned = jnp.concatenate(
            [first * cosine + second * sine, second * cosine - first * sine], axis=-1
        )
    else:
        turned = jnp.concatenate(
            [first * cosine - second * sine, second * cosine + first * sine], axis=-1
        )
    return turned.reshape(count, heads * HEAD_DIM)


def split_heads(values, heads):
    count = values.shape[0] // SEQ
    group = heads // KV_HEADS
    shaped = values.reshape(count, SEQ, KV_HEADS, group, HEAD_DIM)
    return shaped.transpose(0, 2, 1, 3, 4).reshape(count * KV_HEADS, SEQ, group, HEAD_DIM)


def join_heads(blocks, heads):
    count = blocks.shape[0] // KV_HEADS
    group = heads // KV_HEADS
    shaped = blocks.reshape(count, KV_HEADS, SEQ, group, HEAD_DIM)
    return shaped.transpose(0, 2, 1, 3, 4).reshape(count * SEQ, heads * HEAD_DIM)


def masked_scores(query, key):
    scores = jnp.einsum(
        "qgd,sd->gqs", query, key, preferred_element_type=jnp.float32
    ) * HEAD_DIM ** (-0.5)
    rows = lax.broadcasted_iota(jnp.int32, (SEQ, SEQ), 0)
    cols = lax.broadcasted_iota(jnp.int32, (SEQ, SEQ), 1)
    return jnp.where((rows >= cols)[None], scores, -1e30)


def attend_block(block):
    query, key, value = block
    scores = masked_scores(query, key)
    top = jnp.max(scores, axis=-1, keepdims=True)
    weights = jnp.exp(scores - top)
    total = jnp.sum(weights, axis=-1, keepdims=True)
    probs = (weights / total).astype(jnp.bfloat16)
    output = jnp.einsum("gqs,sd->qgd", probs, value, preferred_element_type=jnp.float32)
    return (output.astype(jnp.bfloat16), top + jnp.log(total))


def attend_back(block):
    query, key, value, grad_out, logsum = block
    scores = masked_scores(query, key)
    probs = jnp.exp(scores - logsum)
    rounded = probs.astype(jnp.bfloat16)
    grad_probs = jnp.einsum("qgd,sd->gqs", grad_out, value, preferred_element_type=jnp.float32)
    inner = jnp.sum(probs * grad_probs, axis=-1, keepdims=True)
    grad_scores = (probs * (grad_probs - inner)).astype(jnp.bfloat16)
    scale = HEAD_DIM ** (-0.5)
    grad_query = (
        jnp.einsum("gqs,sd->qgd", grad_scores, key, preferred_element_type=jnp.float32) * scale
    )
    grad_key = (
        jnp.einsum("gqs,qgd->sd", grad_scores, query, preferred_element_type=jnp.float32) * scale
    )
    grad_value = jnp.einsum("gqs,qgd->sd", rounded, grad_out, preferred_element_type=jnp.float32)
    return (grad_query, grad_key, grad_value)


def orthogonal(matrix):
    rows, cols = matrix.shape
    wide = matrix.T if rows > cols else matrix
    state = wide / (jnp.sqrt(jnp.sum(wide * wide)) + 1e-07)
    for turn in range(NS_ITERS):
        gram = jnp.dot(state, state.T, precision=precise)
        poly = coef_two * gram + coef_three * jnp.dot(gram, gram, precision=precise)
        state = coef_one * state + jnp.dot(poly, state, precision=precise)
    return state.T if rows > cols else state


def direction_of(index, flat):
    if index < 7:
        return orthogonal(flat.reshape(matrix_shapes()[index])).reshape(-1)
    halves = flat.reshape(2, D)
    return (halves * lax.rsqrt(jnp.mean(halves * halves, axis=1, keepdims=True) + 1e-06)).reshape(
        -1
    )


def blank_out(flat):
    return jnp.zeros_like(flat)


def project(left, right):
    return jnp.dot(left, right, preferred_element_type=jnp.float32)


def weight_grad(left, right):
    return jnp.einsum("ta,tb->ab", left, right, preferred_element_type=jnp.float32).reshape(-1)


def back_project(grad, weight):
    return jnp.einsum("tb,ab->ta", grad, weight, preferred_element_type=jnp.float32)


def layer(tokens, positions, cotangent, query_w, key_w, value_w, out_w, gate_w, up_w, down_w, first_gain, second_gain):
    bf = jnp.bfloat16
    inputs = tokens.astype(jnp.float32)
    cosine, sine = angles(positions)
    normed_one, scale_one = normalize(inputs)
    attn_in = (normed_one * first_gain).astype(bf)
    query = rotate(project(attn_in, query_w), cosine, sine, HEADS, False).astype(bf)
    key = rotate(project(attn_in, key_w), cosine, sine, KV_HEADS, False).astype(bf)
    value = project(attn_in, value_w).astype(bf)
    query_blocks = split_heads(query, HEADS)
    key_blocks = split_heads(key, KV_HEADS)[:, :, 0, :]
    value_blocks = split_heads(value, KV_HEADS)[:, :, 0, :]
    out_blocks, logsum = lax.map(attend_block, (query_blocks, key_blocks, value_blocks))
    mixed = join_heads(out_blocks, HEADS)
    middle = inputs + project(mixed, out_w)
    normed_two, scale_two = normalize(middle)
    hidden_in = (normed_two * second_gain).astype(bf)
    gate = project(hidden_in, gate_w)
    upper = project(hidden_in, up_w)
    sigma = jax.nn.sigmoid(gate)
    hidden = (gate * sigma * upper).astype(bf)
    block_out = middle + project(hidden, down_w)
    grad_down = weight_grad(hidden, cotangent)
    grad_hidden = back_project(cotangent, down_w)
    grad_gate = (grad_hidden * upper * sigma * (1.0 + gate * (1.0 - sigma))).astype(bf)
    grad_upper = (grad_hidden * gate * sigma).astype(bf)
    grad_gate_w = weight_grad(hidden_in, grad_gate)
    grad_up_w = weight_grad(hidden_in, grad_upper)
    grad_hidden_in = back_project(grad_gate, gate_w) + back_project(grad_upper, up_w)
    grad_gain_two = jnp.sum(grad_hidden_in * normed_two, axis=0)
    grad_middle = cotangent.astype(jnp.float32) + norm_back(
        grad_hidden_in, normed_two, scale_two, second_gain
    )
    grad_attn = grad_middle.astype(bf)
    grad_out_w = weight_grad(mixed, grad_attn)
    grad_mixed = back_project(grad_attn, out_w).astype(bf)
    grad_q_blocks, grad_k_blocks, grad_v_blocks = lax.map(
        attend_back,
        (query_blocks, key_blocks, value_blocks, split_heads(grad_mixed, HEADS), logsum),
    )
    grad_query = rotate(join_heads(grad_q_blocks, HEADS), cosine, sine, HEADS, True).astype(bf)
    grad_key = rotate(
        join_heads(grad_k_blocks[:, :, None, :], KV_HEADS), cosine, sine, KV_HEADS, True
    ).astype(bf)
    grad_value = join_heads(grad_v_blocks[:, :, None, :], KV_HEADS).astype(bf)
    grad_query_w = weight_grad(attn_in, grad_query)
    grad_key_w = weight_grad(attn_in, grad_key)
    grad_value_w = weight_grad(attn_in, grad_value)
    grad_attn_in = (
        back_project(grad_query, query_w)
        + back_project(grad_key, key_w)
        + back_project(grad_value, value_w)
    )
    grad_gain_one = jnp.sum(grad_attn_in * normed_one, axis=0)
    input_grad = grad_middle + norm_back(grad_attn_in, normed_one, scale_one, first_gain)
    grads = (grad_query_w, grad_key_w, grad_value_w, grad_out_w, grad_gate_w, grad_up_w, grad_down)
    return block_out, input_grad, grads, jnp.concatenate([grad_gain_one, grad_gain_two])


def per_device(
    tokens,
    positions,
    cotangent,
    w_query,
    w_key,
    w_value,
    w_out,
    w_gate,
    w_up,
    w_down,
    gains,
    m_query,
    m_key,
    m_value,
    m_out,
    m_gate,
    m_up,
    m_down,
    m_gains,
):
    bf = jnp.bfloat16
    whole = (
        lax.all_gather(w_query.astype(bf), "dp", axis=0, tiled=True),
        lax.all_gather(w_key.astype(bf), "dp", axis=0, tiled=True),
        lax.all_gather(w_value.astype(bf), "dp", axis=0, tiled=True),
        lax.all_gather(w_out.astype(bf), "dp", axis=0, tiled=True),
        lax.all_gather(w_gate.astype(bf), "dp", axis=0, tiled=True),
        lax.all_gather(w_up.astype(bf), "dp", axis=0, tiled=True),
        lax.all_gather(w_down.astype(bf), "dp", axis=0, tiled=True),
        lax.all_gather(gains.astype(bf), "dp", axis=0, tiled=True),
    )
    shapes = matrix_shapes()
    query_w = whole[0].reshape(shapes[0])
    key_w = whole[1].reshape(shapes[1])
    value_w = whole[2].reshape(shapes[2])
    out_w = whole[3].reshape(shapes[3])
    gate_w = whole[4].reshape(shapes[4])
    up_w = whole[5].reshape(shapes[5])
    down_w = whole[6].reshape(shapes[6])
    gain_pair = whole[7].astype(jnp.float32).reshape(2, D)
    first_gain = gain_pair[0]
    second_gain = gain_pair[1]
    block_out, input_grad, parts, grad_gains = layer(
        tokens, positions, cotangent, query_w, key_w, value_w, out_w, gate_w, up_w, down_w, first_gain, second_gain
    )
    grad_query_w, grad_key_w, grad_value_w, grad_out_w, grad_gate_w, grad_up_w, grad_down = parts
    shares = (
        lax.psum_scatter(grad_query_w, "dp", scatter_dimension=0, tiled=True),
        lax.psum_scatter(grad_key_w, "dp", scatter_dimension=0, tiled=True),
        lax.psum_scatter(grad_value_w, "dp", scatter_dimension=0, tiled=True),
        lax.psum_scatter(grad_out_w, "dp", scatter_dimension=0, tiled=True),
        lax.psum_scatter(grad_gate_w, "dp", scatter_dimension=0, tiled=True),
        lax.psum_scatter(grad_up_w, "dp", scatter_dimension=0, tiled=True),
        lax.psum_scatter(grad_down, "dp", scatter_dimension=0, tiled=True),
        lax.psum_scatter(grad_gains, "dp", scatter_dimension=0, tiled=True),
    )
    old_moments = (m_query, m_key, m_value, m_out, m_gate, m_up, m_down, m_gains)
    moments = tuple((momentum_decay * old_moments[i] + shares[i] for i in range(8)))
    device = lax.axis_index("dp")
    count = lax.axis_size("dp")
    stride = count // 8
    owners = [i * stride for i in range(8)]
    full = (
        lax.all_gather(moments[0].astype(jnp.bfloat16), "dp", axis=0, tiled=True).astype(
            jnp.float32
        ),
        lax.all_gather(moments[1].astype(jnp.bfloat16), "dp", axis=0, tiled=True).astype(
            jnp.float32
        ),
        lax.all_gather(moments[2].astype(jnp.bfloat16), "dp", axis=0, tiled=True).astype(
            jnp.float32
        ),
        lax.all_gather(moments[3].astype(jnp.bfloat16), "dp", axis=0, tiled=True).astype(
            jnp.float32
        ),
        lax.all_gather(moments[4].astype(jnp.bfloat16), "dp", axis=0, tiled=True).astype(
            jnp.float32
        ),
        lax.all_gather(moments[5].astype(jnp.bfloat16), "dp", axis=0, tiled=True).astype(
            jnp.float32
        ),
        lax.all_gather(moments[6].astype(jnp.bfloat16), "dp", axis=0, tiled=True).astype(
            jnp.float32
        ),
        lax.all_gather(moments[7].astype(jnp.bfloat16), "dp", axis=0, tiled=True).astype(
            jnp.float32
        ),
    )
    results = [
        lax.cond(device == owners[i], partial(direction_of, i), blank_out, full[i])
        for i in range(8)
    ]
    pieces = (
        lax.psum_scatter(results[0], "dp", scatter_dimension=0, tiled=True),
        lax.psum_scatter(results[1], "dp", scatter_dimension=0, tiled=True),
        lax.psum_scatter(results[2], "dp", scatter_dimension=0, tiled=True),
        lax.psum_scatter(results[3], "dp", scatter_dimension=0, tiled=True),
        lax.psum_scatter(results[4], "dp", scatter_dimension=0, tiled=True),
        lax.psum_scatter(results[5], "dp", scatter_dimension=0, tiled=True),
        lax.psum_scatter(results[6], "dp", scatter_dimension=0, tiled=True),
        lax.psum_scatter(results[7], "dp", scatter_dimension=0, tiled=True),
    )
    masters = (w_query, w_key, w_value, w_out, w_gate, w_up, w_down)
    updated = []
    for i in range(7):
        scale = 0.2 * math.sqrt(max(shapes[i][0], shapes[i][1]))
        updated.append(masters[i] - matrix_rate * (weight_decay * masters[i] + scale * pieces[i]))
    new_gains = gains - gain_rate * pieces[7]
    return (
        block_out,
        input_grad,
        moments[0],
        moments[1],
        moments[2],
        moments[3],
        moments[4],
        moments[5],
        moments[6],
        moments[7],
        updated[0],
        updated[1],
        updated[2],
        updated[3],
        updated[4],
        updated[5],
        updated[6],
        new_gains,
        shares[0],
        shares[1],
        shares[2],
        shares[3],
        shares[4],
        shares[5],
        shares[6],
        shares[7],
    )


MESH = pl.DeviceIdType.MESH
BF = jnp.bfloat16
F32 = jnp.float32

UNITS = {
    "q": (640, 128, 5),
    "kv": (512, 128, 4),
    "o": (640, 128, 5),
    "g": (1536, 256, 6),
    "u": (1536, 256, 6),
}
GROUPS = (("q", "kv"), ("o",), ("g", "u"), ("d",))
ROWS_D = 48


def unit_width(name):
    return UNITS[name][0] + UNITS[name][1]


def group_shape(group):
    if group == ("d",):
        return (ROWS_D, 640)
    return (16, sum(unit_width(u) for u in group))


def unit_offset(name):
    for group in GROUPS:
        off = 0
        for u in group:
            if u == name:
                return off
            off += unit_width(u)
    raise KeyError(name)


def place_of(d):
    y, x, c = d // 4, (d // 2) % 2, d % 2
    return c * 4 + (y * 2 + x if c == 0 else x * 2 + y)


def spread_matrices():
    out = np.zeros((6, 144, 256), np.float32)
    for q in range(6):
        for d in range(8):
            p = place_of(d)
            for r in range(16):
                out[q, 18 * d + r, 16 * p + r] = 1
            for e in range(2):
                out[q, 18 * d + 16 + e, 128 + 16 * p + 8 * e + q] = 1
    return out


def gain_select():
    out = np.zeros((32, 512), np.float32)
    for i in range(32):
        z, d = i // 8, i % 8
        out[i, (place_of(d) * 4 + z) * 16 + 7] = 1
    return out


def gain_lanes():
    out = np.zeros((128, 2 * D), np.float32)
    for j in range(2 * D):
        out[j % 36, j] = 1
    return out


def coords():
    me = lax.axis_index("dp")
    z, y, x, c = me // 8, lax.rem(me // 4, 2), lax.rem(me // 2, 2), lax.rem(me, 2)
    a = y * (1 - c) + x * c
    b = x * (1 - c) + y * c

    def dev(zz, yy, xx, cc):
        return ((zz * 2 + yy) * 2 + xx) * 2 + cc

    peer_b = dev(z, y + (1 - 2 * y) * c, x + (1 - 2 * x) * (1 - c), c)
    peer_a = dev(z, y + (1 - 2 * y) * (1 - c), x + (1 - 2 * x) * c, c)
    sibling = dev(z, y, x, 1 - c)

    def along(step):
        return dev(lax.rem(z + step, 4), y, x, c)

    return me, (z, a, b, c), peer_a, peer_b, sibling, along


def greet(others):
    barrier = pltpu.get_barrier_semaphore()
    for other in others:
        pl.semaphore_signal(barrier, inc=1, device_id=(other,), device_id_type=MESH)
    pl.semaphore_wait(barrier, len(others))


def remote(src, dst, send, recv, target):
    return pltpu.make_async_remote_copy(
        src_ref=src, dst_ref=dst, send_sem=send, recv_sem=recv, device_id=(target,), device_id_type=MESH
    )


def slot(c, a, b, z):
    return ((c * 2 + a) * 2 + b) * 4 + z


class Gather:
    def __init__(self, buf, send, recv, where):
        self.buf, self.send, self.recv = buf, send, recv
        self.me, (self.z, self.a, self.b, self.c), self.peer_a, self.peer_b, self.sibling, self.along = where
        self.count = 0
        self.started = []

    def push(self, index, target):
        ref = self.buf.at[index]
        copy = remote(ref, ref, self.send.at[self.count], self.recv.at[slot(*index)], target)
        copy.start()
        self.started.append(copy)
        self.count += 1

    def arrive(self, index):
        ref = self.buf.at[index]
        remote(ref, ref, self.send.at[0], self.recv.at[slot(*index)], self.sibling).wait_recv()

    def phase_own(self):
        own = (self.c, self.a, self.b, self.z)
        for step in (1, 3, 2):
            self.push(own, self.along(step))
        self.push(own, self.peer_b)
        self.push(own, self.peer_a)
        self.push(own, self.sibling)

    def phase_z(self):
        for step in (1, 3, 2):
            index = (self.c, self.a, self.b, lax.rem(self.z + step, 4))
            self.arrive(index)
            self.push(index, self.peer_b)
            self.push(index, self.peer_a)
            self.push(index, self.sibling)

    def phase_b(self):
        for step in (0, 1, 3, 2):
            index = (self.c, self.a, 1 - self.b, lax.rem(self.z + step, 4))
            self.arrive(index)
            self.push(index, self.peer_a)
            self.push(index, self.sibling)

    def phase_a(self):
        for bb in (self.b, 1 - self.b):
            for step in (0, 1, 3, 2):
                index = (self.c, 1 - self.a, bb, lax.rem(self.z + step, 4))
                self.arrive(index)
                self.push(index, self.sibling)

    def phase_sibling(self):
        for aa in range(2):
            for bb in range(2):
                for zz in range(4):
                    self.arrive((1 - self.c, aa, bb, zz))

    def finish(self):
        for copy in self.started:
            copy.wait_send()


def low_lanes(rows):
    return lax.broadcasted_iota(jnp.int32, (rows, 128), 1) < 64


def turn(v):
    return pltpu.roll(v, 64, axis=1)


def load_rows(flat, scr, rows, tiles2):
    if tiles2 % 2 == 0:
        nt = tiles2 // 2
        for t in range(nt):
            scr[t, 0:rows, :] = flat[pl.ds(t, rows, stride=nt), :]
        return
    half, h = rows // 2, (tiles2 - 1) // 2
    low = low_lanes(half)
    pair = [flat[pl.ds(t, half, stride=tiles2), :] for t in range(tiles2)]
    turned = {t: turn(pair[t]) for t in range(h, tiles2)}
    for j in range(h + 1):
        even = pair[j] if j < h else jnp.where(low, pair[h], 0.0)
        odd = jnp.where(low, turned[h + j], turned[h + j + 1] if j < h else 0.0)
        scr[j, pl.ds(0, half, stride=2), :] = even
        scr[j, pl.ds(1, half, stride=2), :] = odd


def store_rows(scr, flat, rows, tiles2, base=0):
    if tiles2 % 2 == 0:
        nt = tiles2 // 2
        for t in range(nt):
            flat[pl.ds(t, rows, stride=nt), :] = scr[base + t, 0:rows, :]
        return
    half, h = rows // 2, (tiles2 - 1) // 2
    low = low_lanes(half)
    even = [scr[base + j, pl.ds(0, half, stride=2), :] for j in range(h + 1)]
    odd = [turn(scr[base + j, pl.ds(1, half, stride=2), :]) for j in range(h + 1)]
    for t in range(tiles2):
        if t < h:
            value = even[t]
        elif t == h:
            value = jnp.where(low, even[h], odd[0])
        else:
            value = jnp.where(low, odd[t - h - 1], odd[t - h])
        flat[pl.ds(t, half, stride=tiles2), :] = value


PARTS = {
    "q": ((0, 0, 9, 18),),
    "kv": ((1, 0, 3, 18), (2, 2, 3, 18)),
    "o": ((3, 0, 9, 18),),
    "g": ((4, 0, 24, 18),),
    "u": ((5, 0, 24, 18),),
    "d": ((6, 0, 9, 48),),
}


def pack_slab(name, scr, fold_scr, slab, off, gains=None):
    if name == "d":
        for t in range(5):
            slab[:, off + 128 * t : off + 128 * (t + 1)] = scr[t, 0:48, :].astype(BF)
        return
    padded, fold, chunks = UNITS[name]
    for t in range(padded // 128):
        slab[:, off + 128 * t : off + 128 * (t + 1)] = scr[t, 0:16, :].astype(BF)
    fold_scr[...] = jnp.zeros_like(fold_scr)
    per = fold // 128
    for q in range(chunks):
        for k in range(per):
            for e in range(2):
                fold_scr[e * 8 + q : e * 8 + q + 1, 128 * k : 128 * (k + 1)] = scr[q * per + k, 16 + e : 17 + e, :]
    if gains is not None:
        fold_scr[7:8, 0:128] = gains
    slab[:, off + padded : off + padded + fold] = fold_scr[:, 0:fold].astype(BF)


def unpack_slab(name, main, scr, fold_scr):
    if name == "d":
        for t in range(5):
            scr[t, 0:48, :] = main[:, 128 * t : 128 * (t + 1)]
        return
    padded, fold, chunks = UNITS[name]
    for t in range(padded // 128):
        scr[t, 0:16, :] = main[:, 128 * t : 128 * (t + 1)]
    fold_scr[:, 0:fold] = main[:, padded : padded + fold]
    per = fold // 128
    for q in range(chunks):
        for k in range(per):
            for e in range(2):
                scr[q * per + k, 16 + e : 17 + e, :] = fold_scr[e * 8 + q : e * 8 + q + 1, 128 * k : 128 * (k + 1)]


def spread(name, buf, off, spread_ref, dest):
    padded, fold, chunks = UNITS[name]

    def plane(z, _):
        folded = buf[:, :, :, z, :, off + padded : off + padded + fold].reshape(128, fold)
        for q in range(chunks):
            main = buf[:, :, :, z, :, off + q * fold : off + (q + 1) * fold].reshape(128, fold)
            both = jnp.concatenate([main, folded], axis=0)
            block = jnp.dot(spread_ref[q], both, preferred_element_type=F32)
            dest[pl.ds(pl.multiple_of(z * 144, 16), 144), q * fold : (q + 1) * fold] = block.astype(dest.dtype)
        return 0

    lax.fori_loop(0, 4, plane, 0)


def spread_down(buf, dest):
    for z in range(4):
        for d in range(8):
            y, x, c = d // 4, (d // 2) % 2, d % 2
            a, b = (y, x) if c == 0 else (x, y)
            dest[(z * 8 + d) * 48 : (z * 8 + d + 1) * 48, :] = buf[c, a, b, z].astype(dest.dtype)


def collect(name, source, buf, off, collect_ref, extra=None):
    padded, fold, chunks = UNITS[name]

    def plane(z, _):
        rows = pl.ds(pl.multiple_of(z * 144, 16), 144)
        total = jnp.zeros((128, fold), F32)
        for q in range(chunks):
            block = source[rows, q * fold : (q + 1) * fold].astype(BF)
            both = jnp.dot(collect_ref[q], block, preferred_element_type=F32)
            buf[:, :, :, z, :, off + q * fold : off + (q + 1) * fold] = (
                both[0:128].astype(BF).reshape(2, 2, 2, 16, fold)
            )
            total = total + both[128:256]
        if extra is not None:
            total = total + extra(z)
        buf[:, :, :, z, :, off + padded : off + padded + fold] = total.astype(BF).reshape(2, 2, 2, 16, fold)
        return 0

    lax.fori_loop(0, 4, plane, 0)


def collect_down(source, buf):
    for z in range(4):
        for d in range(8):
            y, x, c = d // 4, (d // 2) % 2, d % 2
            a, b = (y, x) if c == 0 else (x, y)
            buf[c, a, b, z] = source[(z * 8 + d) * 48 : (z * 8 + d + 1) * 48, :].astype(BF)


def load_unit(name, flats, scr):
    for index, tile, tiles2, rows in PARTS[name]:
        view = scr if tile == 0 else scr.at[pl.ds(tile, (tiles2 + 1) // 2)]
        load_rows(flats[index], view, rows, tiles2)


def gather_kernel(*refs):
    w = refs[0:7]
    gains_ref, spread_ref, select_ref, lanes_ref = refs[7:11]
    nat_q, nat_kv, nat_o, nat_g, nat_u, nat_d, gains_out = refs[11:18]
    bufs = refs[18:22]
    scr, fold_scr = refs[22:24]
    send, recv = refs[24:26]
    where = coords()
    me, (z, a, b, c), peer_a, peer_b, sibling, along = where
    own = (c, a, b, z)
    for group, buf in zip(GROUPS, bufs):
        for name in group:
            load_unit(name, w, scr)
            gains = None
            if name == "q":
                fold_scr[0:1, 0:128] = jnp.zeros((1, 128), F32)
                fold_scr[0:1, 0:36] = gains_ref[...]
                gains = fold_scr[0:1, 0:128]
            pack_slab(name, scr, fold_scr, buf.at[own], unit_offset(name), gains)
    greet((along(1), along(2), along(3), peer_a, peer_b, sibling))
    moves = [Gather(buf, send.at[k], recv.at[k], where) for k, buf in enumerate(bufs)]
    for move in moves:
        move.phase_own()
    for move in moves:
        move.phase_z()
    for move in moves:
        move.phase_b()
    for move in moves:
        move.phase_a()
    natural = {"q": nat_q, "kv": nat_kv, "o": nat_o, "g": nat_g, "u": nat_u}
    for group, buf, move in zip(GROUPS, bufs, moves):
        move.phase_sibling()
        for name in group:
            if name == "d":
                spread_down(buf, nat_d)
            else:
                spread(name, buf, unit_offset(name), spread_ref, natural[name])
        if "q" in group:
            read_gains(buf, select_ref, lanes_ref, gains_out)
    for move in moves:
        move.finish()


def read_gains(buf, select_ref, lanes_ref, gains_out):
    rows = gain_rows(buf[:, :, :, :, :, 640:768].reshape(512, 128), select_ref)
    wide = jnp.dot(rows.astype(BF), lanes_ref[...], preferred_element_type=F32)
    device = lax.broadcasted_iota(jnp.int32, wide.shape, 0)
    column = lax.broadcasted_iota(jnp.int32, wide.shape, 1)
    low = device * 36
    keep = jnp.logical_and(column >= low, column < low + 36)
    gains_out[...] = jnp.sum(jnp.where(keep, wide, 0.0), axis=0, keepdims=True)


def gain_rows(folds, select_ref):
    return jnp.dot(select_ref[...], folds, preferred_element_type=F32)


def vmem():
    return pl.BlockSpec(memory_space=pltpu.VMEM)


def slab_buffers():
    return [pltpu.VMEM((2, 2, 2, 4) + group_shape(group), BF) for group in GROUPS]


def gather_call(shards, gains, consts):
    spread_c, _, select_c, lanes_c = consts
    shape = jax.ShapeDtypeStruct
    return pl.pallas_call(
        gather_kernel,
        out_shape=(
            shape((D, 640), BF),
            shape((D, 512), BF),
            shape((D, 640), BF),
            shape((D, FF), BF),
            shape((D, FF), BF),
            shape((FF, 640), BF),
            shape((1, 2 * D), F32),
        ),
        in_specs=[vmem()] * 11,
        out_specs=(vmem(),) * 7,
        scratch_shapes=slab_buffers()
        + [
            pltpu.VMEM((12, 48, 128), F32),
            pltpu.VMEM((16, 256), F32),
            pltpu.SemaphoreType.DMA((4, 31)),
            pltpu.SemaphoreType.DMA((4, 32)),
        ],
        compiler_params=pltpu.CompilerParams(
            collective_id=0, has_side_effects=True, vmem_limit_bytes=56 * 2**20
        ),
        name="gather_parameters",
    )(*shards, gains, spread_c, select_c, lanes_c)


OWNERS = {"q": 16, "kv": 18, "o": 12, "g": 8, "u": 22, "d": 14}
UNIT_NAMES = ("q", "kv", "o", "g", "u", "d")


class Reduce:
    def __init__(self, buf, r1, r2, r3, r4, send, recv, where):
        self.buf, self.r1, self.r2, self.r3, self.r4 = buf, r1, r2, r3, r4
        self.send, self.recv = send, recv
        self.me, (self.z, self.a, self.b, self.c), self.peer_a, self.peer_b, self.sibling, self.along = where
        self.copies = {}

    def push(self, k, src, dst, target):
        copy = remote(src, dst, self.send.at[k], self.recv.at[k], target)
        copy.start()
        self.copies[k] = copy

    def stage_one(self):
        self.push(0, self.buf.at[1 - self.c, 1 - self.b], self.r1.at[1 - self.b], self.sibling)
        self.push(1, self.buf.at[1 - self.c, self.b], self.r1.at[self.b], self.sibling)

    def add(self, buf, index, got, count):
        def body(i, _):
            bb, zz = i // 4, lax.rem(i, 4)
            here = index + ((bb, zz) if len(index) == 2 else (zz,))
            there = got[1] + ((bb, zz) if len(index) == 2 else (zz,))
            buf[here] = (buf[here].astype(F32) + got[0][there].astype(F32)).astype(BF)
            return 0

        lax.fori_loop(0, count, body, 0)

    def stage_two(self):
        self.copies[0].wait_recv()
        self.add(self.buf, (self.c, 1 - self.a), (self.r1, (1 - self.a,)), 8)
        self.push(2, self.buf.at[self.c, 1 - self.a], self.r2, self.peer_a)
        self.copies[1].wait_recv()
        self.add(self.buf, (self.c, self.a), (self.r1, (self.a,)), 8)

    def stage_three(self):
        self.copies[2].wait_recv()
        self.add(self.buf, (self.c, self.a, 1 - self.b), (self.r2, (1 - self.b,)), 4)
        self.push(3, self.buf.at[self.c, self.a, 1 - self.b], self.r3, self.peer_b)
        self.add(self.buf, (self.c, self.a, self.b), (self.r2, (self.b,)), 4)

    def stage_four(self):
        self.copies[3].wait_recv()
        self.add(self.buf, (self.c, self.a, self.b), (self.r3, ()), 4)
        for step in (1, 3, 2):
            index = (self.c, self.a, self.b, lax.rem(self.z + step, 4))
            self.push(3 + step, self.buf.at[index], self.r4.at[step - 1], self.along(step))

    def result(self, total):
        for step in (1, 3, 2):
            self.copies[3 + step].wait_recv()
        own = self.buf[self.c, self.a, self.b, self.z].astype(F32)
        total[...] = (
            own + self.r4[0].astype(F32) + self.r4[1].astype(F32) + self.r4[2].astype(F32)
        )

    def finish(self):
        for copy in self.copies.values():
            copy.wait_send()


def diagonal(n):
    return lax.broadcasted_iota(jnp.int32, (n, n), 0) == lax.broadcasted_iota(jnp.int32, (n, n), 1)


def newton_schulz(state, cols=None):
    def read():
        return state[...] if cols is None else state[:, cols]

    def write(value):
        if cols is None:
            state[...] = value
        else:
            state[:, cols] = value

    whole = read()
    tall = whole.shape[0] > whole.shape[1]
    n = min(whole.shape)
    norm = jnp.sqrt(jnp.sum(jnp.sum(whole * whole, axis=1, keepdims=True), axis=0, keepdims=True))
    write(whole / (norm + 1e-07))

    def trace(square):
        kept = jnp.where(diagonal(n), square, 0.0)
        return jnp.sum(jnp.sum(kept, axis=1, keepdims=True), axis=0, keepdims=True) * (1.0 / n)

    def turn_once(_, carry):
        value = read()
        low = value.astype(BF)
        dims = (((0,), (0,)), ((), ())) if tall else (((1,), (1,)), ((), ()))
        gram = lax.dot_general(low, low, dims, preferred_element_type=F32)
        mean = trace(gram)
        rest = gram - jnp.where(diagonal(n), mean, 0.0)
        small = rest.astype(BF)
        rest = (coef_two + 2.0 * coef_three * mean) * rest + coef_three * jnp.dot(
            small, small, preferred_element_type=F32
        )
        more = trace(rest)
        poly = (rest - jnp.where(diagonal(n), more, 0.0)).astype(BF)
        keep = coef_one + coef_two * mean + coef_three * mean * mean + more
        if tall:
            change = jnp.dot(low, poly, preferred_element_type=F32)
        else:
            change = jnp.dot(poly, low, preferred_element_type=F32)
        write(keep * value + change)
        return carry

    lax.fori_loop(0, NS_ITERS, turn_once, 0)


def reduce_kernel(*refs):
    grads = refs[0:7]
    gain_grad = refs[7]
    w, gains_ref = refs[8:15], refs[15]
    m, m_gains = refs[16:23], refs[23]
    spread_ref, collect_ref, select_ref, lanes_back, gain_put = refs[24:29]
    grad_out, grad_gains_out = refs[29:36], refs[36]
    new_m, new_m_gains = refs[37:44], refs[44]
    new_w, new_gains = refs[45:52], refs[52]
    k = 53
    bufs = refs[k : k + 4]
    r1, r2, r3, r4 = (refs[k + 4 + 4 * j : k + 8 + 4 * j] for j in range(4))
    k += 20
    nat640, nat_kv, nat_d, total, scr, scr2, fold_scr, lane_scr = refs[k : k + 8]
    k += 8
    mslab = dict(zip(UNIT_NAMES, refs[k : k + 6]))
    oslab = dict(zip(UNIT_NAMES, refs[k + 6 : k + 12]))
    k += 12
    own_qo, own_kv, own_gu, own_d = refs[k : k + 4]
    x_qo, x_kv, x_gu, x_d = refs[k + 4 : k + 8]
    k += 8
    rs_send, rs_recv, up_send, up_recv, down_send, down_recv = refs[k : k + 6]

    where = coords()
    me, (z, a, b, c), peer_a, peer_b, sibling, along = where
    own = (c, a, b, z)

    barrier = pltpu.get_barrier_semaphore()

    def hello(j, _):
        @pl.when(j != me)
        def _():
            pl.semaphore_signal(barrier, inc=1, device_id=(j,), device_id_type=MESH)

        return 0

    lax.fori_loop(0, 32, hello, 0)

    row = lax.broadcasted_iota(jnp.int32, (32, 2 * D), 0) * 36
    col = lax.broadcasted_iota(jnp.int32, (32, 2 * D), 1)
    keep = jnp.logical_and(col >= row, col < row + 36)
    by_device = jnp.dot(
        jnp.where(keep, jnp.broadcast_to(gain_grad[...], (32, 2 * D)), 0.0).astype(BF),
        lanes_back[...],
        preferred_element_type=F32,
    ).astype(BF)

    def gain_extra(zz):
        return jnp.dot(gain_put[zz], by_device, preferred_element_type=F32)

    nat640[...] = jnp.zeros_like(nat640)
    nat_kv[...] = jnp.zeros_like(nat_kv)
    nat_d[...] = jnp.zeros_like(nat_d)
    nat_d[:, 0:D] = grads[6][...]
    collect_down(nat_d, bufs[3])
    collect("g", grads[4], bufs[2], unit_offset("g"), collect_ref)
    collect("u", grads[5], bufs[2], unit_offset("u"), collect_ref)
    nat640[:, 0:D] = grads[3][...]
    collect("o", nat640, bufs[1], unit_offset("o"), collect_ref)
    nat640[:, 0:D] = grads[0][...]
    collect("q", nat640, bufs[0], unit_offset("q"), collect_ref, gain_extra)
    nat_kv[:, 0:KVD] = grads[1][...]
    nat_kv[:, 256 : 256 + KVD] = grads[2][...]
    collect("kv", nat_kv, bufs[0], unit_offset("kv"), collect_ref)

    pl.semaphore_wait(barrier, 31)

    moves = [
        Reduce(bufs[g], r1[g], r2[g], r3[g], r4[g], rs_send.at[g], rs_recv.at[g], where) for g in range(4)
    ]
    order = (3, 2, 1, 0)
    for g in order:
        moves[g].stage_one()
    for g in order:
        moves[g].stage_two()
    for g in order:
        moves[g].stage_three()
    for g in order:
        moves[g].stage_four()

    up_copies = []

    def to_owner(name, number):
        owner = OWNERS[name]
        held = {"q": own_qo, "o": own_qo, "kv": own_kv, "g": own_gu, "u": own_gu, "d": own_d}[name]

        @pl.when(me != owner)
        def _():
            remote(mslab[name], held.at[own], up_send.at[number], up_recv.at[slot(*own)], owner).start()

        @pl.when(me == owner)
        def _():
            held[own] = mslab[name][...]

    for g in order:
        group = GROUPS[g]
        shape = group_shape(group)
        part = total.at[0 : shape[0], 0 : shape[1]]
        moves[g].result(part)
        for name in group:
            off = unit_offset(name)
            width = 640 if name == "d" else unit_width(name)
            unpack_slab(name, part[:, off : off + width], scr, fold_scr)
            for index, tile, tiles2, rows in PARTS[name]:
                store_rows(scr, grad_out[index], rows, tiles2, tile)
                new_m[index][...] = momentum_decay * m[index][...] + grad_out[index][...]
            if name == "q":
                lane_scr[0:1, :] = jnp.zeros((1, 128), F32)
                lane_scr[0:1, 0:36] = fold_scr[7:8, 0:36]
                grad_gains_out[...] = lane_scr[0:1, 0:36]
                new_m_gains[...] = momentum_decay * m_gains[...] + grad_gains_out[...]
                lane_scr[0:1, 0:36] = new_m_gains[...]
            load_unit(name, new_m, scr2)
            pack_slab(
                name, scr2, fold_scr, mslab[name], 0, lane_scr[0:1, :] if name == "q" else None
            )
            to_owner(name, UNIT_NAMES.index(name))

    def arrived(held):
        def one(j, _):
            @pl.when(j != slot(*own))
            def _():
                ref = held.at[j // 16, lax.rem(j // 8, 2), lax.rem(j // 4, 2), lax.rem(j, 4)]
                remote(ref, ref, up_send.at[0], up_recv.at[j], sibling).wait_recv()

            return 0

        lax.fori_loop(0, 32, one, 0)

    def give_back(held, name_of):
        def one(j, wait):
            cc, aa, bb, zz = j // 16, lax.rem(j // 8, 2), lax.rem(j // 4, 2), lax.rem(j, 4)
            y = aa * (1 - cc) + bb * cc
            x = bb * (1 - cc) + aa * cc
            target = ((zz * 2 + y) * 2 + x) * 2 + cc
            ref = held.at[cc, aa, bb, zz]

            @pl.when(j != slot(*own))
            def _():
                copy = remote(ref, oslab[name_of], down_send.at[j], down_recv.at[UNIT_NAMES.index(name_of)], target)
                if wait:
                    copy.wait_send()
                else:
                    copy.start()

        def start(j, _):
            one(j, False)
            return 0

        def finish(j, _):
            one(j, True)
            return 0

        lax.fori_loop(0, 32, start, 0)
        oslab[name_of][...] = held[own]
        lax.fori_loop(0, 32, finish, 0)

    @pl.when(jnp.logical_or(me == OWNERS["g"], me == OWNERS["u"]))
    def _():
        arrived(own_gu)
        spread("g", own_gu, 0, spread_ref, x_gu)
        newton_schulz(x_gu)
        collect("g", x_gu, own_gu, 0, collect_ref)

        @pl.when(me == OWNERS["g"])
        def _():
            give_back(own_gu, "g")

        @pl.when(me == OWNERS["u"])
        def _():
            give_back(own_gu, "u")

    @pl.when(me == OWNERS["d"])
    def _():
        arrived(own_d)
        spread_down(own_d, x_d)
        newton_schulz(x_d, slice(0, D))
        collect_down(x_d, own_d)
        give_back(own_d, "d")

    @pl.when(jnp.logical_or(me == OWNERS["q"], me == OWNERS["o"]))
    def _():
        arrived(own_qo)
        spread("q", own_qo, 0, spread_ref, x_qo)
        rows_of = gain_rows(own_qo[:, :, :, :, :, 640:768].reshape(512, 128), select_ref)
        squares = jnp.sum(rows_of * rows_of, axis=1, keepdims=True)
        scales = [
            lax.rsqrt(jnp.sum(squares[16 * h : 16 * h + 16], axis=0, keepdims=True) * (1.0 / D) + 1e-06)
            for h in range(2)
        ]
        newton_schulz(x_qo)

        def scale_extra(zz):
            scale = jnp.where(zz < 2, scales[0], scales[1])
            high = scale.astype(BF).astype(F32)
            row16 = lax.rem(lax.broadcasted_iota(jnp.int32, (128, 128), 0), 16)
            return jnp.where(row16 == 7, high, 0.0) + jnp.where(row16 == 15, scale - high, 0.0)

        collect("q", x_qo, own_qo, 0, collect_ref, scale_extra)

        @pl.when(me == OWNERS["q"])
        def _():
            give_back(own_qo, "q")

        @pl.when(me == OWNERS["o"])
        def _():
            give_back(own_qo, "o")

    @pl.when(me == OWNERS["kv"])
    def _():
        arrived(own_kv)
        spread("kv", own_kv, 0, spread_ref, x_kv)
        newton_schulz(x_kv, slice(0, KVD))
        newton_schulz(x_kv, slice(256, 256 + KVD))
        collect("kv", x_kv, own_kv, 0, collect_ref)
        give_back(own_kv, "kv")

    shapes = matrix_shapes()
    for name in ("d", "g", "u", "o", "kv", "q"):
        number = UNIT_NAMES.index(name)

        @pl.when(me != OWNERS[name])
        def _():
            remote(oslab[name], oslab[name], down_send.at[0], down_recv.at[number], sibling).wait_recv()

        unpack_slab(name, oslab[name][...].astype(F32), scr, fold_scr)
        for index, tile, tiles2, rows in PARTS[name]:
            store_rows(scr, new_w[index], rows, tiles2, tile)
            rate = 0.2 * math.sqrt(max(shapes[index]))
            old = w[index][...]
            new_w[index][...] = old - matrix_rate * (weight_decay * old + rate * new_w[index][...])
        if name == "q":
            scale = fold_scr[7:8, 0:36] + fold_scr[15:16, 0:36]
            new_gains[...] = gains_ref[...] - gain_rate * (new_m_gains[...] * scale)

    for name in UNIT_NAMES:
        owner = OWNERS[name]
        number = UNIT_NAMES.index(name)
        held = {"q": own_qo, "o": own_qo, "kv": own_kv, "g": own_gu, "u": own_gu, "d": own_d}[name]

        @pl.when(me != owner)
        def _():
            remote(mslab[name], held.at[own], up_send.at[number], up_recv.at[slot(*own)], owner).wait_send()

    for move in moves:
        move.finish()


def collect_constants():
    forward = spread_matrices()
    put = np.zeros((4, 128, 32), np.float32)
    for zz in range(4):
        for d in range(8):
            put[zz, 16 * place_of(d) + 7, 8 * zz + d] = 1
    low = ml_dtypes.bfloat16
    return (
        forward.astype(low),
        forward.transpose(0, 2, 1).astype(low),
        gain_select().astype(low),
        gain_lanes().astype(low),
        gain_lanes().T.astype(low),
        put.astype(low),
    )


def reduce_call(grads, gain_grad, w, gains, m, m_gains, consts):
    spread_c, collect_c, select_c, _, lanes_back, put = consts
    shape = jax.ShapeDtypeStruct
    flats = [shape(v.shape, F32) for v in w]
    one = [shape((1, 36), F32)]
    slabs = [pltpu.VMEM((16, unit_width(n)) if n != "d" else (ROWS_D, 640), BF) for n in UNIT_NAMES]
    stages = []
    for lead in ((2, 2, 4), (2, 4), (4,), (3,)):
        stages += [pltpu.VMEM(lead + group_shape(group), BF) for group in GROUPS]
    return pl.pallas_call(
        reduce_kernel,
        out_shape=tuple((flats + one) * 3),
        in_specs=[vmem()] * 29,
        out_specs=(vmem(),) * 24,
        scratch_shapes=slab_buffers()
        + stages
        + [
            pltpu.VMEM((D, 640), BF),
            pltpu.VMEM((D, 512), BF),
            pltpu.VMEM((FF, 640), BF),
            pltpu.VMEM((48, 3584), F32),
            pltpu.VMEM((12, 48, 128), F32),
            pltpu.VMEM((12, 48, 128), F32),
            pltpu.VMEM((16, 256), F32),
            pltpu.VMEM((8, 128), F32),
        ]
        + slabs
        + slabs
        + [
            pltpu.VMEM((2, 2, 2, 4, 16, unit_width("q")), BF),
            pltpu.VMEM((2, 2, 2, 4, 16, unit_width("kv")), BF),
            pltpu.VMEM((2, 2, 2, 4, 16, unit_width("g")), BF),
            pltpu.VMEM((2, 2, 2, 4, ROWS_D, 640), BF),
            pltpu.VMEM((D, 640), F32),
            pltpu.VMEM((D, 512), F32),
            pltpu.VMEM((D, FF), F32),
            pltpu.VMEM((FF, 640), F32),
            pltpu.SemaphoreType.DMA((4, 7)),
            pltpu.SemaphoreType.DMA((4, 7)),
            pltpu.SemaphoreType.DMA((6,)),
            pltpu.SemaphoreType.DMA((32,)),
            pltpu.SemaphoreType.DMA((32,)),
            pltpu.SemaphoreType.DMA((6,)),
        ],
        compiler_params=pltpu.CompilerParams(
            collective_id=1, has_side_effects=True, vmem_limit_bytes=60 * 2**20
        ),
        name="reduce_and_step",
    )(*grads, gain_grad, *w, gains, *m, m_gains, spread_c, collect_c, select_c, lanes_back, put)


def per_device_32(tokens, positions, cotangent, *rest):
    w, gains, m, m_gains = rest[0:7], rest[7], rest[8:15], rest[15]
    consts = collect_constants()
    w = [v.reshape(-1, 128) for v in w]
    m = [v.reshape(-1, 128) for v in m]
    gains, m_gains = gains.reshape(1, -1), m_gains.reshape(1, -1)
    nat_q, nat_kv, nat_o, nat_g, nat_u, nat_d, whole_gains = gather_call(w, gains, consts[0:4])
    block_out, input_grad, grads, gain_grad = layer(
        tokens,
        positions,
        cotangent,
        nat_q[:, :D],
        nat_kv[:, :KVD],
        nat_kv[:, 256 : 256 + KVD],
        nat_o[:, :D],
        nat_g,
        nat_u,
        nat_d[:, :D],
        whole_gains[0, :D],
        whole_gains[0, D:],
    )
    grads = [g.reshape(s).astype(BF) for g, s in zip(grads, matrix_shapes())]
    outs = reduce_call(grads, gain_grad.reshape(1, -1), w, gains, m, m_gains, consts)
    flat = [v.reshape(-1) for v in outs]
    return (block_out, input_grad, *flat[8:16], *flat[16:24], *flat[0:8])


def solution(mesh):
    placed = (P("dp", None), P("dp"), P("dp", None)) + (P("dp"),) * 16
    return jax.shard_map(
        per_device_32 if mesh.shape["dp"] == 32 else per_device,
        mesh=mesh,
        in_specs=placed,
        out_specs=(P("dp", None), P("dp", None)) + (P("dp"),) * 24,
        check_vma=False,
    )
```

```python
import math

import jax
import jax.numpy as jnp
import ml_dtypes
import numpy as np
from jax import lax
from jax.experimental import pallas as pl
from jax.experimental.pallas import tpu as pltpu
from jax.sharding import PartitionSpec as P

HEADS = 9
KV_HEADS = 3
HEAD_DIM = 64
D = 576
KVD = 192
FF = 1536
SEQ = 1024
NS_ITERS = 5


eps_norm = 1e-05
rope_base = 100000.0
momentum_decay = 0.95
matrix_rate = 0.1
weight_decay = 0.1
gain_rate = 0.25
coef_one = 3.4445
coef_two = -4.775
coef_three = 2.0315
precise = lax.Precision.HIGHEST
BF = jnp.bfloat16
F32 = jnp.float32
MESH = pl.DeviceIdType.MESH


def matrix_shapes():
    return ((D, D), (D, KVD), (D, KVD), (D, D), (D, FF), (D, FF), (FF, D))


UNITS = {
    "q": (640, 128, 5),
    "kv": (512, 128, 4),
    "o": (640, 128, 5),
    "g": (1536, 256, 6),
    "u": (1536, 256, 6),
}
GROUPS = (("q", "kv"), ("o",), ("g", "u"), ("d",))
ROWS_D = 48


def unit_width(name):
    return UNITS[name][0] + UNITS[name][1]


def group_shape(group):
    if group == ("d",):
        return (ROWS_D, 640)
    return (16, sum(unit_width(u) for u in group))


def unit_offset(name):
    for group in GROUPS:
        off = 0
        for u in group:
            if u == name:
                return off
            off += unit_width(u)
    raise KeyError(name)


def place_of(d):
    y, x, c = d // 4, (d // 2) % 2, d % 2
    return c * 4 + (y * 2 + x if c == 0 else x * 2 + y)


def spread_matrices():
    out = np.zeros((6, 144, 256), np.float32)
    for q in range(6):
        for d in range(8):
            p = place_of(d)
            for r in range(16):
                out[q, 18 * d + r, 16 * p + r] = 1
            for e in range(2):
                out[q, 18 * d + 16 + e, 128 + 16 * p + 8 * e + q] = 1
    return out


def gain_select():
    out = np.zeros((32, 512), np.float32)
    for i in range(32):
        z, d = i // 8, i % 8
        out[i, (place_of(d) * 4 + z) * 16 + 7] = 1
    return out


def gain_lanes():
    out = np.zeros((128, 2 * D), np.float32)
    for j in range(2 * D):
        out[j % 36, j] = 1
    return out


def coords():
    me = lax.axis_index("dp")
    z, y, x, c = me // 8, lax.rem(me // 4, 2), lax.rem(me // 2, 2), lax.rem(me, 2)
    a = y * (1 - c) + x * c
    b = x * (1 - c) + y * c

    def dev(zz, yy, xx, cc):
        return ((zz * 2 + yy) * 2 + xx) * 2 + cc

    peer_b = dev(z, y + (1 - 2 * y) * c, x + (1 - 2 * x) * (1 - c), c)
    peer_a = dev(z, y + (1 - 2 * y) * (1 - c), x + (1 - 2 * x) * c, c)
    sibling = dev(z, y, x, 1 - c)

    def along(step):
        return dev(lax.rem(z + step, 4), y, x, c)

    return me, (z, a, b, c), peer_a, peer_b, sibling, along


def greet(others):
    barrier = pltpu.get_barrier_semaphore()
    for other in others:
        pl.semaphore_signal(barrier, inc=1, device_id=(other,), device_id_type=MESH)
    pl.semaphore_wait(barrier, len(others))


def remote(src, dst, send, recv, target):
    return pltpu.make_async_remote_copy(
        src_ref=src, dst_ref=dst, send_sem=send, recv_sem=recv, device_id=(target,), device_id_type=MESH
    )


def slot(c, a, b, z):
    return ((c * 2 + a) * 2 + b) * 4 + z


class Gather:
    def __init__(self, buf, send, recv, where):
        self.buf, self.send, self.recv = buf, send, recv
        self.me, (self.z, self.a, self.b, self.c), self.peer_a, self.peer_b, self.sibling, self.along = where
        self.count = 0
        self.started = []

    def push(self, index, target):
        ref = self.buf.at[index]
        copy = remote(ref, ref, self.send.at[self.count], self.recv.at[slot(*index)], target)
        copy.start()
        self.started.append(copy)
        self.count += 1

    def arrive(self, index):
        ref = self.buf.at[index]
        remote(ref, ref, self.send.at[0], self.recv.at[slot(*index)], self.sibling).wait_recv()

    def phase_own(self):
        own = (self.c, self.a, self.b, self.z)
        for step in (1, 3, 2):
            self.push(own, self.along(step))
        self.push(own, self.peer_b)
        self.push(own, self.peer_a)
        self.push(own, self.sibling)

    def phase_z(self):
        for step in (1, 3, 2):
            index = (self.c, self.a, self.b, lax.rem(self.z + step, 4))
            self.arrive(index)
            self.push(index, self.peer_b)
            self.push(index, self.peer_a)
            self.push(index, self.sibling)

    def phase_b(self):
        for step in (0, 1, 3, 2):
            index = (self.c, self.a, 1 - self.b, lax.rem(self.z + step, 4))
            self.arrive(index)
            self.push(index, self.peer_a)
            self.push(index, self.sibling)

    def phase_a(self):
        for bb in (self.b, 1 - self.b):
            for step in (0, 1, 3, 2):
                index = (self.c, 1 - self.a, bb, lax.rem(self.z + step, 4))
                self.arrive(index)
                self.push(index, self.sibling)

    def phase_sibling(self):
        for aa in range(2):
            for bb in range(2):
                for zz in range(4):
                    self.arrive((1 - self.c, aa, bb, zz))

    def finish(self):
        for copy in self.started:
            copy.wait_send()


def low_lanes(rows):
    return lax.broadcasted_iota(jnp.int32, (rows, 128), 1) < 64


def turn(v):
    return pltpu.roll(v, 64, axis=1)


def load_rows(flat, scr, rows, tiles2):
    if tiles2 % 2 == 0:
        nt = tiles2 // 2
        for t in range(nt):
            scr[t, 0:rows, :] = flat[pl.ds(t, rows, stride=nt), :]
        return
    half, h = rows // 2, (tiles2 - 1) // 2
    low = low_lanes(half)
    pair = [flat[pl.ds(t, half, stride=tiles2), :] for t in range(tiles2)]
    turned = {t: turn(pair[t]) for t in range(h, tiles2)}
    for j in range(h + 1):
        even = pair[j] if j < h else jnp.where(low, pair[h], 0.0)
        odd = jnp.where(low, turned[h + j], turned[h + j + 1] if j < h else 0.0)
        scr[j, pl.ds(0, half, stride=2), :] = even
        scr[j, pl.ds(1, half, stride=2), :] = odd


def store_rows(scr, flat, rows, tiles2, base=0):
    if tiles2 % 2 == 0:
        nt = tiles2 // 2
        for t in range(nt):
            flat[pl.ds(t, rows, stride=nt), :] = scr[base + t, 0:rows, :]
        return
    half, h = rows // 2, (tiles2 - 1) // 2
    low = low_lanes(half)
    even = [scr[base + j, pl.ds(0, half, stride=2), :] for j in range(h + 1)]
    odd = [turn(scr[base + j, pl.ds(1, half, stride=2), :]) for j in range(h + 1)]
    for t in range(tiles2):
        if t < h:
            value = even[t]
        elif t == h:
            value = jnp.where(low, even[h], odd[0])
        else:
            value = jnp.where(low, odd[t - h - 1], odd[t - h])
        flat[pl.ds(t, half, stride=tiles2), :] = value


PARTS = {
    "q": ((0, 0, 9, 18),),
    "kv": ((1, 0, 3, 18), (2, 2, 3, 18)),
    "o": ((3, 0, 9, 18),),
    "g": ((4, 0, 24, 18),),
    "u": ((5, 0, 24, 18),),
    "d": ((6, 0, 9, 48),),
}


def pack_slab(name, scr, fold_scr, slab, off, gains=None):
    if name == "d":
        for t in range(5):
            slab[:, off + 128 * t : off + 128 * (t + 1)] = scr[t, 0:48, :].astype(BF)
        return
    padded, fold, chunks = UNITS[name]
    for t in range(padded // 128):
        slab[:, off + 128 * t : off + 128 * (t + 1)] = scr[t, 0:16, :].astype(BF)
    fold_scr[...] = jnp.zeros_like(fold_scr)
    per = fold // 128
    for q in range(chunks):
        for k in range(per):
            for e in range(2):
                fold_scr[e * 8 + q : e * 8 + q + 1, 128 * k : 128 * (k + 1)] = scr[q * per + k, 16 + e : 17 + e, :]
    if gains is not None:
        fold_scr[7:8, 0:128] = gains
    slab[:, off + padded : off + padded + fold] = fold_scr[:, 0:fold].astype(BF)


def unpack_slab(name, main, scr, fold_scr):
    if name == "d":
        for t in range(5):
            scr[t, 0:48, :] = main[:, 128 * t : 128 * (t + 1)]
        return
    padded, fold, chunks = UNITS[name]
    for t in range(padded // 128):
        scr[t, 0:16, :] = main[:, 128 * t : 128 * (t + 1)]
    fold_scr[:, 0:fold] = main[:, padded : padded + fold]
    per = fold // 128
    for q in range(chunks):
        for k in range(per):
            for e in range(2):
                scr[q * per + k, 16 + e : 17 + e, :] = fold_scr[e * 8 + q : e * 8 + q + 1, 128 * k : 128 * (k + 1)]


def spread(name, buf, off, spread_ref, dest):
    padded, fold, chunks = UNITS[name]

    def plane(z, _):
        folded = buf[:, :, :, z, :, off + padded : off + padded + fold].reshape(128, fold)
        for q in range(chunks):
            main = buf[:, :, :, z, :, off + q * fold : off + (q + 1) * fold].reshape(128, fold)
            both = jnp.concatenate([main, folded], axis=0)
            block = jnp.dot(spread_ref[q], both, preferred_element_type=F32)
            dest[pl.ds(pl.multiple_of(z * 144, 16), 144), q * fold : (q + 1) * fold] = block.astype(dest.dtype)
        return 0

    lax.fori_loop(0, 4, plane, 0)


def spread_down(buf, dest):
    for z in range(4):
        for d in range(8):
            y, x, c = d // 4, (d // 2) % 2, d % 2
            a, b = (y, x) if c == 0 else (x, y)
            dest[(z * 8 + d) * 48 : (z * 8 + d + 1) * 48, :] = buf[c, a, b, z].astype(dest.dtype)


def collect(name, source, buf, off, collect_ref, extra=None):
    padded, fold, chunks = UNITS[name]

    def plane(z, _):
        rows = pl.ds(pl.multiple_of(z * 144, 16), 144)
        total = jnp.zeros((128, fold), F32)
        for q in range(chunks):
            block = source[rows, q * fold : (q + 1) * fold].astype(BF)
            both = jnp.dot(collect_ref[q], block, preferred_element_type=F32)
            buf[:, :, :, z, :, off + q * fold : off + (q + 1) * fold] = (
                both[0:128].astype(BF).reshape(2, 2, 2, 16, fold)
            )
            total = total + both[128:256]
        if extra is not None:
            total = total + extra(z)
        buf[:, :, :, z, :, off + padded : off + padded + fold] = total.astype(BF).reshape(2, 2, 2, 16, fold)
        return 0

    lax.fori_loop(0, 4, plane, 0)


def collect_down(source, buf):
    for z in range(4):
        for d in range(8):
            y, x, c = d // 4, (d // 2) % 2, d % 2
            a, b = (y, x) if c == 0 else (x, y)
            buf[c, a, b, z] = source[(z * 8 + d) * 48 : (z * 8 + d + 1) * 48, :].astype(BF)


def load_unit(name, flats, scr):
    for index, tile, tiles2, rows in PARTS[name]:
        view = scr if tile == 0 else scr.at[pl.ds(tile, (tiles2 + 1) // 2)]
        load_rows(flats[index], view, rows, tiles2)


def gather_kernel(*refs):
    w = refs[0:7]
    gains_ref, spread_ref, select_ref, lanes_ref = refs[7:11]
    nat_q, nat_kv, nat_o, nat_g, nat_u, nat_d, gains_out = refs[11:18]
    bufs = refs[18:22]
    scr, fold_scr = refs[22:24]
    send, recv = refs[24:26]
    where = coords()
    me, (z, a, b, c), peer_a, peer_b, sibling, along = where
    own = (c, a, b, z)
    for group, buf in zip(GROUPS, bufs):
        for name in group:
            load_unit(name, w, scr)
            gains = None
            if name == "q":
                fold_scr[0:1, 0:128] = jnp.zeros((1, 128), F32)
                fold_scr[0:1, 0:36] = gains_ref[...]
                gains = fold_scr[0:1, 0:128]
            pack_slab(name, scr, fold_scr, buf.at[own], unit_offset(name), gains)
    greet((along(1), along(2), along(3), peer_a, peer_b, sibling))
    moves = [Gather(buf, send.at[k], recv.at[k], where) for k, buf in enumerate(bufs)]
    for move in moves:
        move.phase_own()
    for move in moves:
        move.phase_z()
    for move in moves:
        move.phase_b()
    for move in moves:
        move.phase_a()
    natural = {"q": nat_q, "kv": nat_kv, "o": nat_o, "g": nat_g, "u": nat_u}
    for group, buf, move in zip(GROUPS, bufs, moves):
        move.phase_sibling()
        for name in group:
            if name == "d":
                spread_down(buf, nat_d)
            else:
                spread(name, buf, unit_offset(name), spread_ref, natural[name])
        if "q" in group:
            read_gains(buf, select_ref, lanes_ref, gains_out)
    for move in moves:
        move.finish()


def read_gains(buf, select_ref, lanes_ref, gains_out):
    rows = gain_rows(buf[:, :, :, :, :, 640:768].reshape(512, 128), select_ref)
    wide = jnp.dot(rows.astype(BF), lanes_ref[...], preferred_element_type=F32)
    device = lax.broadcasted_iota(jnp.int32, wide.shape, 0)
    column = lax.broadcasted_iota(jnp.int32, wide.shape, 1)
    low = device * 36
    keep = jnp.logical_and(column >= low, column < low + 36)
    gains_out[...] = jnp.sum(jnp.where(keep, wide, 0.0), axis=0, keepdims=True)


def gain_rows(folds, select_ref):
    return jnp.dot(select_ref[...], folds, preferred_element_type=F32)


def vmem():
    return pl.BlockSpec(memory_space=pltpu.VMEM)


def slab_buffers():
    return [pltpu.VMEM((2, 2, 2, 4) + group_shape(group), BF) for group in GROUPS]


def gather_call(shards, gains, consts):
    spread_c, _, select_c, lanes_c = consts
    shape = jax.ShapeDtypeStruct
    return pl.pallas_call(
        gather_kernel,
        out_shape=(
            shape((D, 640), BF),
            shape((D, 512), BF),
            shape((D, 640), BF),
            shape((D, FF), BF),
            shape((D, FF), BF),
            shape((FF, 640), BF),
            shape((1, 2 * D), F32),
        ),
        in_specs=[vmem()] * 11,
        out_specs=(vmem(),) * 7,
        scratch_shapes=slab_buffers()
        + [
            pltpu.VMEM((12, 48, 128), F32),
            pltpu.VMEM((16, 256), F32),
            pltpu.SemaphoreType.DMA((4, 31)),
            pltpu.SemaphoreType.DMA((4, 32)),
        ],
        compiler_params=pltpu.CompilerParams(
            collective_id=0, has_side_effects=True, vmem_limit_bytes=56 * 2**20
        ),
        name="gather_parameters",
    )(*shards, gains, spread_c, select_c, lanes_c)


NN = (((1,), (0,)), ((), ()))
NT = (((1,), (1,)), ((), ()))
TN = (((0,), (0,)), ((), ()))
TILES = 5
BLOCK = 256
LOG2E = 1.4426950408889634


def mm(left, right, dims=NN):
    return lax.dot_general(left, right, dims, preferred_element_type=F32)


def block_rows(i, size=BLOCK):
    return pl.ds(pl.multiple_of(i * size, size), size)


def frequencies():
    half = HEAD_DIM // 2
    freqs = rope_base ** (-np.arange(half) * 2.0 / HEAD_DIM)
    return np.tile(freqs.astype(np.float32), 4).reshape(1, 128)


def lane(shape):
    return lax.broadcasted_iota(jnp.int32, shape, len(shape) - 1)


def cos_sin(angle):
    turns = jnp.floor(angle * 0.6366197723675814 + 0.5)
    rest = ((angle - turns * 1.5703125) - turns * 4.837512969970703e-4) - turns * 7.549789948768648e-8
    square = rest * rest
    sine = rest + rest * square * (
        -1.6666654611e-1 + square * (8.3321608736e-3 + square * -1.9515295891e-4)
    )
    cosine = (1.0 - 0.5 * square) + square * square * (
        4.166664568298827e-2 + square * (-1.388731625493765e-3 + square * 2.443315711809948e-5)
    )
    quarter = turns - 4.0 * jnp.floor(turns * 0.25)
    odd = jnp.logical_or(quarter == 1.0, quarter == 3.0)
    swapped_cos = jnp.where(odd, sine, cosine)
    swapped_sin = jnp.where(odd, cosine, sine)
    cos_sign = jnp.logical_or(quarter == 1.0, quarter == 2.0)
    return (
        jnp.where(cos_sign, -swapped_cos, swapped_cos),
        jnp.where(quarter >= 2.0, -swapped_sin, swapped_sin),
    )


def make_tables(positions, freqs, cos_ref, sin_ref):
    for r in range(SEQ // 128):
        row = jnp.broadcast_to(positions[r : r + 1, :].astype(F32), (128, 128))
        column = jnp.sum(jnp.where(diagonal(128), row, 0.0), axis=1, keepdims=True)
        cosine, sine = cos_sin(column * freqs[...])
        cos_ref[128 * r : 128 * (r + 1), :] = cosine
        sin_ref[128 * r : 128 * (r + 1), :] = jnp.where(lax.rem(lane((128, 128)), 64) < 32, -sine, sine)


def rotate_tile(value, cosine, sine, inverse=False):
    first = lax.rem(lane(value.shape), 64) < 32
    swapped = jnp.where(first, pltpu.roll(value, 96, axis=1), pltpu.roll(value, 32, axis=1))
    if inverse:
        return value * cosine - swapped * sine
    return value * cosine + swapped * sine


def row_scale(value):
    return lax.rsqrt(jnp.sum(value * value, axis=1, keepdims=True) * (1.0 / D) + eps_norm)


def normalize_tokens(tokens, gain, a_ref):
    def body(i, _):
        rows = block_rows(i)
        x = tokens[rows, :].astype(F32)
        a_ref[rows, :] = (x * row_scale(x) * gain).astype(BF)
        return 0

    lax.fori_loop(0, SEQ // BLOCK, body, 0)


def heads_in(a_ref, w_q, w_kv, cos_ref, sin_ref, q_ref, k_ref, v_ref):
    def body(i, _):
        rows = block_rows(i)
        a = a_ref[rows, :]
        cosine, sine = cos_ref[rows, :], sin_ref[rows, :]
        pq = mm(a, w_q[...])
        for t in range(TILES):
            turned = rotate_tile(pq[:, 128 * t : 128 * (t + 1)], cosine, sine).astype(BF)
            q_ref[t, rows, :] = turned * jnp.asarray(HEAD_DIM ** (-0.5), BF)
        pkv = mm(a, w_kv[...])
        low = lane((BLOCK, 128)) < 64
        for ref, base, rotary in ((k_ref, 0, True), (v_ref, 256, False)):
            for half in range(2):
                tile = pkv[:, base + 128 * half : base + 128 * (half + 1)]
                if rotary:
                    tile = rotate_tile(tile, cosine, sine)
                other = turn(tile)
                ref[2 * half, rows, :] = jnp.where(low, tile, other).astype(BF)
                if half == 0:
                    ref[1, rows, :] = jnp.where(low, other, tile).astype(BF)
        return 0

    lax.fori_loop(0, SEQ // BLOCK, body, 0)


def own_lanes(value, parity):
    here = lane(value.shape) // 64 == parity
    return jnp.where(here, value, jnp.zeros_like(value))


def attend_group(g, q_ref, k_ref, v_ref, o_ref, lse_ref):
    for h in range(HEADS // KV_HEADS):
        j = 3 * g + h
        t, parity = j // 2, lax.rem(j, 2)
        for i in range(SEQ // BLOCK):
            end = BLOCK * (i + 1)
            query = q_ref[t, BLOCK * i : end, :]
            s = mm(own_lanes(k_ref[g, 0:end, :], parity), query, NT)
            rows = lax.broadcasted_iota(jnp.int32, (BLOCK, BLOCK), 0)
            cols = lax.broadcasted_iota(jnp.int32, (BLOCK, BLOCK), 1)
            corner = jnp.where(cols >= rows, s[BLOCK * i :, :], -1e30)
            s = jnp.concatenate([s[: BLOCK * i, :], corner], axis=0) if i else corner
            top = jnp.max(s, axis=0, keepdims=True)
            weights = jnp.exp2((s - top) * LOG2E)
            total = jnp.sum(weights, axis=0, keepdims=True)
            probs = (weights * (1.0 / total)).astype(BF)
            out = mm(probs, own_lanes(v_ref[g, 0:end, :], parity), TN)
            o_ref[t, BLOCK * i : end, :] += out.astype(BF)
            lse_ref[j, :, BLOCK * i : end] = top * LOG2E + jnp.log2(total)


def attend_all(q_ref, k_ref, v_ref, o_ref, lse_ref):
    o_ref[...] = jnp.zeros_like(o_ref)

    def body(g, _):
        attend_group(g, q_ref, k_ref, v_ref, o_ref, lse_ref)
        return 0

    lax.fori_loop(0, KV_HEADS, body, 0)


def feed_forward(tokens, cot, gain, w_o, w_g, w_u, w_d, o_ref, out_ref, h_ref, z_ref, dg_ref, du_ref, e_ref, dx_ref, do_ref, d_ref, gain_ref):
    gain_ref[...] = jnp.zeros_like(gain_ref)

    def body(i, _):
        rows = block_rows(i)
        o = jnp.concatenate([o_ref[t, rows, :] for t in range(TILES)], axis=1)
        x2 = tokens[rows, :].astype(F32) + mm(o[:, 0:D], w_o[:, 0:D])
        r2 = row_scale(x2)
        n2 = x2 * r2
        h = (n2 * gain).astype(BF)
        h_ref[rows, :] = h
        c = cot[rows, :]
        gate = mm(h, w_g[...])
        upper = mm(h, w_u[...])
        grad = mm(c, w_d[:, 0:D], NT)
        sigma = 0.5 * jnp.tanh(0.5 * gate) + 0.5
        silu = gate * sigma
        z = (silu * upper).astype(BF)
        z_ref[rows, :] = z
        dg = (grad * upper * (sigma + silu * (1.0 - sigma))).astype(BF)
        du = (grad * silu).astype(BF)
        dg_ref[rows, :] = dg
        du_ref[rows, :] = du
        out_ref[rows, :] = x2 + mm(z, w_d[:, 0:D])
        dh = mm(dg, w_g[...], NT) + mm(du, w_u[...], NT)
        gain_ref[...] += jnp.sum(dh * n2, axis=0, keepdims=True)
        scaled = dh * gain
        mean = jnp.sum(scaled * n2, axis=1, keepdims=True) * (1.0 / D)
        dx = c.astype(F32) + r2 * (scaled - n2 * mean)
        dx_ref[rows, :] = dx
        e = dx.astype(BF)
        e_ref[rows, :] = e
        do = mm(e, w_o[:, 0:D], NT)
        pick = (lax.broadcasted_iota(jnp.int32, (8, 128), 0) == lane((8, 128)) // 64).astype(BF)
        for t in range(TILES):
            if t < TILES - 1:
                tile = do[:, 128 * t : 128 * (t + 1)]
            else:
                tile = jnp.concatenate([do[:, 512:576], jnp.zeros((BLOCK, 64), F32)], axis=1)
            tile = tile.astype(BF)
            do_ref[t, rows, :] = tile
            product = tile.astype(F32) * o[:, 128 * t : 128 * (t + 1)].astype(F32)
            high = product.astype(BF)
            low = (product - high.astype(F32)).astype(BF)
            inner = mm(pick, high, NT) + mm(pick, low, NT)
            d_ref[2 * t, :, rows] = inner[0:1]
            if t < TILES - 1:
                d_ref[2 * t + 1, :, rows] = inner[1:2]
        return 0

    lax.fori_loop(0, SEQ // BLOCK, body, 0)


def down_gradient(z_ref, cot, g_d):
    for k in range(3):
        g_d[512 * k : 512 * (k + 1), 0:D] = mm(z_ref[:, 512 * k : 512 * (k + 1)], cot[...], TN).astype(BF)
    g_d[:, D:] = jnp.zeros((FF, 64), BF)


def wide_gradient(h_ref, d_ref, g):
    for k in range(3):
        g[:, 512 * k : 512 * (k + 1)] = mm(h_ref[...], d_ref[:, 512 * k : 512 * (k + 1)], TN).astype(BF)


def out_gradient(o_ref, e_ref, g_o):
    for t in range(TILES):
        part = mm(o_ref[t], e_ref[...], TN).astype(BF)
        if t < TILES - 1:
            g_o[128 * t : 128 * (t + 1), 0:D] = part
        else:
            g_o[512:576, 0:D] = part[0:64]
    g_o[:, D:] = jnp.zeros((D, 64), BF)


def attend_back_group(g, q_ref, k_ref, v_ref, do_ref, lse_ref, d_ref, dq_ref, dk_ref, dv_ref):
    for h in range(HEADS // KV_HEADS):
        j = 3 * g + h
        t, parity = j // 2, lax.rem(j, 2)
        for i in range(SEQ // BLOCK):
            start = BLOCK * i
            rows = slice(start, start + BLOCK)
            key = own_lanes(k_ref[g, rows, :], parity)
            value = own_lanes(v_ref[g, rows, :], parity)
            query, grad = q_ref[t, start:, :], do_ref[t, start:, :]
            probs = jnp.exp2(mm(key, query, NT) * LOG2E - lse_ref[j, :, start:])
            down = lax.broadcasted_iota(jnp.int32, (BLOCK, BLOCK), 0)
            across = lax.broadcasted_iota(jnp.int32, (BLOCK, BLOCK), 1)
            corner = jnp.where(across >= down, probs[:, :BLOCK], 0.0)
            probs = jnp.concatenate([corner, probs[:, BLOCK:]], axis=1) if start + BLOCK < SEQ else corner
            ds = (probs * (mm(value, grad, NT) - d_ref[j, :, start:])).astype(BF)
            dv_ref[g, parity, rows, :] += mm(probs.astype(BF), grad)
            dk_ref[g, parity, rows, :] += mm(ds, query)
            dq_ref[t, start:, :] += mm(ds, key, TN)


def attend_back_all(q_ref, k_ref, v_ref, do_ref, lse_ref, d_ref, dq_ref, dk_ref, dv_ref):
    dq_ref[...] = jnp.zeros_like(dq_ref)
    dk_ref[...] = jnp.zeros_like(dk_ref)
    dv_ref[...] = jnp.zeros_like(dv_ref)

    def body(g, _):
        attend_back_group(g, q_ref, k_ref, v_ref, do_ref, lse_ref, d_ref, dq_ref, dk_ref, dv_ref)
        return 0

    lax.fori_loop(0, KV_HEADS, body, 0)


def heads_out(dq_ref, dk_ref, dv_ref, cos_ref, sin_ref, dpq_ref, dkv_ref):
    def body(i, _):
        rows = block_rows(i)
        cosine, sine = cos_ref[rows, :], sin_ref[rows, :]
        for t in range(TILES):
            tile = dq_ref[t, rows, :] * HEAD_DIM ** (-0.5)
            dpq_ref[rows, 128 * t : 128 * (t + 1)] = rotate_tile(tile, cosine, sine, True).astype(BF)
        low = lane((BLOCK, 128)) < 64
        for ref, base, rotary in ((dk_ref, 0, True), (dv_ref, 256, False)):
            whole = [ref[g, 0, rows, :] + turn(ref[g, 1, rows, :]) for g in range(KV_HEADS)]
            tiles = (jnp.where(low, whole[0], turn(whole[1])), jnp.where(low, whole[2], 0.0))
            for half in range(2):
                tile = rotate_tile(tiles[half], cosine, sine, True) if rotary else tiles[half]
                dkv_ref[rows, base + 128 * half : base + 128 * (half + 1)] = tile.astype(BF)
        return 0

    lax.fori_loop(0, SEQ // BLOCK, body, 0)


def first_gradients(a_ref, dpq_ref, dkv_ref, g_q, g_kv):
    g_q[...] = mm(a_ref[...], dpq_ref[...], TN).astype(BF)
    g_kv[...] = mm(a_ref[...], dkv_ref[...], TN).astype(BF)


def input_gradient(tokens, gain, dx_ref, dpq_ref, dkv_ref, w_q, w_kv, out_ref, gain_ref):
    gain_ref[...] = jnp.zeros_like(gain_ref)

    def body(i, _):
        rows = block_rows(i)
        da = mm(dpq_ref[rows, :], w_q[...], NT) + mm(dkv_ref[rows, :], w_kv[...], NT)
        x = tokens[rows, :].astype(F32)
        r1 = row_scale(x)
        n1 = x * r1
        gain_ref[...] += jnp.sum(da * n1, axis=0, keepdims=True)
        scaled = da * gain
        mean = jnp.sum(scaled * n1, axis=1, keepdims=True) * (1.0 / D)
        out_ref[rows, :] = dx_ref[rows, :] + r1 * (scaled - n1 * mean)
        return 0

    lax.fori_loop(0, SEQ // BLOCK, body, 0)


def front_kernel(tokens, positions, cot, gains, freqs, w_q, w_kv, w_o, w_g, w_u, w_d, out_ref, a_ref, cos_ref, sin_ref, q_ref, k_ref, v_ref, lse_ref, do_ref, d_ref, dx_ref, g_o, g_g, g_u, g_d, gain_ref, o_ref, h_ref, z_ref, dg_ref, du_ref, e_ref):
    make_tables(positions, freqs, cos_ref, sin_ref)
    normalize_tokens(tokens, gains[:, 0:D], a_ref)
    heads_in(a_ref, w_q, w_kv, cos_ref, sin_ref, q_ref, k_ref, v_ref)
    attend_all(q_ref, k_ref, v_ref, o_ref, lse_ref)
    feed_forward(tokens, cot, gains[:, D : 2 * D], w_o, w_g, w_u, w_d, o_ref, out_ref, h_ref, z_ref, dg_ref, du_ref, e_ref, dx_ref, do_ref, d_ref, gain_ref)
    down_gradient(z_ref, cot, g_d)
    wide_gradient(h_ref, dg_ref, g_g)
    wide_gradient(h_ref, du_ref, g_u)
    out_gradient(o_ref, e_ref, g_o)


def back_kernel(tokens, gains, w_q, w_kv, a_ref, cos_ref, sin_ref, q_ref, k_ref, v_ref, lse_ref, do_ref, d_ref, dx_ref, out_ref, g_q, g_kv, gain_ref, dq_ref, dk_ref, dv_ref, dpq_ref, dkv_ref):
    attend_back_all(q_ref, k_ref, v_ref, do_ref, lse_ref, d_ref, dq_ref, dk_ref, dv_ref)
    heads_out(dq_ref, dk_ref, dv_ref, cos_ref, sin_ref, dpq_ref, dkv_ref)
    first_gradients(a_ref, dpq_ref, dkv_ref, g_q, g_kv)
    input_gradient(tokens, gains[:, 0:D], dx_ref, dpq_ref, dkv_ref, w_q, w_kv, out_ref, gain_ref)


def local_call(kernel, name, args, outs, scratch):
    return pl.pallas_call(
        kernel,
        out_shape=tuple(jax.ShapeDtypeStruct(*o) for o in outs),
        in_specs=[vmem()] * len(args),
        out_specs=(vmem(),) * len(outs),
        scratch_shapes=[pltpu.VMEM(*s) for s in scratch],
        compiler_params=pltpu.CompilerParams(vmem_limit_bytes=60 * 2**20),
        name=name,
    )(*args)


def layer(tokens, positions, cotangent, gains, w_q, w_kv, w_o, w_g, w_u, w_d):
    T = SEQ
    front = local_call(
        front_kernel,
        "forward_and_feed_forward_back",
        (tokens, positions.reshape(-1, 128), cotangent, gains, jnp.asarray(frequencies()), w_q, w_kv, w_o, w_g, w_u, w_d),
        (
            ((T, D), F32),
            ((T, D), BF),
            ((T, 128), F32),
            ((T, 128), F32),
            ((TILES, T, 128), BF),
            ((KV_HEADS, T, 128), BF),
            ((KV_HEADS, T, 128), BF),
            ((HEADS, 1, T), F32),
            ((TILES, T, 128), BF),
            ((HEADS, 1, T), F32),
            ((T, D), F32),
            ((D, 640), BF),
            ((D, FF), BF),
            ((D, FF), BF),
            ((FF, 640), BF),
            ((1, D), F32),
        ),
        (((TILES, T, 128), BF), ((T, D), BF), ((T, FF), BF), ((T, FF), BF), ((T, FF), BF), ((T, D), BF)),
    )
    out, a, cosine, sine, q, k, v, lse, do, inner, dx, g_o, g_g, g_u, g_d, gain_two = front
    input_grad, g_q, g_kv, gain_one = local_call(
        back_kernel,
        "attention_back",
        (tokens, gains, w_q, w_kv, a, cosine, sine, q, k, v, lse, do, inner, dx),
        (((T, D), F32), ((D, 640), BF), ((D, 512), BF), ((1, D), F32)),
        (
            ((TILES, T, 128), F32),
            ((KV_HEADS, 2, T, 128), F32),
            ((KV_HEADS, 2, T, 128), F32),
            ((T, 640), BF),
            ((T, 512), BF),
        ),
    )
    return out, input_grad, (g_q, g_kv, g_o, g_g, g_u, g_d), jnp.concatenate([gain_one, gain_two], axis=1)


OWNERS = {"q": 16, "kv": 18, "o": 12, "g": 8, "u": 22, "d": 14}
UNIT_NAMES = ("q", "kv", "o", "g", "u", "d")


class Reduce:
    def __init__(self, buf, r1, r2, r3, r4, send, recv, where):
        self.buf, self.r1, self.r2, self.r3, self.r4 = buf, r1, r2, r3, r4
        self.send, self.recv = send, recv
        self.me, (self.z, self.a, self.b, self.c), self.peer_a, self.peer_b, self.sibling, self.along = where
        self.copies = {}

    def push(self, k, src, dst, target):
        copy = remote(src, dst, self.send.at[k], self.recv.at[k], target)
        copy.start()
        self.copies[k] = copy

    def stage_one(self):
        self.push(0, self.buf.at[1 - self.c, 1 - self.b], self.r1.at[1 - self.b], self.sibling)
        self.push(1, self.buf.at[1 - self.c, self.b], self.r1.at[self.b], self.sibling)

    def add(self, buf, index, got, count):
        def body(i, _):
            bb, zz = i // 4, lax.rem(i, 4)
            here = index + ((bb, zz) if len(index) == 2 else (zz,))
            there = got[1] + ((bb, zz) if len(index) == 2 else (zz,))
            buf[here] = (buf[here].astype(F32) + got[0][there].astype(F32)).astype(BF)
            return 0

        lax.fori_loop(0, count, body, 0)

    def stage_two(self):
        self.copies[0].wait_recv()
        self.add(self.buf, (self.c, 1 - self.a), (self.r1, (1 - self.a,)), 8)
        self.push(2, self.buf.at[self.c, 1 - self.a], self.r2, self.peer_a)
        self.copies[1].wait_recv()
        self.add(self.buf, (self.c, self.a), (self.r1, (self.a,)), 8)

    def stage_three(self):
        self.copies[2].wait_recv()
        self.add(self.buf, (self.c, self.a, 1 - self.b), (self.r2, (1 - self.b,)), 4)
        self.push(3, self.buf.at[self.c, self.a, 1 - self.b], self.r3, self.peer_b)
        self.add(self.buf, (self.c, self.a, self.b), (self.r2, (self.b,)), 4)

    def stage_four(self):
        self.copies[3].wait_recv()
        self.add(self.buf, (self.c, self.a, self.b), (self.r3, ()), 4)
        for step in (1, 3, 2):
            index = (self.c, self.a, self.b, lax.rem(self.z + step, 4))
            self.push(3 + step, self.buf.at[index], self.r4.at[step - 1], self.along(step))

    def result(self, total):
        for step in (1, 3, 2):
            self.copies[3 + step].wait_recv()
        own = self.buf[self.c, self.a, self.b, self.z].astype(F32)
        total[...] = (
            own + self.r4[0].astype(F32) + self.r4[1].astype(F32) + self.r4[2].astype(F32)
        )

    def finish(self):
        for copy in self.copies.values():
            copy.wait_send()


def diagonal(n):
    return lax.broadcasted_iota(jnp.int32, (n, n), 0) == lax.broadcasted_iota(jnp.int32, (n, n), 1)


def newton_schulz(state, cols=None):
    def read():
        return state[...] if cols is None else state[:, cols]

    def write(value):
        if cols is None:
            state[...] = value
        else:
            state[:, cols] = value

    whole = read()
    tall = whole.shape[0] > whole.shape[1]
    n = min(whole.shape)
    norm = jnp.sqrt(jnp.sum(jnp.sum(whole * whole, axis=1, keepdims=True), axis=0, keepdims=True))
    write(whole / (norm + 1e-07))

    def trace(square):
        kept = jnp.where(diagonal(n), square, 0.0)
        return jnp.sum(jnp.sum(kept, axis=1, keepdims=True), axis=0, keepdims=True) * (1.0 / n)

    def turn_once(_, carry):
        value = read()
        low = value.astype(BF)
        dims = (((0,), (0,)), ((), ())) if tall else (((1,), (1,)), ((), ()))
        gram = lax.dot_general(low, low, dims, preferred_element_type=F32)
        mean = trace(gram)
        rest = gram - jnp.where(diagonal(n), mean, 0.0)
        small = rest.astype(BF)
        rest = (coef_two + 2.0 * coef_three * mean) * rest + coef_three * jnp.dot(
            small, small, preferred_element_type=F32
        )
        more = trace(rest)
        poly = (rest - jnp.where(diagonal(n), more, 0.0)).astype(BF)
        keep = coef_one + coef_two * mean + coef_three * mean * mean + more
        if tall:
            change = jnp.dot(low, poly, preferred_element_type=F32)
        else:
            change = jnp.dot(poly, low, preferred_element_type=F32)
        write(keep * value + change)
        return carry

    lax.fori_loop(0, NS_ITERS, turn_once, 0)


def reduce_kernel(*refs):
    grads = refs[0:6]
    gain_grad = refs[6]
    w, gains_ref = refs[7:14], refs[14]
    m, m_gains = refs[15:22], refs[22]
    spread_ref, collect_ref, select_ref, lanes_back, gain_put = refs[23:28]
    grad_out, grad_gains_out = refs[28:35], refs[35]
    new_m, new_m_gains = refs[36:43], refs[43]
    new_w, new_gains = refs[44:51], refs[51]
    k = 52
    bufs = refs[k : k + 4]
    r1, r2, r3, r4 = (refs[k + 4 + 4 * j : k + 8 + 4 * j] for j in range(4))
    k += 20
    total, scr, scr2, fold_scr, lane_scr = refs[k : k + 5]
    k += 5
    mslab = dict(zip(UNIT_NAMES, refs[k : k + 6]))
    oslab = dict(zip(UNIT_NAMES, refs[k + 6 : k + 12]))
    k += 12
    own_qo, own_kv, own_gu, own_d = refs[k : k + 4]
    x_qo, x_kv, x_gu, x_d = refs[k + 4 : k + 8]
    k += 8
    rs_send, rs_recv, up_send, up_recv, down_send, down_recv = refs[k : k + 6]

    where = coords()
    me, (z, a, b, c), peer_a, peer_b, sibling, along = where
    own = (c, a, b, z)

    barrier = pltpu.get_barrier_semaphore()

    def hello(j, _):
        @pl.when(j != me)
        def _():
            pl.semaphore_signal(barrier, inc=1, device_id=(j,), device_id_type=MESH)

        return 0

    lax.fori_loop(0, 32, hello, 0)

    row = lax.broadcasted_iota(jnp.int32, (32, 2 * D), 0) * 36
    col = lax.broadcasted_iota(jnp.int32, (32, 2 * D), 1)
    keep = jnp.logical_and(col >= row, col < row + 36)
    by_device = jnp.dot(
        jnp.where(keep, jnp.broadcast_to(gain_grad[...], (32, 2 * D)), 0.0).astype(BF),
        lanes_back[...],
        preferred_element_type=F32,
    ).astype(BF)

    def gain_extra(zz):
        return jnp.dot(gain_put[zz], by_device, preferred_element_type=F32)

    collect_down(grads[5], bufs[3])
    collect("g", grads[3], bufs[2], unit_offset("g"), collect_ref)
    collect("u", grads[4], bufs[2], unit_offset("u"), collect_ref)
    collect("o", grads[2], bufs[1], unit_offset("o"), collect_ref)
    collect("q", grads[0], bufs[0], unit_offset("q"), collect_ref, gain_extra)
    collect("kv", grads[1], bufs[0], unit_offset("kv"), collect_ref)

    pl.semaphore_wait(barrier, 31)

    moves = [
        Reduce(bufs[g], r1[g], r2[g], r3[g], r4[g], rs_send.at[g], rs_recv.at[g], where) for g in range(4)
    ]
    order = (3, 2, 1, 0)
    for g in order:
        moves[g].stage_one()
    for g in order:
        moves[g].stage_two()
    for g in order:
        moves[g].stage_three()
    for g in order:
        moves[g].stage_four()

    up_copies = []

    def to_owner(name, number):
        owner = OWNERS[name]
        held = {"q": own_qo, "o": own_qo, "kv": own_kv, "g": own_gu, "u": own_gu, "d": own_d}[name]

        @pl.when(me != owner)
        def _():
            remote(mslab[name], held.at[own], up_send.at[number], up_recv.at[slot(*own)], owner).start()

        @pl.when(me == owner)
        def _():
            held[own] = mslab[name][...]

    for g in order:
        group = GROUPS[g]
        shape = group_shape(group)
        part = total.at[0 : shape[0], 0 : shape[1]]
        moves[g].result(part)
        for name in group:
            off = unit_offset(name)
            width = 640 if name == "d" else unit_width(name)
            unpack_slab(name, part[:, off : off + width], scr, fold_scr)
            for index, tile, tiles2, rows in PARTS[name]:
                store_rows(scr, grad_out[index], rows, tiles2, tile)
                new_m[index][...] = momentum_decay * m[index][...] + grad_out[index][...]
            if name == "q":
                lane_scr[0:1, :] = jnp.zeros((1, 128), F32)
                lane_scr[0:1, 0:36] = fold_scr[7:8, 0:36]
                grad_gains_out[...] = lane_scr[0:1, 0:36]
                new_m_gains[...] = momentum_decay * m_gains[...] + grad_gains_out[...]
                lane_scr[0:1, 0:36] = new_m_gains[...]
            load_unit(name, new_m, scr2)
            pack_slab(
                name, scr2, fold_scr, mslab[name], 0, lane_scr[0:1, :] if name == "q" else None
            )
            to_owner(name, UNIT_NAMES.index(name))

    def arrived(held):
        def one(j, _):
            @pl.when(j != slot(*own))
            def _():
                ref = held.at[j // 16, lax.rem(j // 8, 2), lax.rem(j // 4, 2), lax.rem(j, 4)]
                remote(ref, ref, up_send.at[0], up_recv.at[j], sibling).wait_recv()

            return 0

        lax.fori_loop(0, 32, one, 0)

    def give_back(held, name_of):
        def one(j, wait):
            cc, aa, bb, zz = j // 16, lax.rem(j // 8, 2), lax.rem(j // 4, 2), lax.rem(j, 4)
            y = aa * (1 - cc) + bb * cc
            x = bb * (1 - cc) + aa * cc
            target = ((zz * 2 + y) * 2 + x) * 2 + cc
            ref = held.at[cc, aa, bb, zz]

            @pl.when(j != slot(*own))
            def _():
                copy = remote(ref, oslab[name_of], down_send.at[j], down_recv.at[UNIT_NAMES.index(name_of)], target)
                if wait:
                    copy.wait_send()
                else:
                    copy.start()

        def start(j, _):
            one(j, False)
            return 0

        def finish(j, _):
            one(j, True)
            return 0

        lax.fori_loop(0, 32, start, 0)
        oslab[name_of][...] = held[own]
        lax.fori_loop(0, 32, finish, 0)

    @pl.when(jnp.logical_or(me == OWNERS["g"], me == OWNERS["u"]))
    def _():
        arrived(own_gu)
        spread("g", own_gu, 0, spread_ref, x_gu)
        newton_schulz(x_gu)
        collect("g", x_gu, own_gu, 0, collect_ref)

        @pl.when(me == OWNERS["g"])
        def _():
            give_back(own_gu, "g")

        @pl.when(me == OWNERS["u"])
        def _():
            give_back(own_gu, "u")

    @pl.when(me == OWNERS["d"])
    def _():
        arrived(own_d)
        spread_down(own_d, x_d)
        newton_schulz(x_d, slice(0, D))
        collect_down(x_d, own_d)
        give_back(own_d, "d")

    @pl.when(jnp.logical_or(me == OWNERS["q"], me == OWNERS["o"]))
    def _():
        arrived(own_qo)
        spread("q", own_qo, 0, spread_ref, x_qo)
        rows_of = gain_rows(own_qo[:, :, :, :, :, 640:768].reshape(512, 128), select_ref)
        squares = jnp.sum(rows_of * rows_of, axis=1, keepdims=True)
        scales = [
            lax.rsqrt(jnp.sum(squares[16 * h : 16 * h + 16], axis=0, keepdims=True) * (1.0 / D) + 1e-06)
            for h in range(2)
        ]
        newton_schulz(x_qo)

        def scale_extra(zz):
            scale = jnp.where(zz < 2, scales[0], scales[1])
            high = scale.astype(BF).astype(F32)
            row16 = lax.rem(lax.broadcasted_iota(jnp.int32, (128, 128), 0), 16)
            return jnp.where(row16 == 7, high, 0.0) + jnp.where(row16 == 15, scale - high, 0.0)

        collect("q", x_qo, own_qo, 0, collect_ref, scale_extra)

        @pl.when(me == OWNERS["q"])
        def _():
            give_back(own_qo, "q")

        @pl.when(me == OWNERS["o"])
        def _():
            give_back(own_qo, "o")

    @pl.when(me == OWNERS["kv"])
    def _():
        arrived(own_kv)
        spread("kv", own_kv, 0, spread_ref, x_kv)
        newton_schulz(x_kv, slice(0, KVD))
        newton_schulz(x_kv, slice(256, 256 + KVD))
        collect("kv", x_kv, own_kv, 0, collect_ref)
        give_back(own_kv, "kv")

    shapes = matrix_shapes()
    for name in ("d", "g", "u", "o", "kv", "q"):
        number = UNIT_NAMES.index(name)

        @pl.when(me != OWNERS[name])
        def _():
            remote(oslab[name], oslab[name], down_send.at[0], down_recv.at[number], sibling).wait_recv()

        unpack_slab(name, oslab[name][...].astype(F32), scr, fold_scr)
        for index, tile, tiles2, rows in PARTS[name]:
            store_rows(scr, new_w[index], rows, tiles2, tile)
            rate = 0.2 * math.sqrt(max(shapes[index]))
            old = w[index][...]
            new_w[index][...] = old - matrix_rate * (weight_decay * old + rate * new_w[index][...])
        if name == "q":
            scale = fold_scr[7:8, 0:36] + fold_scr[15:16, 0:36]
            new_gains[...] = gains_ref[...] - gain_rate * (new_m_gains[...] * scale)

    for name in UNIT_NAMES:
        owner = OWNERS[name]
        number = UNIT_NAMES.index(name)
        held = {"q": own_qo, "o": own_qo, "kv": own_kv, "g": own_gu, "u": own_gu, "d": own_d}[name]

        @pl.when(me != owner)
        def _():
            remote(mslab[name], held.at[own], up_send.at[number], up_recv.at[slot(*own)], owner).wait_send()

    for move in moves:
        move.finish()


def collect_constants():
    forward = spread_matrices()
    put = np.zeros((4, 128, 32), np.float32)
    for zz in range(4):
        for d in range(8):
            put[zz, 16 * place_of(d) + 7, 8 * zz + d] = 1
    low = ml_dtypes.bfloat16
    return (
        forward.astype(low),
        forward.transpose(0, 2, 1).astype(low),
        gain_select().astype(low),
        gain_lanes().astype(low),
        gain_lanes().T.astype(low),
        put.astype(low),
    )


def reduce_call(grads, gain_grad, w, gains, m, m_gains, consts):
    spread_c, collect_c, select_c, _, lanes_back, put = consts
    shape = jax.ShapeDtypeStruct
    flats = [shape(v.shape, F32) for v in w]
    one = [shape((1, 36), F32)]
    slabs = [pltpu.VMEM((16, unit_width(n)) if n != "d" else (ROWS_D, 640), BF) for n in UNIT_NAMES]
    stages = []
    for lead in ((2, 2, 4), (2, 4), (4,), (3,)):
        stages += [pltpu.VMEM(lead + group_shape(group), BF) for group in GROUPS]
    return pl.pallas_call(
        reduce_kernel,
        out_shape=tuple((flats + one) * 3),
        in_specs=[vmem()] * 28,
        out_specs=(vmem(),) * 24,
        scratch_shapes=slab_buffers()
        + stages
        + [
            pltpu.VMEM((48, 3584), F32),
            pltpu.VMEM((12, 48, 128), F32),
            pltpu.VMEM((12, 48, 128), F32),
            pltpu.VMEM((16, 256), F32),
            pltpu.VMEM((8, 128), F32),
        ]
        + slabs
        + slabs
        + [
            pltpu.VMEM((2, 2, 2, 4, 16, unit_width("q")), BF),
            pltpu.VMEM((2, 2, 2, 4, 16, unit_width("kv")), BF),
            pltpu.VMEM((2, 2, 2, 4, 16, unit_width("g")), BF),
            pltpu.VMEM((2, 2, 2, 4, ROWS_D, 640), BF),
            pltpu.VMEM((D, 640), F32),
            pltpu.VMEM((D, 512), F32),
            pltpu.VMEM((D, FF), F32),
            pltpu.VMEM((FF, 640), F32),
            pltpu.SemaphoreType.DMA((4, 7)),
            pltpu.SemaphoreType.DMA((4, 7)),
            pltpu.SemaphoreType.DMA((6,)),
            pltpu.SemaphoreType.DMA((32,)),
            pltpu.SemaphoreType.DMA((32,)),
            pltpu.SemaphoreType.DMA((6,)),
        ],
        compiler_params=pltpu.CompilerParams(
            collective_id=1, has_side_effects=True, vmem_limit_bytes=60 * 2**20
        ),
        name="reduce_and_step",
    )(*grads, gain_grad, *w, gains, *m, m_gains, spread_c, collect_c, select_c, lanes_back, put)


def orthogonal(matrix):
    rows, cols = matrix.shape
    wide = matrix.T if rows > cols else matrix
    state = wide / (jnp.sqrt(jnp.sum(wide * wide)) + 1e-07)
    for turn_number in range(NS_ITERS):
        gram = jnp.dot(state, state.T, precision=precise)
        poly = coef_two * gram + coef_three * jnp.dot(gram, gram, precision=precise)
        state = coef_one * state + jnp.dot(poly, state, precision=precise)
    return state.T if rows > cols else state


def direction_of(index, flat):
    if index < 7:
        return orthogonal(flat.reshape(matrix_shapes()[index])).reshape(-1)
    halves = flat.reshape(2, D)
    return (halves * lax.rsqrt(jnp.mean(halves * halves, axis=1, keepdims=True) + 1e-06)).reshape(-1)


def gather_all(flat):
    return lax.all_gather(flat.astype(BF), "dp", axis=0, tiled=True)


def scatter_sum(whole):
    return lax.psum_scatter(whole, "dp", scatter_dimension=0, tiled=True)


def pad_columns(matrix, width):
    return jnp.pad(matrix, ((0, 0), (0, width - matrix.shape[1])))


def per_device(tokens, positions, cotangent, *rest):
    w, gains, m, m_gains = rest[0:7], rest[7], rest[8:15], rest[15]
    shapes = matrix_shapes()
    whole = [gather_all(v).reshape(s) for v, s in zip(w, shapes)]
    padded = (
        pad_columns(whole[0], 640),
        jnp.concatenate([pad_columns(whole[1], 256), pad_columns(whole[2], 256)], axis=1),
        pad_columns(whole[3], 640),
        whole[4],
        whole[5],
        pad_columns(whole[6], 640),
    )
    block_out, input_grad, grads, gain_grad = layer(
        tokens, positions, cotangent, gather_all(gains).astype(F32).reshape(1, -1), *padded
    )
    parts = (
        grads[0][:, :D],
        grads[1][:, :KVD],
        grads[1][:, 256 : 256 + KVD],
        grads[2][:, :D],
        grads[3],
        grads[4],
        grads[5][:, :D],
    )
    shares = [scatter_sum(g.astype(F32).reshape(-1)) for g in parts] + [scatter_sum(gain_grad.reshape(-1))]
    moments = [momentum_decay * old + share for old, share in zip((*m, m_gains), shares)]
    device = lax.axis_index("dp")
    stride = lax.axis_size("dp") // 8
    pieces = []
    for i in range(8):
        full = gather_all(moments[i]).astype(F32)
        found = lax.cond(
            device == i * stride, lambda v, i=i: direction_of(i, v), jnp.zeros_like, full
        )
        pieces.append(scatter_sum(found))
    updated = []
    for i in range(7):
        scale = 0.2 * math.sqrt(max(shapes[i]))
        updated.append(w[i] - matrix_rate * (weight_decay * w[i] + scale * pieces[i]))
    new_gains = gains - gain_rate * pieces[7]
    return (block_out, input_grad, *moments, *updated, new_gains, *shares)


def per_device_32(tokens, positions, cotangent, *rest):
    w, gains, m, m_gains = rest[0:7], rest[7], rest[8:15], rest[15]
    consts = collect_constants()
    w = [v.reshape(-1, 128) for v in w]
    m = [v.reshape(-1, 128) for v in m]
    gains, m_gains = gains.reshape(1, -1), m_gains.reshape(1, -1)
    *natural, whole_gains = gather_call(w, gains, consts[0:4])
    block_out, input_grad, grads, gain_grad = layer(tokens, positions, cotangent, whole_gains, *natural)
    outs = reduce_call(grads, gain_grad, w, gains, m, m_gains, consts)
    flat = [v.reshape(-1) for v in outs]
    return (block_out, input_grad, *flat[8:16], *flat[16:24], *flat[0:8])


def solution(mesh):
    placed = (P("dp", None), P("dp"), P("dp", None)) + (P("dp"),) * 16
    return jax.shard_map(
        per_device_32 if mesh.shape["dp"] == 32 else per_device,
        mesh=mesh,
        in_specs=placed,
        out_specs=(P("dp", None), P("dp", None)) + (P("dp"),) * 24,
        check_vma=False,
    )
```

```python
import math

import jax
import jax.numpy as jnp
import ml_dtypes
import numpy as np
from jax import lax
from jax.experimental import pallas as pl
from jax.experimental.pallas import tpu as pltpu
from jax.sharding import PartitionSpec as P

HEADS = 9
KV_HEADS = 3
HEAD_DIM = 64
D = 576
KVD = 192
FF = 1536
SEQ = 1024
NS_ITERS = 5


eps_norm = 1e-05
rope_base = 100000.0
momentum_decay = 0.95
matrix_rate = 0.1
weight_decay = 0.1
gain_rate = 0.25
coef_one = 3.4445
coef_two = -4.775
coef_three = 2.0315
precise = lax.Precision.HIGHEST
BF = jnp.bfloat16
F32 = jnp.float32
MESH = pl.DeviceIdType.MESH


def matrix_shapes():
    return ((D, D), (D, KVD), (D, KVD), (D, D), (D, FF), (D, FF), (FF, D))


UNITS = {
    "q": (640, 128, 5),
    "kv": (512, 128, 4),
    "o": (640, 128, 5),
    "g": (1536, 256, 6),
    "u": (1536, 256, 6),
}
GROUPS = (("q", "kv"), ("o",), ("g", "u"), ("d",))
ROWS_D = 48


def unit_width(name):
    return UNITS[name][0] + UNITS[name][1]


def group_shape(group):
    if group == ("d",):
        return (ROWS_D, 640)
    return (16, sum(unit_width(u) for u in group))


def unit_offset(name):
    for group in GROUPS:
        off = 0
        for u in group:
            if u == name:
                return off
            off += unit_width(u)
    raise KeyError(name)


def place_of(d):
    y, x, c = d // 4, (d // 2) % 2, d % 2
    return c * 4 + (y * 2 + x if c == 0 else x * 2 + y)


def spread_matrices():
    out = np.zeros((6, 144, 256), np.float32)
    for q in range(6):
        for d in range(8):
            p = place_of(d)
            for r in range(16):
                out[q, 18 * d + r, 16 * p + r] = 1
            for e in range(2):
                out[q, 18 * d + 16 + e, 128 + 16 * p + 8 * e + q] = 1
    return out


def gain_select():
    out = np.zeros((32, 512), np.float32)
    for i in range(32):
        z, d = i // 8, i % 8
        out[i, (place_of(d) * 4 + z) * 16 + 7] = 1
    return out


def gain_lanes():
    out = np.zeros((128, 2 * D), np.float32)
    for j in range(2 * D):
        out[j % 36, j] = 1
    return out


def coords():
    me = lax.axis_index("dp")
    z, y, x, c = me // 8, lax.rem(me // 4, 2), lax.rem(me // 2, 2), lax.rem(me, 2)
    a = y * (1 - c) + x * c
    b = x * (1 - c) + y * c

    def dev(zz, yy, xx, cc):
        return ((zz * 2 + yy) * 2 + xx) * 2 + cc

    peer_b = dev(z, y + (1 - 2 * y) * c, x + (1 - 2 * x) * (1 - c), c)
    peer_a = dev(z, y + (1 - 2 * y) * (1 - c), x + (1 - 2 * x) * c, c)
    sibling = dev(z, y, x, 1 - c)

    def along(step):
        return dev(lax.rem(z + step, 4), y, x, c)

    return me, (z, a, b, c), peer_a, peer_b, sibling, along


def say_hello(others):
    barrier = pltpu.get_barrier_semaphore()
    for other in others:
        pl.semaphore_signal(barrier, inc=1, device_id=(other,), device_id_type=MESH)
    return barrier


def remote(src, dst, send, recv, target):
    return pltpu.make_async_remote_copy(
        src_ref=src, dst_ref=dst, send_sem=send, recv_sem=recv, device_id=(target,), device_id_type=MESH
    )


def slot(c, a, b, z):
    return ((c * 2 + a) * 2 + b) * 4 + z


class Gather:
    def __init__(self, buf, send, recv, where):
        self.buf, self.send, self.recv = buf, send, recv
        self.me, (self.z, self.a, self.b, self.c), self.peer_a, self.peer_b, self.sibling, self.along = where
        self.count = 0

    def push(self, index, target):
        ref = self.buf.at[index]
        copy = remote(ref, ref, self.send.at[self.count], self.recv.at[slot(*index)], target)
        copy.start()
        self.count += 1

    def arrive(self, index):
        ref = self.buf.at[index]
        remote(ref, ref, self.send.at[0], self.recv.at[slot(*index)], self.sibling).wait_recv()

    def phase_own(self):
        own = (self.c, self.a, self.b, self.z)
        for step in (1, 3, 2):
            self.push(own, self.along(step))
        self.push(own, self.peer_b)
        self.push(own, self.peer_a)
        self.push(own, self.sibling)

    def phase_z(self):
        for step in (1, 3, 2):
            index = (self.c, self.a, self.b, lax.rem(self.z + step, 4))
            self.arrive(index)
            self.push(index, self.peer_b)
            self.push(index, self.peer_a)
            self.push(index, self.sibling)

    def phase_b(self):
        for step in (0, 1, 3, 2):
            index = (self.c, self.a, 1 - self.b, lax.rem(self.z + step, 4))
            self.arrive(index)
            self.push(index, self.peer_a)
            self.push(index, self.sibling)

    def phase_a(self):
        for bb in (self.b, 1 - self.b):
            for step in (0, 1, 3, 2):
                index = (self.c, 1 - self.a, bb, lax.rem(self.z + step, 4))
                self.arrive(index)
                self.push(index, self.sibling)

    def phase_sibling(self):
        for aa in range(2):
            for bb in range(2):
                for zz in range(4):
                    self.arrive((1 - self.c, aa, bb, zz))

    def finish(self):
        own = (self.c, self.a, self.b, self.z)
        ref = self.buf.at[own]
        for n in range(self.count):
            remote(ref, ref, self.send.at[n], self.recv.at[slot(*own)], self.sibling).wait_send()


def low_lanes(rows):
    return lax.broadcasted_iota(jnp.int32, (rows, 128), 1) < 64


def turn(v):
    return pltpu.roll(v, 64, axis=1)


def load_rows(flat, scr, rows, tiles2):
    if tiles2 % 2 == 0:
        nt = tiles2 // 2
        for t in range(nt):
            scr[t, 0:rows, :] = flat[pl.ds(t, rows, stride=nt), :]
        return
    half, h = rows // 2, (tiles2 - 1) // 2
    low = low_lanes(half)
    pair = [flat[pl.ds(t, half, stride=tiles2), :] for t in range(tiles2)]
    turned = {t: turn(pair[t]) for t in range(h, tiles2)}
    for j in range(h + 1):
        even = pair[j] if j < h else jnp.where(low, pair[h], 0.0)
        odd = jnp.where(low, turned[h + j], turned[h + j + 1] if j < h else 0.0)
        scr[j, pl.ds(0, half, stride=2), :] = even
        scr[j, pl.ds(1, half, stride=2), :] = odd


def store_rows(scr, flat, rows, tiles2, base=0):
    if tiles2 % 2 == 0:
        nt = tiles2 // 2
        for t in range(nt):
            flat[pl.ds(t, rows, stride=nt), :] = scr[base + t, 0:rows, :]
        return
    half, h = rows // 2, (tiles2 - 1) // 2
    low = low_lanes(half)
    even = [scr[base + j, pl.ds(0, half, stride=2), :] for j in range(h + 1)]
    odd = [turn(scr[base + j, pl.ds(1, half, stride=2), :]) for j in range(h + 1)]
    for t in range(tiles2):
        if t < h:
            value = even[t]
        elif t == h:
            value = jnp.where(low, even[h], odd[0])
        else:
            value = jnp.where(low, odd[t - h - 1], odd[t - h])
        flat[pl.ds(t, half, stride=tiles2), :] = value


PARTS = {
    "q": ((0, 0, 9, 18),),
    "kv": ((1, 0, 3, 18), (2, 2, 3, 18)),
    "o": ((3, 0, 9, 18),),
    "g": ((4, 0, 24, 18),),
    "u": ((5, 0, 24, 18),),
    "d": ((6, 0, 9, 48),),
}


def pack_slab(name, scr, fold_scr, slab, off, gains=None):
    if name == "d":
        for t in range(5):
            slab[:, off + 128 * t : off + 128 * (t + 1)] = scr[t, 0:48, :].astype(slab.dtype)
        return
    padded, fold, chunks = UNITS[name]
    for t in range(padded // 128):
        slab[:, off + 128 * t : off + 128 * (t + 1)] = scr[t, 0:16, :].astype(slab.dtype)
    fold_scr[...] = jnp.zeros_like(fold_scr)
    per = fold // 128
    for q in range(chunks):
        for k in range(per):
            for e in range(2):
                fold_scr[e * 8 + q : e * 8 + q + 1, 128 * k : 128 * (k + 1)] = scr[q * per + k, 16 + e : 17 + e, :]
    if gains is not None:
        fold_scr[7:8, 0:128] = gains
    slab[:, off + padded : off + padded + fold] = fold_scr[:, 0:fold].astype(slab.dtype)


def unpack_slab(name, main, scr, fold_scr):
    if name == "d":
        for t in range(5):
            scr[t, 0:48, :] = main[:, 128 * t : 128 * (t + 1)]
        return
    padded, fold, chunks = UNITS[name]
    for t in range(padded // 128):
        scr[t, 0:16, :] = main[:, 128 * t : 128 * (t + 1)]
    fold_scr[:, 0:fold] = main[:, padded : padded + fold]
    per = fold // 128
    for q in range(chunks):
        for k in range(per):
            for e in range(2):
                scr[q * per + k, 16 + e : 17 + e, :] = fold_scr[e * 8 + q : e * 8 + q + 1, 128 * k : 128 * (k + 1)]


def spread(name, buf, off, spread_ref, dest):
    padded, fold, chunks = UNITS[name]

    def plane(z, _):
        folded = buf[:, :, :, z, :, off + padded : off + padded + fold].reshape(128, fold)
        for q in range(chunks):
            main = buf[:, :, :, z, :, off + q * fold : off + (q + 1) * fold].reshape(128, fold)
            both = jnp.concatenate([main, folded], axis=0)
            block = jnp.dot(spread_ref[q], both, preferred_element_type=F32)
            dest[pl.ds(pl.multiple_of(z * 144, 16), 144), q * fold : (q + 1) * fold] = block.astype(dest.dtype)
        return 0

    lax.fori_loop(0, 4, plane, 0)


def spread_down(buf, dest):
    for z in range(4):
        for d in range(8):
            y, x, c = d // 4, (d // 2) % 2, d % 2
            a, b = (y, x) if c == 0 else (x, y)
            dest[(z * 8 + d) * 48 : (z * 8 + d + 1) * 48, :] = buf[c, a, b, z].astype(dest.dtype)


def collect(name, source, buf, off, collect_ref, extra=None):
    padded, fold, chunks = UNITS[name]

    def plane(z, _):
        rows = pl.ds(pl.multiple_of(z * 144, 16), 144)
        total = jnp.zeros((128, fold), F32)
        for q in range(chunks):
            block = source[rows, q * fold : (q + 1) * fold].astype(BF)
            both = jnp.dot(collect_ref[q], block, preferred_element_type=F32)
            buf[:, :, :, z, :, off + q * fold : off + (q + 1) * fold] = (
                both[0:128].astype(BF).reshape(2, 2, 2, 16, fold)
            )
            total = total + both[128:256]
        if extra is not None:
            total = total + extra(z)
        buf[:, :, :, z, :, off + padded : off + padded + fold] = total.astype(BF).reshape(2, 2, 2, 16, fold)
        return 0

    lax.fori_loop(0, 4, plane, 0)


def collect_down(source, buf):
    for z in range(4):
        for d in range(8):
            y, x, c = d // 4, (d // 2) % 2, d % 2
            a, b = (y, x) if c == 0 else (x, y)
            buf[c, a, b, z] = source[(z * 8 + d) * 48 : (z * 8 + d + 1) * 48, :].astype(BF)


def load_unit(name, flats, scr):
    for index, tile, tiles2, rows in PARTS[name]:
        view = scr if tile == 0 else scr.at[pl.ds(tile, (tiles2 + 1) // 2)]
        load_rows(flats[index], view, rows, tiles2)


def read_gains(buf, select_ref, lanes_ref, gains_out):
    rows = gain_rows(buf[:, :, :, :, :, 640:768].reshape(512, 128), select_ref)
    wide = jnp.dot(rows.astype(BF), lanes_ref[...], preferred_element_type=F32)
    device = lax.broadcasted_iota(jnp.int32, wide.shape, 0)
    column = lax.broadcasted_iota(jnp.int32, wide.shape, 1)
    low = device * 36
    keep = jnp.logical_and(column >= low, column < low + 36)
    gains_out[...] = jnp.sum(jnp.where(keep, wide, 0.0), axis=0, keepdims=True)


def gain_rows(folds, select_ref):
    return jnp.dot(select_ref[...], folds, preferred_element_type=F32)


def vmem():
    return pl.BlockSpec(memory_space=pltpu.VMEM)


def slab_buffers():
    return [pltpu.VMEM((2, 2, 2, 4) + group_shape(group), BF) for group in GROUPS]


NN = (((1,), (0,)), ((), ()))
NT = (((1,), (1,)), ((), ()))
TN = (((0,), (0,)), ((), ()))
TILES = 5
BLOCK = 256
LOG2E = 1.4426950408889634


def mm(left, right, dims=NN):
    return lax.dot_general(left, right, dims, preferred_element_type=F32)


def block_rows(i, size=BLOCK):
    return pl.ds(pl.multiple_of(i * size, size), size)


def frequencies():
    half = HEAD_DIM // 2
    freqs = rope_base ** (-np.arange(half) * 2.0 / HEAD_DIM)
    return np.tile(freqs.astype(np.float32), 4).reshape(1, 128)


def lane(shape):
    return lax.broadcasted_iota(jnp.int32, shape, len(shape) - 1)


def cos_sin(angle):
    turns = jnp.floor(angle * 0.6366197723675814 + 0.5)
    rest = ((angle - turns * 1.5703125) - turns * 4.837512969970703e-4) - turns * 7.549789948768648e-8
    square = rest * rest
    sine = rest + rest * square * (
        -1.6666654611e-1 + square * (8.3321608736e-3 + square * -1.9515295891e-4)
    )
    cosine = (1.0 - 0.5 * square) + square * square * (
        4.166664568298827e-2 + square * (-1.388731625493765e-3 + square * 2.443315711809948e-5)
    )
    quarter = turns - 4.0 * jnp.floor(turns * 0.25)
    odd = jnp.logical_or(quarter == 1.0, quarter == 3.0)
    swapped_cos = jnp.where(odd, sine, cosine)
    swapped_sin = jnp.where(odd, cosine, sine)
    cos_sign = jnp.logical_or(quarter == 1.0, quarter == 2.0)
    return (
        jnp.where(cos_sign, -swapped_cos, swapped_cos),
        jnp.where(quarter >= 2.0, -swapped_sin, swapped_sin),
    )


def make_tables(positions, freqs, cos_ref, sin_ref):
    for r in range(SEQ // 128):
        row = jnp.broadcast_to(positions[r : r + 1, :].astype(F32), (128, 128))
        column = jnp.sum(jnp.where(diagonal(128), row, 0.0), axis=1, keepdims=True)
        cosine, sine = cos_sin(column * freqs[...])
        cos_ref[128 * r : 128 * (r + 1), :] = cosine
        sin_ref[128 * r : 128 * (r + 1), :] = jnp.where(lax.rem(lane((128, 128)), 64) < 32, -sine, sine)


def rotate_tile(value, cosine, sine, inverse=False):
    first = lax.rem(lane(value.shape), 64) < 32
    swapped = jnp.where(first, pltpu.roll(value, 96, axis=1), pltpu.roll(value, 32, axis=1))
    if inverse:
        return value * cosine - swapped * sine
    return value * cosine + swapped * sine


def row_scale(value):
    return lax.rsqrt(jnp.sum(value * value, axis=1, keepdims=True) * (1.0 / D) + eps_norm)


def turn_over(source, dest):
    def body(i, _):
        rows = block_rows(i)
        dest[rows, :] = source[:, rows].T
        return 0

    lax.fori_loop(0, SEQ // BLOCK, body, 0)


def normalize_tokens(tokens, gain, a_ref):
    def body(i, _):
        rows = block_rows(i)
        x = tokens[rows, :].astype(F32)
        a_ref[rows, :] = (x * row_scale(x) * gain).astype(BF)
        return 0

    lax.fori_loop(0, SEQ // BLOCK, body, 0)


def heads_in(a_ref, w_q, w_kv, cos_ref, sin_ref, q_ref, k_ref, v_ref):
    def body(i, _):
        rows = block_rows(i)
        a = a_ref[rows, :]
        cosine, sine = cos_ref[rows, :], sin_ref[rows, :]
        pq = mm(a, w_q[...])
        for t in range(TILES):
            turned = rotate_tile(pq[:, 128 * t : 128 * (t + 1)], cosine, sine).astype(BF)
            q_ref[t, rows, :] = turned * jnp.asarray(HEAD_DIM ** (-0.5), BF)
        pkv = mm(a, w_kv[...])
        low = lane((BLOCK, 128)) < 64
        for ref, base, rotary in ((k_ref, 0, True), (v_ref, 256, False)):
            for half in range(2):
                tile = pkv[:, base + 128 * half : base + 128 * (half + 1)]
                if rotary:
                    tile = rotate_tile(tile, cosine, sine)
                other = turn(tile)
                ref[2 * half, rows, :] = jnp.where(low, tile, other).astype(BF)
                if half == 0:
                    ref[1, rows, :] = jnp.where(low, other, tile).astype(BF)
        return 0

    lax.fori_loop(0, SEQ // BLOCK, body, 0)


def own_lanes(value, parity):
    here = lane(value.shape) // 64 == parity
    return jnp.where(here, value, jnp.zeros_like(value))


def attend_group(g, q_ref, k_ref, v_ref, o_ref, lse_ref):
    for h in range(HEADS // KV_HEADS):
        j = 3 * g + h
        t, parity = j // 2, lax.rem(j, 2)
        for i in range(SEQ // BLOCK):
            end = BLOCK * (i + 1)
            query = q_ref[t, BLOCK * i : end, :]
            s = mm(own_lanes(k_ref[g, 0:end, :], parity), query, NT)
            rows = lax.broadcasted_iota(jnp.int32, (BLOCK, BLOCK), 0)
            cols = lax.broadcasted_iota(jnp.int32, (BLOCK, BLOCK), 1)
            corner = jnp.where(cols >= rows, s[BLOCK * i :, :], -1e30)
            s = jnp.concatenate([s[: BLOCK * i, :], corner], axis=0) if i else corner
            top = jnp.max(s, axis=0, keepdims=True)
            weights = jnp.exp2((s - top) * LOG2E)
            total = jnp.sum(weights, axis=0, keepdims=True)
            probs = (weights * (1.0 / total)).astype(BF)
            out = mm(probs, own_lanes(v_ref[g, 0:end, :], parity), TN)
            o_ref[t, BLOCK * i : end, :] += out.astype(BF)
            lse_ref[j, :, BLOCK * i : end] = top * LOG2E + jnp.log2(total)


def attend_all(q_ref, k_ref, v_ref, o_ref, lse_ref, between=()):
    o_ref[...] = jnp.zeros_like(o_ref)

    def body(g, _):
        attend_group(g, q_ref, k_ref, v_ref, o_ref, lse_ref)
        for number, action in enumerate(between):
            pl.when(g == number)(action)
        return 0

    lax.fori_loop(0, KV_HEADS, body, 0)


def feed_forward(tokens, cot, gain, w_o, w_g, w_u, w_d, o_ref, out_ref, h_ref, z_ref, dg_ref, du_ref, e_ref, dx_ref, do_ref, d_ref, gain_ref):
    gain_ref[...] = jnp.zeros_like(gain_ref)

    def body(i, _):
        rows = block_rows(i)
        o = jnp.concatenate([o_ref[t, rows, :] for t in range(TILES)], axis=1)
        x2 = tokens[rows, :].astype(F32) + mm(o[:, 0:D], w_o[:, 0:D])
        r2 = row_scale(x2)
        n2 = x2 * r2
        h = (n2 * gain).astype(BF)
        h_ref[rows, :] = h
        c = cot[rows, :]
        gate = mm(h, w_g[...])
        upper = mm(h, w_u[...])
        grad = mm(c, w_d[:, 0:D], NT)
        sigma = 0.5 * jnp.tanh(0.5 * gate) + 0.5
        silu = gate * sigma
        z = (silu * upper).astype(BF)
        z_ref[rows, :] = z
        dg = (grad * upper * (sigma + silu * (1.0 - sigma))).astype(BF)
        du = (grad * silu).astype(BF)
        dg_ref[rows, :] = dg
        du_ref[rows, :] = du
        out_ref[:, rows] = (x2 + mm(z, w_d[:, 0:D])).T
        dh = mm(dg, w_g[...], NT) + mm(du, w_u[...], NT)
        gain_ref[...] += jnp.sum(dh * n2, axis=0, keepdims=True)
        scaled = dh * gain
        mean = jnp.sum(scaled * n2, axis=1, keepdims=True) * (1.0 / D)
        dx = c.astype(F32) + r2 * (scaled - n2 * mean)
        dx_ref[rows, :] = dx
        e = dx.astype(BF)
        e_ref[rows, :] = e
        do = mm(e, w_o[:, 0:D], NT)
        pick = (lax.broadcasted_iota(jnp.int32, (8, 128), 0) == lane((8, 128)) // 64).astype(BF)
        for t in range(TILES):
            if t < TILES - 1:
                tile = do[:, 128 * t : 128 * (t + 1)]
            else:
                tile = jnp.concatenate([do[:, 512:576], jnp.zeros((BLOCK, 64), F32)], axis=1)
            tile = tile.astype(BF)
            do_ref[t, rows, :] = tile
            product = tile.astype(F32) * o[:, 128 * t : 128 * (t + 1)].astype(F32)
            high = product.astype(BF)
            low = (product - high.astype(F32)).astype(BF)
            inner = mm(pick, high, NT) + mm(pick, low, NT)
            d_ref[2 * t, :, rows] = inner[0:1]
            if t < TILES - 1:
                d_ref[2 * t + 1, :, rows] = inner[1:2]
        return 0

    lax.fori_loop(0, SEQ // BLOCK, body, 0)


def down_gradient(z_ref, cot, g_d):
    for k in range(3):
        g_d[512 * k : 512 * (k + 1), 0:D] = mm(z_ref[:, 512 * k : 512 * (k + 1)], cot[...], TN).astype(BF)
    g_d[:, D:] = jnp.zeros((FF, 64), BF)


def wide_gradient(h_ref, d_ref, g):
    for k in range(3):
        g[:, 512 * k : 512 * (k + 1)] = mm(h_ref[...], d_ref[:, 512 * k : 512 * (k + 1)], TN).astype(BF)


def out_gradient(o_ref, e_ref, g_o):
    for t in range(TILES):
        part = mm(o_ref[t], e_ref[...], TN).astype(BF)
        if t < TILES - 1:
            g_o[128 * t : 128 * (t + 1), 0:D] = part
        else:
            g_o[512:576, 0:D] = part[0:64]
    g_o[:, D:] = jnp.zeros((D, 64), BF)


def attend_back_group(g, q_ref, k_ref, v_ref, do_ref, lse_ref, d_ref, dq_ref, dk_ref, dv_ref):
    for h in range(HEADS // KV_HEADS):
        j = 3 * g + h
        t, parity = j // 2, lax.rem(j, 2)
        for i in range(SEQ // BLOCK):
            start = BLOCK * i
            rows = slice(start, start + BLOCK)
            key = own_lanes(k_ref[g, rows, :], parity)
            value = own_lanes(v_ref[g, rows, :], parity)
            query, grad = q_ref[t, start:, :], do_ref[t, start:, :]
            probs = jnp.exp2(mm(key, query, NT) * LOG2E - lse_ref[j, :, start:])
            down = lax.broadcasted_iota(jnp.int32, (BLOCK, BLOCK), 0)
            across = lax.broadcasted_iota(jnp.int32, (BLOCK, BLOCK), 1)
            corner = jnp.where(across >= down, probs[:, :BLOCK], 0.0)
            probs = jnp.concatenate([corner, probs[:, BLOCK:]], axis=1) if start + BLOCK < SEQ else corner
            ds = (probs * (mm(value, grad, NT) - d_ref[j, :, start:])).astype(BF)
            dv_ref[g, parity, rows, :] += mm(probs.astype(BF), grad)
            dk_ref[g, parity, rows, :] += mm(ds, query)
            dq_ref[t, start:, :] += mm(ds, key, TN)


def attend_back_all(q_ref, k_ref, v_ref, do_ref, lse_ref, d_ref, dq_ref, dk_ref, dv_ref):
    dq_ref[...] = jnp.zeros_like(dq_ref)
    dk_ref[...] = jnp.zeros_like(dk_ref)
    dv_ref[...] = jnp.zeros_like(dv_ref)

    def body(g, _):
        attend_back_group(g, q_ref, k_ref, v_ref, do_ref, lse_ref, d_ref, dq_ref, dk_ref, dv_ref)
        return 0

    lax.fori_loop(0, KV_HEADS, body, 0)


def heads_out(dq_ref, dk_ref, dv_ref, cos_ref, sin_ref, dpq_ref, dkv_ref):
    def body(i, _):
        rows = block_rows(i)
        cosine, sine = cos_ref[rows, :], sin_ref[rows, :]
        for t in range(TILES):
            tile = dq_ref[t, rows, :] * HEAD_DIM ** (-0.5)
            dpq_ref[rows, 128 * t : 128 * (t + 1)] = rotate_tile(tile, cosine, sine, True).astype(BF)
        low = lane((BLOCK, 128)) < 64
        for ref, base, rotary in ((dk_ref, 0, True), (dv_ref, 256, False)):
            whole = [ref[g, 0, rows, :] + turn(ref[g, 1, rows, :]) for g in range(KV_HEADS)]
            tiles = (jnp.where(low, whole[0], turn(whole[1])), jnp.where(low, whole[2], 0.0))
            for half in range(2):
                tile = rotate_tile(tiles[half], cosine, sine, True) if rotary else tiles[half]
                dkv_ref[rows, base + 128 * half : base + 128 * (half + 1)] = tile.astype(BF)
        return 0

    lax.fori_loop(0, SEQ // BLOCK, body, 0)


def first_gradients(a_ref, dpq_ref, dkv_ref, g_q, g_kv):
    g_q[...] = mm(a_ref[...], dpq_ref[...], TN).astype(BF)
    g_kv[...] = mm(a_ref[...], dkv_ref[...], TN).astype(BF)


def input_gradient(tokens, gain, dx_ref, dpq_ref, dkv_ref, w_q, w_kv, out_ref, gain_ref):
    gain_ref[...] = jnp.zeros_like(gain_ref)

    def body(i, _):
        rows = block_rows(i)
        da = mm(dpq_ref[rows, :], w_q[...], NT) + mm(dkv_ref[rows, :], w_kv[...], NT)
        x = tokens[rows, :].astype(F32)
        r1 = row_scale(x)
        n1 = x * r1
        gain_ref[...] += jnp.sum(da * n1, axis=0, keepdims=True)
        scaled = da * gain
        mean = jnp.sum(scaled * n1, axis=1, keepdims=True) * (1.0 / D)
        out_ref[:, rows] = (dx_ref[rows, :] + r1 * (scaled - n1 * mean)).T
        return 0

    lax.fori_loop(0, SEQ // BLOCK, body, 0)


FRONT_OUTS = (
    ((D, SEQ), F32),
    ((SEQ, D), BF),
    ((SEQ, D), BF),
    ((SEQ, 128), F32),
    ((SEQ, 128), F32),
    ((TILES, SEQ, 128), BF),
    ((KV_HEADS, SEQ, 128), BF),
    ((KV_HEADS, SEQ, 128), BF),
    ((HEADS, 1, SEQ), F32),
    ((TILES, SEQ, 128), BF),
    ((HEADS, 1, SEQ), F32),
    ((SEQ, D), F32),
    ((D, 640), BF),
    ((D, FF), BF),
    ((D, FF), BF),
    ((FF, 640), BF),
    ((1, D), F32),
)
FRONT_SCRATCH = (
    ((SEQ, D), BF),
    ((TILES, SEQ, 128), BF),
    ((SEQ, D), BF),
    ((SEQ, FF), BF),
    ((SEQ, FF), BF),
    ((SEQ, FF), BF),
    ((SEQ, D), BF),
)


def front(tok_t, positions, cot_t, freqs, outs, scratch, begin, first, between, second):
    out_ref, tok, a_ref, cos_ref, sin_ref, q_ref, k_ref, v_ref, lse_ref, do_ref, d_ref, dx_ref, g_o, g_g, g_u, g_d, gain_ref = outs
    cot, o_ref, h_ref, z_ref, dg_ref, du_ref, e_ref = scratch
    begin()
    turn_over(tok_t, tok)
    turn_over(cot_t, cot)
    make_tables(positions, freqs, cos_ref, sin_ref)
    w_q, w_kv, gains = first()
    normalize_tokens(tok, gains[:, 0:D], a_ref)
    heads_in(a_ref, w_q, w_kv, cos_ref, sin_ref, q_ref, k_ref, v_ref)
    attend_all(q_ref, k_ref, v_ref, o_ref, lse_ref, between)
    w_o, w_g, w_u, w_d = second()
    feed_forward(tok, cot, gains[:, D : 2 * D], w_o, w_g, w_u, w_d, o_ref, out_ref, h_ref, z_ref, dg_ref, du_ref, e_ref, dx_ref, do_ref, d_ref, gain_ref)
    down_gradient(z_ref, cot, g_d)
    wide_gradient(h_ref, dg_ref, g_g)
    wide_gradient(h_ref, du_ref, g_u)
    out_gradient(o_ref, e_ref, g_o)


def front_kernel(tok_t, positions, cot_t, freqs, gains, w_q, w_kv, w_o, w_g, w_u, w_d, *refs):
    count = len(FRONT_OUTS)
    front(
        tok_t,
        positions,
        cot_t,
        freqs,
        refs[:count],
        refs[count:],
        lambda: None,
        lambda: (w_q, w_kv, gains),
        (),
        lambda: (w_o, w_g, w_u, w_d),
    )


def front_gather_kernel(tok_t, positions, cot_t, freqs, *refs):
    w = refs[0:7]
    gains_ref, spread_ref, select_ref, lanes_ref = refs[7:11]
    k = 11
    outs = refs[k : k + len(FRONT_OUTS)]
    k += len(FRONT_OUTS)
    nat_q, nat_kv, gains = refs[k : k + 3]
    k += 3
    scratch = refs[k : k + len(FRONT_SCRATCH)]
    k += len(FRONT_SCRATCH)
    nat_o, nat_g, nat_u, nat_d = refs[k : k + 4]
    bufs = refs[k + 4 : k + 8]
    scr, fold_scr, send, recv = refs[k + 8 : k + 12]
    natural = {"q": nat_q, "kv": nat_kv, "o": nat_o, "g": nat_g, "u": nat_u}

    where = coords()
    me, (z, a, b, c), peer_a, peer_b, sibling, along = where
    peers = (along(1), along(2), along(3), peer_a, peer_b, sibling)
    moves = [Gather(buf, send.at[n], recv.at[n], where) for n, buf in enumerate(bufs)]
    late = moves[1:]

    def begin():
        barrier = say_hello(peers)
        for group, buf in zip(GROUPS, bufs):
            for name in group:
                load_unit(name, w, scr)
                own_gains = None
                if name == "q":
                    fold_scr[0:1, 0:128] = jnp.zeros((1, 128), F32)
                    fold_scr[0:1, 0:36] = gains_ref[...]
                    own_gains = fold_scr[0:1, 0:128]
                pack_slab(name, scr, fold_scr, buf.at[c, a, b, z], unit_offset(name), own_gains)
        pl.semaphore_wait(barrier, len(peers))
        moves[0].phase_own()

    def first():
        moves[0].phase_z()
        moves[0].phase_b()
        moves[0].phase_a()
        for move in late:
            move.phase_own()
        moves[0].phase_sibling()
        for name in GROUPS[0]:
            spread(name, bufs[0], unit_offset(name), spread_ref, natural[name])
        read_gains(bufs[0], select_ref, lanes_ref, gains)
        return nat_q, nat_kv, gains

    def phase_z():
        for move in late:
            move.phase_z()

    def phase_b():
        for move in late:
            move.phase_b()

    def phase_a():
        for move in late:
            move.phase_a()

    def second():
        for n in (1, 2):
            moves[n].phase_sibling()
            for name in GROUPS[n]:
                spread(name, bufs[n], unit_offset(name), spread_ref, natural[name])
        moves[3].phase_sibling()
        spread_down(bufs[3], nat_d)
        return nat_o, nat_g, nat_u, nat_d

    front(tok_t, positions, cot_t, freqs, outs, scratch, begin, first, (phase_z, phase_b, phase_a), second)
    for move in moves:
        move.finish()


def back_kernel(tokens, gains, w_q, w_kv, a_ref, cos_ref, sin_ref, q_ref, k_ref, v_ref, lse_ref, do_ref, d_ref, dx_ref, out_ref, g_q, g_kv, gain_ref, dq_ref, dk_ref, dv_ref, dpq_ref, dkv_ref):
    attend_back_all(q_ref, k_ref, v_ref, do_ref, lse_ref, d_ref, dq_ref, dk_ref, dv_ref)
    heads_out(dq_ref, dk_ref, dv_ref, cos_ref, sin_ref, dpq_ref, dkv_ref)
    first_gradients(a_ref, dpq_ref, dkv_ref, g_q, g_kv)
    input_gradient(tokens, gains[:, 0:D], dx_ref, dpq_ref, dkv_ref, w_q, w_kv, out_ref, gain_ref)


def local_call(kernel, name, args, outs, scratch):
    return pl.pallas_call(
        kernel,
        out_shape=tuple(jax.ShapeDtypeStruct(*o) for o in outs),
        in_specs=[vmem()] * len(args),
        out_specs=(vmem(),) * len(outs),
        scratch_shapes=[pltpu.VMEM(*s) for s in scratch],
        compiler_params=pltpu.CompilerParams(vmem_limit_bytes=60 * 2**20),
        name=name,
    )(*args)


def front_inputs(tokens, positions, cotangent):
    return tokens.T, positions.reshape(-1, 128), cotangent.T, jnp.asarray(frequencies())


def front_local(tokens, positions, cotangent, gains, natural):
    args = (*front_inputs(tokens, positions, cotangent), gains, *natural)
    return local_call(front_kernel, "forward_and_feed_forward_back", args, FRONT_OUTS, FRONT_SCRATCH)


def front_gather(tokens, positions, cotangent, shards, gains, consts):
    spread_c, _, select_c, lanes_c = consts
    args = (*front_inputs(tokens, positions, cotangent), *shards, gains, spread_c, select_c, lanes_c)
    outs = FRONT_OUTS + (((D, 640), BF), ((D, 512), BF), ((1, 2 * D), F32))
    scratch = FRONT_SCRATCH + (((D, 640), BF), ((D, FF), BF), ((D, FF), BF), ((FF, 640), BF))
    return pl.pallas_call(
        front_gather_kernel,
        out_shape=tuple(jax.ShapeDtypeStruct(*o) for o in outs),
        in_specs=[vmem()] * len(args),
        out_specs=(vmem(),) * len(outs),
        scratch_shapes=[pltpu.VMEM(*s) for s in scratch]
        + slab_buffers()
        + [
            pltpu.VMEM((12, 48, 128), F32),
            pltpu.VMEM((16, 256), F32),
            pltpu.SemaphoreType.DMA((4, 31)),
            pltpu.SemaphoreType.DMA((4, 32)),
        ],
        compiler_params=pltpu.CompilerParams(
            collective_id=0, has_side_effects=True, vmem_limit_bytes=62 * 2**20
        ),
        name="gather_and_forward",
    )(*args)


def back_local(front_outs, gains, w_q, w_kv):
    out, tok, a, cosine, sine, q, k, v, lse, do, inner, dx, g_o, g_g, g_u, g_d, gain_two = front_outs
    T = SEQ
    input_grad, g_q, g_kv, gain_one = local_call(
        back_kernel,
        "attention_back",
        (tok, gains, w_q, w_kv, a, cosine, sine, q, k, v, lse, do, inner, dx),
        (((D, T), F32), ((D, 640), BF), ((D, 512), BF), ((1, D), F32)),
        (
            ((TILES, T, 128), F32),
            ((KV_HEADS, 2, T, 128), F32),
            ((KV_HEADS, 2, T, 128), F32),
            ((T, 640), BF),
            ((T, 512), BF),
        ),
    )
    return out.T, input_grad.T, (g_q, g_kv, g_o, g_g, g_u, g_d), gain_one, gain_two


def layer(tokens, positions, cotangent, gains, *natural):
    outs = front_local(tokens, positions, cotangent, gains, natural)
    return back_local(outs, gains, natural[0], natural[1])


OWNERS = {"q": 16, "kv": 18, "o": 12, "g": 8, "u": 22, "d": 14}
UNIT_NAMES = ("q", "kv", "o", "g", "u", "d")


class Reduce:
    def __init__(self, buf, r1, r2, r3, r4, send, recv, where):
        self.buf, self.r1, self.r2, self.r3, self.r4 = buf, r1, r2, r3, r4
        self.send, self.recv = send, recv
        self.me, (self.z, self.a, self.b, self.c), self.peer_a, self.peer_b, self.sibling, self.along = where
        self.copies = {}

    def push(self, k, src, dst, target):
        copy = remote(src, dst, self.send.at[k], self.recv.at[k], target)
        copy.start()
        self.copies[k] = copy

    def stage_one(self):
        self.push(0, self.buf.at[1 - self.c, 1 - self.b], self.r1.at[1 - self.b], self.sibling)
        self.push(1, self.buf.at[1 - self.c, self.b], self.r1.at[self.b], self.sibling)

    def add(self, buf, index, got, count):
        def body(i, _):
            bb, zz = i // 4, lax.rem(i, 4)
            here = index + ((bb, zz) if len(index) == 2 else (zz,))
            there = got[1] + ((bb, zz) if len(index) == 2 else (zz,))
            buf[here] = (buf[here].astype(F32) + got[0][there].astype(F32)).astype(BF)
            return 0

        lax.fori_loop(0, count, body, 0)

    def stage_two(self):
        self.copies[0].wait_recv()
        self.add(self.buf, (self.c, 1 - self.a), (self.r1, (1 - self.a,)), 8)
        self.push(2, self.buf.at[self.c, 1 - self.a], self.r2, self.peer_a)
        self.copies[1].wait_recv()
        self.add(self.buf, (self.c, self.a), (self.r1, (self.a,)), 8)

    def stage_three(self):
        self.copies[2].wait_recv()
        self.add(self.buf, (self.c, self.a, 1 - self.b), (self.r2, (1 - self.b,)), 4)
        self.push(3, self.buf.at[self.c, self.a, 1 - self.b], self.r3, self.peer_b)
        self.add(self.buf, (self.c, self.a, self.b), (self.r2, (self.b,)), 4)

    def stage_four(self):
        self.copies[3].wait_recv()
        self.add(self.buf, (self.c, self.a, self.b), (self.r3, ()), 4)
        for step in (1, 3, 2):
            index = (self.c, self.a, self.b, lax.rem(self.z + step, 4))
            self.push(3 + step, self.buf.at[index], self.r4.at[step - 1], self.along(step))

    def result(self, total):
        for step in (1, 3, 2):
            self.copies[3 + step].wait_recv()
        own = self.buf[self.c, self.a, self.b, self.z].astype(F32)
        total[...] = (
            own + self.r4[0].astype(F32) + self.r4[1].astype(F32) + self.r4[2].astype(F32)
        )

    def finish(self):
        for copy in self.copies.values():
            copy.wait_send()


def diagonal(n):
    return lax.broadcasted_iota(jnp.int32, (n, n), 0) == lax.broadcasted_iota(jnp.int32, (n, n), 1)


def newton_schulz(state, cols=None):
    def read():
        return state[...] if cols is None else state[:, cols]

    def write(value):
        if cols is None:
            state[...] = value
        else:
            state[:, cols] = value

    whole = read()
    tall = whole.shape[0] > whole.shape[1]
    n = min(whole.shape)
    norm = jnp.sqrt(jnp.sum(jnp.sum(whole * whole, axis=1, keepdims=True), axis=0, keepdims=True))
    write(whole / (norm + 1e-07))

    def trace(square):
        kept = jnp.where(diagonal(n), square, 0.0)
        return jnp.sum(jnp.sum(kept, axis=1, keepdims=True), axis=0, keepdims=True) * (1.0 / n)

    def turn_once(_, carry):
        value = read()
        low = value.astype(BF)
        dims = (((0,), (0,)), ((), ())) if tall else (((1,), (1,)), ((), ()))
        gram = lax.dot_general(low, low, dims, preferred_element_type=F32)
        mean = trace(gram)
        rest = gram - jnp.where(diagonal(n), mean, 0.0)
        small = rest.astype(BF)
        rest = (coef_two + 2.0 * coef_three * mean) * rest + coef_three * jnp.dot(
            small, small, preferred_element_type=F32
        )
        more = trace(rest)
        poly = (rest - jnp.where(diagonal(n), more, 0.0)).astype(BF)
        keep = coef_one + coef_two * mean + coef_three * mean * mean + more
        if tall:
            change = jnp.dot(low, poly, preferred_element_type=F32)
        else:
            change = jnp.dot(poly, low, preferred_element_type=F32)
        write(keep * value + change)
        return carry

    lax.fori_loop(0, NS_ITERS, turn_once, 0)


def reduce_kernel(*refs):
    grads = refs[0:6]
    gain_one, gain_two = refs[6:8]
    m, m_gains = refs[8:15], refs[15]
    spread_ref, collect_ref, select_ref, lanes_back, gain_put = refs[16:21]
    totals = refs[21:25]
    directions = dict(zip(UNIT_NAMES, refs[25:31]))
    k = 31
    bufs = refs[k : k + 4]
    r1, r2, r3, r4 = (refs[k + 4 + 4 * j : k + 8 + 4 * j] for j in range(4))
    k += 20
    scr, fold_scr, lane_scr = refs[k : k + 3]
    k += 3
    old = dict(zip(UNIT_NAMES, refs[k : k + 6]))
    mslab = dict(zip(UNIT_NAMES, refs[k + 6 : k + 12]))
    oslab = dict(zip(UNIT_NAMES, refs[k + 12 : k + 18]))
    k += 18
    own_qo, own_kv, own_gu, own_d = refs[k : k + 4]
    x_qo, x_kv, x_gu, x_d = refs[k + 4 : k + 8]
    k += 8
    rs_send, rs_recv, up_send, up_recv, down_send, down_recv = refs[k : k + 6]

    where = coords()
    me, (z, a, b, c), peer_a, peer_b, sibling, along = where
    own = (c, a, b, z)

    barrier = pltpu.get_barrier_semaphore()

    def hello(j, _):
        @pl.when(j != me)
        def _():
            pl.semaphore_signal(barrier, inc=1, device_id=(j,), device_id_type=MESH)

        return 0

    lax.fori_loop(0, 32, hello, 0)

    row = lax.broadcasted_iota(jnp.int32, (32, 2 * D), 0) * 36
    col = lax.broadcasted_iota(jnp.int32, (32, 2 * D), 1)
    keep = jnp.logical_and(col >= row, col < row + 36)
    both_gains = jnp.concatenate([gain_one[...], gain_two[...]], axis=1)
    by_device = jnp.dot(
        jnp.where(keep, jnp.broadcast_to(both_gains, (32, 2 * D)), 0.0).astype(BF),
        lanes_back[...],
        preferred_element_type=F32,
    ).astype(BF)

    def gain_extra(zz):
        return jnp.dot(gain_put[zz], by_device, preferred_element_type=F32)

    collect_down(grads[5], bufs[3])
    collect("g", grads[3], bufs[2], unit_offset("g"), collect_ref)
    collect("u", grads[4], bufs[2], unit_offset("u"), collect_ref)
    collect("o", grads[2], bufs[1], unit_offset("o"), collect_ref)
    collect("q", grads[0], bufs[0], unit_offset("q"), collect_ref, gain_extra)
    collect("kv", grads[1], bufs[0], unit_offset("kv"), collect_ref)

    lane_scr[0:1, :] = jnp.zeros((1, 128), F32)
    lane_scr[0:1, 0:36] = m_gains[...]
    for name in UNIT_NAMES:
        load_unit(name, m, scr)
        pack_slab(name, scr, fold_scr, old[name], 0, lane_scr[0:1, :] if name == "q" else None)

    pl.semaphore_wait(barrier, 31)

    moves = [
        Reduce(bufs[g], r1[g], r2[g], r3[g], r4[g], rs_send.at[g], rs_recv.at[g], where) for g in range(4)
    ]
    order = (3, 2, 1, 0)
    for g in order:
        moves[g].stage_one()
    for g in order:
        moves[g].stage_two()
    for g in order:
        moves[g].stage_three()
    for g in order:
        moves[g].stage_four()

    up_copies = []

    def to_owner(name, number):
        owner = OWNERS[name]
        held = {"q": own_qo, "o": own_qo, "kv": own_kv, "g": own_gu, "u": own_gu, "d": own_d}[name]

        @pl.when(me != owner)
        def _():
            remote(mslab[name], held.at[own], up_send.at[number], up_recv.at[slot(*own)], owner).start()

        @pl.when(me == owner)
        def _():
            held[own] = mslab[name][...]

    for g in order:
        moves[g].result(totals[g])
        for name in GROUPS[g]:
            off = unit_offset(name)
            width = old[name].shape[1]
            fresh = momentum_decay * old[name][...] + totals[g][:, off : off + width]
            mslab[name][...] = fresh.astype(BF)
            to_owner(name, UNIT_NAMES.index(name))

    def arrived(held):
        def one(j, _):
            @pl.when(j != slot(*own))
            def _():
                ref = held.at[j // 16, lax.rem(j // 8, 2), lax.rem(j // 4, 2), lax.rem(j, 4)]
                remote(ref, ref, up_send.at[0], up_recv.at[j], sibling).wait_recv()

            return 0

        lax.fori_loop(0, 32, one, 0)

    def give_back(held, name_of):
        def one(j, wait):
            cc, aa, bb, zz = j // 16, lax.rem(j // 8, 2), lax.rem(j // 4, 2), lax.rem(j, 4)
            y = aa * (1 - cc) + bb * cc
            x = bb * (1 - cc) + aa * cc
            target = ((zz * 2 + y) * 2 + x) * 2 + cc
            ref = held.at[cc, aa, bb, zz]

            @pl.when(j != slot(*own))
            def _():
                copy = remote(ref, oslab[name_of], down_send.at[j], down_recv.at[UNIT_NAMES.index(name_of)], target)
                if wait:
                    copy.wait_send()
                else:
                    copy.start()

        def start(j, _):
            one(j, False)
            return 0

        def finish(j, _):
            one(j, True)
            return 0

        lax.fori_loop(0, 32, start, 0)
        oslab[name_of][...] = held[own]
        lax.fori_loop(0, 32, finish, 0)

    @pl.when(jnp.logical_or(me == OWNERS["g"], me == OWNERS["u"]))
    def _():
        arrived(own_gu)
        spread("g", own_gu, 0, spread_ref, x_gu)
        newton_schulz(x_gu)
        collect("g", x_gu, own_gu, 0, collect_ref)

        @pl.when(me == OWNERS["g"])
        def _():
            give_back(own_gu, "g")

        @pl.when(me == OWNERS["u"])
        def _():
            give_back(own_gu, "u")

    @pl.when(me == OWNERS["d"])
    def _():
        arrived(own_d)
        spread_down(own_d, x_d)
        newton_schulz(x_d, slice(0, D))
        collect_down(x_d, own_d)
        give_back(own_d, "d")

    @pl.when(jnp.logical_or(me == OWNERS["q"], me == OWNERS["o"]))
    def _():
        arrived(own_qo)
        spread("q", own_qo, 0, spread_ref, x_qo)
        rows_of = gain_rows(own_qo[:, :, :, :, :, 640:768].reshape(512, 128), select_ref)
        squares = jnp.sum(rows_of * rows_of, axis=1, keepdims=True)
        scales = [
            lax.rsqrt(jnp.sum(squares[16 * h : 16 * h + 16], axis=0, keepdims=True) * (1.0 / D) + 1e-06)
            for h in range(2)
        ]
        newton_schulz(x_qo)

        def scale_extra(zz):
            scale = jnp.where(zz < 2, scales[0], scales[1])
            high = scale.astype(BF).astype(F32)
            row16 = lax.rem(lax.broadcasted_iota(jnp.int32, (128, 128), 0), 16)
            return jnp.where(row16 == 7, high, 0.0) + jnp.where(row16 == 15, scale - high, 0.0)

        collect("q", x_qo, own_qo, 0, collect_ref, scale_extra)

        @pl.when(me == OWNERS["q"])
        def _():
            give_back(own_qo, "q")

        @pl.when(me == OWNERS["o"])
        def _():
            give_back(own_qo, "o")

    @pl.when(me == OWNERS["kv"])
    def _():
        arrived(own_kv)
        spread("kv", own_kv, 0, spread_ref, x_kv)
        newton_schulz(x_kv, slice(0, KVD))
        newton_schulz(x_kv, slice(256, 256 + KVD))
        collect("kv", x_kv, own_kv, 0, collect_ref)
        give_back(own_kv, "kv")

    for name in ("d", "g", "u", "o", "kv", "q"):
        number = UNIT_NAMES.index(name)

        @pl.when(me != OWNERS[name])
        def _():
            remote(oslab[name], oslab[name], down_send.at[0], down_recv.at[number], sibling).wait_recv()

        directions[name][...] = oslab[name][...]

    for name in UNIT_NAMES:
        owner = OWNERS[name]
        number = UNIT_NAMES.index(name)
        held = {"q": own_qo, "o": own_qo, "kv": own_kv, "g": own_gu, "u": own_gu, "d": own_d}[name]

        @pl.when(me != owner)
        def _():
            remote(mslab[name], held.at[own], up_send.at[number], up_recv.at[slot(*own)], owner).wait_send()

    for move in moves:
        move.finish()


def collect_constants():
    forward = spread_matrices()
    put = np.zeros((4, 128, 32), np.float32)
    for zz in range(4):
        for d in range(8):
            put[zz, 16 * place_of(d) + 7, 8 * zz + d] = 1
    low = ml_dtypes.bfloat16
    return (
        forward.astype(low),
        forward.transpose(0, 2, 1).astype(low),
        gain_select().astype(low),
        gain_lanes().astype(low),
        gain_lanes().T.astype(low),
        put.astype(low),
    )


def slab_shape(name):
    return (ROWS_D, 640) if name == "d" else (16, unit_width(name))


def reduce_call(grads, gain_one, gain_two, m, m_gains, consts):
    spread_c, collect_c, select_c, _, lanes_back, put = consts
    shape = jax.ShapeDtypeStruct
    slabs = [pltpu.VMEM(slab_shape(n), BF) for n in UNIT_NAMES]
    stages = []
    for lead in ((2, 2, 4), (2, 4), (4,), (3,)):
        stages += [pltpu.VMEM(lead + group_shape(group), BF) for group in GROUPS]
    outs = [shape(group_shape(group), F32) for group in GROUPS] + [shape(slab_shape(n), BF) for n in UNIT_NAMES]
    return pl.pallas_call(
        reduce_kernel,
        out_shape=tuple(outs),
        in_specs=[vmem()] * 21,
        out_specs=(vmem(),) * len(outs),
        scratch_shapes=slab_buffers()
        + stages
        + [pltpu.VMEM((12, 48, 128), F32), pltpu.VMEM((16, 256), F32), pltpu.VMEM((8, 128), F32)]
        + [pltpu.VMEM(slab_shape(n), F32) for n in UNIT_NAMES]
        + slabs
        + slabs
        + [
            pltpu.VMEM((2, 2, 2, 4, 16, unit_width("q")), BF),
            pltpu.VMEM((2, 2, 2, 4, 16, unit_width("kv")), BF),
            pltpu.VMEM((2, 2, 2, 4, 16, unit_width("g")), BF),
            pltpu.VMEM((2, 2, 2, 4, ROWS_D, 640), BF),
            pltpu.VMEM((D, 640), F32),
            pltpu.VMEM((D, 512), F32),
            pltpu.VMEM((D, FF), F32),
            pltpu.VMEM((FF, 640), F32),
            pltpu.SemaphoreType.DMA((4, 7)),
            pltpu.SemaphoreType.DMA((4, 7)),
            pltpu.SemaphoreType.DMA((6,)),
            pltpu.SemaphoreType.DMA((32,)),
            pltpu.SemaphoreType.DMA((32,)),
            pltpu.SemaphoreType.DMA((6,)),
        ],
        compiler_params=pltpu.CompilerParams(
            collective_id=1, has_side_effects=True, vmem_limit_bytes=60 * 2**20
        ),
        name="reduce_and_step",
    )(*grads, gain_one, gain_two, *m, m_gains, spread_c, collect_c, select_c, lanes_back, put)


def finish_kernel(*refs):
    totals = refs[0:4]
    directions = dict(zip(UNIT_NAMES, refs[4:10]))
    w, gains = refs[10:17], refs[17]
    m, m_gains = refs[18:25], refs[25]
    grad_out, grad_gains = refs[26:33], refs[33]
    new_m, new_m_gains = refs[34:41], refs[41]
    new_w, new_gains = refs[42:49], refs[49]
    scr, fold_scr = refs[50:52]
    shapes = matrix_shapes()
    for group, total in zip(GROUPS, totals):
        for name in group:
            off = unit_offset(name)
            unpack_slab(name, total[:, off : off + slab_shape(name)[1]], scr, fold_scr)
            for index, tile, tiles2, rows in PARTS[name]:
                store_rows(scr, grad_out[index], rows, tiles2, tile)
                new_m[index][...] = momentum_decay * m[index][...] + grad_out[index][...]
            if name == "q":
                grad_gains[...] = fold_scr[7:8, 0:36]
                new_m_gains[...] = momentum_decay * m_gains[...] + grad_gains[...]
            unpack_slab(name, directions[name][...].astype(F32), scr, fold_scr)
            for index, tile, tiles2, rows in PARTS[name]:
                store_rows(scr, new_w[index], rows, tiles2, tile)
                rate = 0.2 * math.sqrt(max(shapes[index]))
                old = w[index][...]
                new_w[index][...] = old - matrix_rate * (weight_decay * old + rate * new_w[index][...])
            if name == "q":
                scale = fold_scr[7:8, 0:36] + fold_scr[15:16, 0:36]
                new_gains[...] = gains[...] - gain_rate * (new_m_gains[...] * scale)


def finish_call(slabs, w, gains, m, m_gains):
    outs = [(v.shape, F32) for v in (*w, gains)] * 3
    return local_call(
        finish_kernel, "finish", (*slabs, *w, gains, *m, m_gains), outs, (((12, 48, 128), F32), ((16, 256), F32))
    )


def orthogonal(matrix):
    rows, cols = matrix.shape
    wide = matrix.T if rows > cols else matrix
    state = wide / (jnp.sqrt(jnp.sum(wide * wide)) + 1e-07)
    for turn_number in range(NS_ITERS):
        gram = jnp.dot(state, state.T, precision=precise)
        poly = coef_two * gram + coef_three * jnp.dot(gram, gram, precision=precise)
        state = coef_one * state + jnp.dot(poly, state, precision=precise)
    return state.T if rows > cols else state


def direction_of(index, flat):
    if index < 7:
        return orthogonal(flat.reshape(matrix_shapes()[index])).reshape(-1)
    halves = flat.reshape(2, D)
    return (halves * lax.rsqrt(jnp.mean(halves * halves, axis=1, keepdims=True) + 1e-06)).reshape(-1)


def gather_all(flat):
    return lax.all_gather(flat.astype(BF), "dp", axis=0, tiled=True)


def scatter_sum(whole):
    return lax.psum_scatter(whole, "dp", scatter_dimension=0, tiled=True)


def pad_columns(matrix, width):
    return jnp.pad(matrix, ((0, 0), (0, width - matrix.shape[1])))


def per_device(tokens, positions, cotangent, *rest):
    w, gains, m, m_gains = rest[0:7], rest[7], rest[8:15], rest[15]
    shapes = matrix_shapes()
    whole = [gather_all(v).reshape(s) for v, s in zip(w, shapes)]
    padded = (
        pad_columns(whole[0], 640),
        jnp.concatenate([pad_columns(whole[1], 256), pad_columns(whole[2], 256)], axis=1),
        pad_columns(whole[3], 640),
        whole[4],
        whole[5],
        pad_columns(whole[6], 640),
    )
    block_out, input_grad, grads, *gain_grads = layer(
        tokens, positions, cotangent, gather_all(gains).astype(F32).reshape(1, -1), *padded
    )
    parts = (
        grads[0][:, :D],
        grads[1][:, :KVD],
        grads[1][:, 256 : 256 + KVD],
        grads[2][:, :D],
        grads[3],
        grads[4],
        grads[5][:, :D],
    )
    shares = [scatter_sum(g.astype(F32).reshape(-1)) for g in parts] + [scatter_sum(jnp.concatenate(gain_grads, axis=1).reshape(-1))]
    moments = [momentum_decay * old + share for old, share in zip((*m, m_gains), shares)]
    device = lax.axis_index("dp")
    stride = lax.axis_size("dp") // 8
    pieces = []
    for i in range(8):
        full = gather_all(moments[i]).astype(F32)
        found = lax.cond(
            device == i * stride, lambda v, i=i: direction_of(i, v), jnp.zeros_like, full
        )
        pieces.append(scatter_sum(found))
    updated = []
    for i in range(7):
        scale = 0.2 * math.sqrt(max(shapes[i]))
        updated.append(w[i] - matrix_rate * (weight_decay * w[i] + scale * pieces[i]))
    new_gains = gains - gain_rate * pieces[7]
    return (block_out, input_grad, *moments, *updated, new_gains, *shares)


def per_device_32(tokens, positions, cotangent, *rest):
    w, gains, m, m_gains = rest[0:7], rest[7], rest[8:15], rest[15]
    consts = collect_constants()
    w = [v.reshape(-1, 128) for v in w]
    m = [v.reshape(-1, 128) for v in m]
    gains, m_gains = gains.reshape(1, -1), m_gains.reshape(1, -1)
    *front_outs, w_q, w_kv, whole_gains = front_gather(tokens, positions, cotangent, w, gains, consts[0:4])
    block_out, input_grad, grads, gain_one, gain_two = back_local(front_outs, whole_gains, w_q, w_kv)
    slabs = reduce_call(grads, gain_one, gain_two, m, m_gains, consts)
    flat = [v.reshape(-1) for v in finish_call(slabs, w, gains, m, m_gains)]
    return (block_out, input_grad, *flat[8:16], *flat[16:24], *flat[0:8])


def solution(mesh):
    placed = (P("dp", None), P("dp"), P("dp", None)) + (P("dp"),) * 16
    return jax.shard_map(
        per_device_32 if mesh.shape["dp"] == 32 else per_device,
        mesh=mesh,
        in_specs=placed,
        out_specs=(P("dp", None), P("dp", None)) + (P("dp"),) * 24,
        check_vma=False,
    )
```

```python
import math
import types

import jax
import jax.numpy as jnp
import ml_dtypes
import numpy as np
from jax import lax
from jax.experimental import pallas as pl
from jax.experimental.pallas import tpu as pltpu
from jax.sharding import PartitionSpec as P

HEADS = 9
KV_HEADS = 3
HEAD_DIM = 64
D = 576
KVD = 192
FF = 1536
SEQ = 1024
NS_ITERS = 5


eps_norm = 1e-05
rope_base = 100000.0
momentum_decay = 0.95
matrix_rate = 0.1
weight_decay = 0.1
gain_rate = 0.25
coef_one = 3.4445
coef_two = -4.775
coef_three = 2.0315
precise = lax.Precision.HIGHEST
BF = jnp.bfloat16
F32 = jnp.float32
MESH = pl.DeviceIdType.MESH
VMEM_LIMIT = 63 * 2**20


def matrix_shapes():
    return ((D, D), (D, KVD), (D, KVD), (D, D), (D, FF), (D, FF), (FF, D))


UNITS = {
    "q": (640, 128, 5),
    "kv": (512, 128, 4),
    "o": (640, 128, 5),
    "g": (1536, 256, 6),
    "u": (1536, 256, 6),
}
GROUPS = (("q", "kv"), ("o",), ("g", "u"), ("d",))
ROWS_D = 48


def unit_width(name):
    return UNITS[name][0] + UNITS[name][1]


def group_shape(group):
    if group == ("d",):
        return (ROWS_D, 640)
    return (16, sum(unit_width(u) for u in group))


def unit_offset(name):
    for group in GROUPS:
        off = 0
        for u in group:
            if u == name:
                return off
            off += unit_width(u)
    raise KeyError(name)


def place_of(d):
    y, x, c = d // 4, (d // 2) % 2, d % 2
    return c * 4 + (y * 2 + x if c == 0 else x * 2 + y)


def spread_matrices():
    out = np.zeros((6, 144, 256), np.float32)
    for q in range(6):
        for d in range(8):
            p = place_of(d)
            for r in range(16):
                out[q, 18 * d + r, 16 * p + r] = 1
            for e in range(2):
                out[q, 18 * d + 16 + e, 128 + 16 * p + 8 * e + q] = 1
    return out


def gain_select():
    out = np.zeros((32, 512), np.float32)
    for i in range(32):
        z, d = i // 8, i % 8
        out[i, (place_of(d) * 4 + z) * 16 + 7] = 1
    return out


def gain_lanes():
    out = np.zeros((128, 2 * D), np.float32)
    for j in range(2 * D):
        out[j % 36, j] = 1
    return out


def coords():
    me = lax.axis_index("dp")
    z, y, x, c = me // 8, lax.rem(me // 4, 2), lax.rem(me // 2, 2), lax.rem(me, 2)
    a = y * (1 - c) + x * c
    b = x * (1 - c) + y * c

    def dev(zz, yy, xx, cc):
        return ((zz * 2 + yy) * 2 + xx) * 2 + cc

    peer_b = dev(z, y + (1 - 2 * y) * c, x + (1 - 2 * x) * (1 - c), c)
    peer_a = dev(z, y + (1 - 2 * y) * (1 - c), x + (1 - 2 * x) * c, c)
    sibling = dev(z, y, x, 1 - c)

    def along(step):
        return dev(lax.rem(z + step, 4), y, x, c)

    return me, (z, a, b, c), peer_a, peer_b, sibling, along


def remote(src, dst, send, recv, target):
    return pltpu.make_async_remote_copy(
        src_ref=src, dst_ref=dst, send_sem=send, recv_sem=recv, device_id=(target,), device_id_type=MESH
    )


def slot(c, a, b, z):
    return ((c * 2 + a) * 2 + b) * 4 + z


class Gather:
    def __init__(self, buf, send, recv, where):
        self.buf, self.send, self.recv = buf, send, recv
        self.me, (self.z, self.a, self.b, self.c), self.peer_a, self.peer_b, self.sibling, self.along = where
        self.count = 0

    def push(self, index, target):
        ref = self.buf.at[index]
        copy = remote(ref, ref, self.send.at[self.count], self.recv.at[slot(*index)], target)
        copy.start()
        self.count += 1

    def arrive(self, index):
        ref = self.buf.at[index]
        remote(ref, ref, self.send.at[0], self.recv.at[slot(*index)], self.sibling).wait_recv()

    def phase_own(self):
        own = (self.c, self.a, self.b, self.z)
        for step in (1, 3, 2):
            self.push(own, self.along(step))
        self.push(own, self.peer_b)
        self.push(own, self.peer_a)
        self.push(own, self.sibling)

    def phase_z(self):
        for step in (1, 3, 2):
            index = (self.c, self.a, self.b, lax.rem(self.z + step, 4))
            self.arrive(index)
            self.push(index, self.peer_b)
            self.push(index, self.peer_a)
            self.push(index, self.sibling)

    def phase_b(self):
        for step in (0, 1, 3, 2):
            index = (self.c, self.a, 1 - self.b, lax.rem(self.z + step, 4))
            self.arrive(index)
            self.push(index, self.peer_a)
            self.push(index, self.sibling)

    def phase_a(self):
        for bb in (self.b, 1 - self.b):
            for step in (0, 1, 3, 2):
                index = (self.c, 1 - self.a, bb, lax.rem(self.z + step, 4))
                self.arrive(index)
                self.push(index, self.sibling)

    def phase_sibling(self):
        for aa in range(2):
            for bb in range(2):
                for zz in range(4):
                    self.arrive((1 - self.c, aa, bb, zz))

    def finish(self):
        own = (self.c, self.a, self.b, self.z)
        ref = self.buf.at[own]
        for n in range(self.count):
            remote(ref, ref, self.send.at[n], self.recv.at[slot(*own)], self.sibling).wait_send()


def low_lanes(rows):
    return lax.broadcasted_iota(jnp.int32, (rows, 128), 1) < 64


def turn(v):
    return pltpu.roll(v, 64, axis=1)


def load_rows(flat, scr, rows, tiles2):
    if tiles2 % 2 == 0:
        nt = tiles2 // 2
        for t in range(nt):
            scr[t, 0:rows, :] = flat[pl.ds(t, rows, stride=nt), :]
        return
    half, h = rows // 2, (tiles2 - 1) // 2
    low = low_lanes(half)
    pair = [flat[pl.ds(t, half, stride=tiles2), :] for t in range(tiles2)]
    turned = {t: turn(pair[t]) for t in range(h, tiles2)}
    for j in range(h + 1):
        even = pair[j] if j < h else jnp.where(low, pair[h], 0.0)
        odd = jnp.where(low, turned[h + j], turned[h + j + 1] if j < h else 0.0)
        scr[j, pl.ds(0, half, stride=2), :] = even
        scr[j, pl.ds(1, half, stride=2), :] = odd


def store_rows(scr, flat, rows, tiles2, base=0):
    if tiles2 % 2 == 0:
        nt = tiles2 // 2
        for t in range(nt):
            flat[pl.ds(t, rows, stride=nt), :] = scr[base + t, 0:rows, :]
        return
    half, h = rows // 2, (tiles2 - 1) // 2
    low = low_lanes(half)
    even = [scr[base + j, pl.ds(0, half, stride=2), :] for j in range(h + 1)]
    odd = [turn(scr[base + j, pl.ds(1, half, stride=2), :]) for j in range(h + 1)]
    for t in range(tiles2):
        if t < h:
            value = even[t]
        elif t == h:
            value = jnp.where(low, even[h], odd[0])
        else:
            value = jnp.where(low, odd[t - h - 1], odd[t - h])
        flat[pl.ds(t, half, stride=tiles2), :] = value


PARTS = {
    "q": ((0, 0, 9, 18),),
    "kv": ((1, 0, 3, 18), (2, 2, 3, 18)),
    "o": ((3, 0, 9, 18),),
    "g": ((4, 0, 24, 18),),
    "u": ((5, 0, 24, 18),),
    "d": ((6, 0, 9, 48),),
}


def pack_slab(name, scr, fold_scr, slab, off, gains=None):
    if name == "d":
        for t in range(5):
            slab[:, off + 128 * t : off + 128 * (t + 1)] = scr[t, 0:48, :].astype(slab.dtype)
        return
    padded, fold, chunks = UNITS[name]
    for t in range(padded // 128):
        slab[:, off + 128 * t : off + 128 * (t + 1)] = scr[t, 0:16, :].astype(slab.dtype)
    fold_scr[...] = jnp.zeros_like(fold_scr)
    per = fold // 128
    for q in range(chunks):
        for k in range(per):
            for e in range(2):
                fold_scr[e * 8 + q : e * 8 + q + 1, 128 * k : 128 * (k + 1)] = scr[q * per + k, 16 + e : 17 + e, :]
    if gains is not None:
        fold_scr[7:8, 0:128] = gains
    slab[:, off + padded : off + padded + fold] = fold_scr[:, 0:fold].astype(slab.dtype)


def unpack_slab(name, main, scr, fold_scr):
    if name == "d":
        for t in range(5):
            scr[t, 0:48, :] = main[:, 128 * t : 128 * (t + 1)]
        return
    padded, fold, chunks = UNITS[name]
    for t in range(padded // 128):
        scr[t, 0:16, :] = main[:, 128 * t : 128 * (t + 1)]
    fold_scr[:, 0:fold] = main[:, padded : padded + fold]
    per = fold // 128
    for q in range(chunks):
        for k in range(per):
            for e in range(2):
                scr[q * per + k, 16 + e : 17 + e, :] = fold_scr[e * 8 + q : e * 8 + q + 1, 128 * k : 128 * (k + 1)]


def spread(name, buf, off, spread_ref, dest):
    padded, fold, chunks = UNITS[name]

    def plane(z, _):
        folded = buf[:, :, :, z, :, off + padded : off + padded + fold].reshape(128, fold)
        for q in range(chunks):
            main = buf[:, :, :, z, :, off + q * fold : off + (q + 1) * fold].reshape(128, fold)
            both = jnp.concatenate([main, folded], axis=0)
            block = jnp.dot(spread_ref[q], both, preferred_element_type=F32)
            dest[pl.ds(pl.multiple_of(z * 144, 16), 144), q * fold : (q + 1) * fold] = block.astype(dest.dtype)
        return 0

    lax.fori_loop(0, 4, plane, 0)


def spread_down(buf, dest):
    for z in range(4):
        for d in range(8):
            y, x, c = d // 4, (d // 2) % 2, d % 2
            a, b = (y, x) if c == 0 else (x, y)
            dest[(z * 8 + d) * 48 : (z * 8 + d + 1) * 48, :] = buf[c, a, b, z].astype(dest.dtype)


def reader(source):
    return lambda first, q, fold: source[pl.ds(first, 144), q * fold : (q + 1) * fold].astype(BF)


def collect(name, read, buf, off, collect_ref, extra=None):
    padded, fold, chunks = UNITS[name]

    def plane(z, _):
        first = pl.multiple_of(z * 144, 16)
        total = jnp.zeros((128, fold), F32)
        for q in range(chunks):
            both = jnp.dot(collect_ref[q], read(first, q, fold), preferred_element_type=F32)
            buf[:, :, :, z, :, off + q * fold : off + (q + 1) * fold] = (
                both[0:128].astype(BF).reshape(2, 2, 2, 16, fold)
            )
            total = total + both[128:256]
        if extra is not None:
            total = total + extra(z)
        buf[:, :, :, z, :, off + padded : off + padded + fold] = total.astype(BF).reshape(2, 2, 2, 16, fold)
        return 0

    lax.fori_loop(0, 4, plane, 0)


def collect_down(source, buf):
    for z in range(4):
        for d in range(8):
            y, x, c = d // 4, (d // 2) % 2, d % 2
            a, b = (y, x) if c == 0 else (x, y)
            buf[c, a, b, z] = source[(z * 8 + d) * 48 : (z * 8 + d + 1) * 48, :].astype(BF)


def spread_own_down(buf, dest):
    for z in range(4):
        for d in range(8):
            y, x, c = d // 4, (d // 2) % 2, d % 2
            a, b = (y, x) if c == 0 else (x, y)
            for k in range(3):
                first = (z * 8 + d) * 48 + 16 * k
                dest[first : first + 16, :] = buf[c, a, b, z, :, 640 * k : 640 * (k + 1)]


def collect_own_down(source, buf):
    for z in range(4):
        for d in range(8):
            y, x, c = d // 4, (d // 2) % 2, d % 2
            a, b = (y, x) if c == 0 else (x, y)
            for k in range(3):
                first = (z * 8 + d) * 48 + 16 * k
                buf[c, a, b, z, :, 640 * k : 640 * (k + 1)] = source[first : first + 16, :]


def load_unit(name, flats, scr):
    for index, tile, tiles2, rows in PARTS[name]:
        view = scr if tile == 0 else scr.at[pl.ds(tile, (tiles2 + 1) // 2)]
        load_rows(flats[index], view, rows, tiles2)


def read_gains(buf, select_ref, lanes_ref, gains_out):
    rows = gain_rows(buf[:, :, :, :, :, 640:768].reshape(512, 128), select_ref)
    wide = jnp.dot(rows.astype(BF), lanes_ref[...], preferred_element_type=F32)
    device = lax.broadcasted_iota(jnp.int32, wide.shape, 0)
    column = lax.broadcasted_iota(jnp.int32, wide.shape, 1)
    low = device * 36
    keep = jnp.logical_and(column >= low, column < low + 36)
    gains_out[...] = jnp.sum(jnp.where(keep, wide, 0.0), axis=0, keepdims=True)


def gain_rows(folds, select_ref):
    return jnp.dot(select_ref[...], folds, preferred_element_type=F32)


def vmem():
    return pl.BlockSpec(memory_space=pltpu.VMEM)


def slab_buffers():
    return [pltpu.VMEM((2, 2, 2, 4) + group_shape(group), BF) for group in GROUPS]


NN = (((1,), (0,)), ((), ()))
NT = (((1,), (1,)), ((), ()))
TN = (((0,), (0,)), ((), ()))
TILES = 5
BLOCK = 256
LOG2E = 1.4426950408889634


def mm(left, right, dims=NN):
    return lax.dot_general(left, right, dims, preferred_element_type=F32)


def block_rows(i, size=BLOCK):
    return pl.ds(pl.multiple_of(i * size, size), size)


def frequencies():
    half = HEAD_DIM // 2
    freqs = rope_base ** (-np.arange(half) * 2.0 / HEAD_DIM)
    return np.tile(freqs.astype(np.float32), 4).reshape(1, 128)


def lane(shape):
    return lax.broadcasted_iota(jnp.int32, shape, len(shape) - 1)


def cos_sin(angle):
    turns = jnp.floor(angle * 0.6366197723675814 + 0.5)
    rest = ((angle - turns * 1.5703125) - turns * 4.837512969970703e-4) - turns * 7.549789948768648e-8
    square = rest * rest
    sine = rest + rest * square * (
        -1.6666654611e-1 + square * (8.3321608736e-3 + square * -1.9515295891e-4)
    )
    cosine = (1.0 - 0.5 * square) + square * square * (
        4.166664568298827e-2 + square * (-1.388731625493765e-3 + square * 2.443315711809948e-5)
    )
    quarter = turns - 4.0 * jnp.floor(turns * 0.25)
    odd = jnp.logical_or(quarter == 1.0, quarter == 3.0)
    swapped_cos = jnp.where(odd, sine, cosine)
    swapped_sin = jnp.where(odd, cosine, sine)
    cos_sign = jnp.logical_or(quarter == 1.0, quarter == 2.0)
    return (
        jnp.where(cos_sign, -swapped_cos, swapped_cos),
        jnp.where(quarter >= 2.0, -swapped_sin, swapped_sin),
    )


def make_tables(positions, freqs, cos_ref, sin_ref):
    for r in range(SEQ // 128):
        row = jnp.broadcast_to(positions[r : r + 1, :].astype(F32), (128, 128))
        column = jnp.sum(jnp.where(diagonal(128), row, 0.0), axis=1, keepdims=True)
        cosine, sine = cos_sin(column * freqs[...])
        cos_ref[128 * r : 128 * (r + 1), :] = cosine
        sin_ref[128 * r : 128 * (r + 1), :] = jnp.where(lax.rem(lane((128, 128)), 64) < 32, -sine, sine)


def rotate_tile(value, cosine, sine, inverse=False):
    first = lax.rem(lane(value.shape), 64) < 32
    swapped = jnp.where(first, pltpu.roll(value, 96, axis=1), pltpu.roll(value, 32, axis=1))
    if inverse:
        return value * cosine - swapped * sine
    return value * cosine + swapped * sine


def row_scale(value):
    return lax.rsqrt(jnp.sum(value * value, axis=1, keepdims=True) * (1.0 / D) + eps_norm)


def turn_over(source, dest):
    def body(i, _):
        rows = block_rows(i)
        dest[rows, :] = source[:, rows].T
        return 0

    lax.fori_loop(0, SEQ // BLOCK, body, 0)


def normalize_tokens(tokens, gain, a_ref):
    def body(i, _):
        rows = block_rows(i)
        x = tokens[rows, :].astype(F32)
        a_ref[rows, :] = (x * row_scale(x) * gain).astype(BF)
        return 0

    lax.fori_loop(0, SEQ // BLOCK, body, 0)


def heads_in(a_ref, w_q, w_kv, cos_ref, sin_ref, q_ref, k_ref, v_ref):
    def body(i, _):
        rows = block_rows(i)
        a = a_ref[rows, :]
        cosine, sine = cos_ref[rows, :], sin_ref[rows, :]
        pq = mm(a, w_q[...])
        for t in range(TILES):
            turned = rotate_tile(pq[:, 128 * t : 128 * (t + 1)], cosine, sine).astype(BF)
            q_ref[t, rows, :] = turned * jnp.asarray(HEAD_DIM ** (-0.5), BF)
        pkv = mm(a, w_kv[...])
        low = lane((BLOCK, 128)) < 64
        for ref, base, rotary in ((k_ref, 0, True), (v_ref, 256, False)):
            for half in range(2):
                tile = pkv[:, base + 128 * half : base + 128 * (half + 1)]
                if rotary:
                    tile = rotate_tile(tile, cosine, sine)
                other = turn(tile)
                ref[2 * half, rows, :] = jnp.where(low, tile, other).astype(BF)
                if half == 0:
                    ref[1, rows, :] = jnp.where(low, other, tile).astype(BF)
        return 0

    lax.fori_loop(0, SEQ // BLOCK, body, 0)


def own_lanes(value, parity):
    here = lane(value.shape) // 64 == parity
    return jnp.where(here, value, jnp.zeros_like(value))


def attend_group(g, q_ref, k_ref, v_ref, o_ref, lse_ref):
    for h in range(HEADS // KV_HEADS):
        j = 3 * g + h
        t, parity = j // 2, lax.rem(j, 2)
        for i in range(SEQ // BLOCK):
            end = BLOCK * (i + 1)
            query = q_ref[t, BLOCK * i : end, :]
            s = mm(own_lanes(k_ref[g, 0:end, :], parity), query, NT)
            rows = lax.broadcasted_iota(jnp.int32, (BLOCK, BLOCK), 0)
            cols = lax.broadcasted_iota(jnp.int32, (BLOCK, BLOCK), 1)
            corner = jnp.where(cols >= rows, s[BLOCK * i :, :], -1e30)
            s = jnp.concatenate([s[: BLOCK * i, :], corner], axis=0) if i else corner
            top = jnp.max(s, axis=0, keepdims=True)
            weights = jnp.exp2((s - top) * LOG2E)
            total = jnp.sum(weights, axis=0, keepdims=True)
            probs = (weights * (1.0 / total)).astype(BF)
            out = mm(probs, own_lanes(v_ref[g, 0:end, :], parity), TN)
            o_ref[t, BLOCK * i : end, :] += out.astype(BF)
            lse_ref[j, :, BLOCK * i : end] = top * LOG2E + jnp.log2(total)


def attend_all(q_ref, k_ref, v_ref, o_ref, lse_ref, between=()):
    o_ref[...] = jnp.zeros_like(o_ref)

    def body(g, _):
        attend_group(g, q_ref, k_ref, v_ref, o_ref, lse_ref)
        for number, action in enumerate(between):
            pl.when(g == number)(action)
        return 0

    lax.fori_loop(0, KV_HEADS, body, 0)


DK_BASE = TILES * SEQ
DV_BASE = DK_BASE + 2 * KV_HEADS * SEQ
WIDE_ROWS = DV_BASE + 2 * KV_HEADS * SEQ
GATE_BASE = 0
UP_BASE = 12 * D


def read_z(z_buf, first, count):
    blocks = []
    for i in range(SEQ // BLOCK):
        half, column = i // 2, (i % 2) * FF + first
        blocks.append(z_buf[half, :, :, :, :, column : column + count].reshape(BLOCK, count))
    return jnp.concatenate(blocks, axis=0)


STAGE_BASE = UP_BASE + 12 * D


class Drain:
    def __init__(self, wide, sems, result):
        self.wide, self.sems, self.result = wide, sems, result

    def rows(self, number, half):
        return pl.ds(pl.multiple_of(STAGE_BASE + (2 * number + half) * D, 8), D)

    def copy(self, i, number, half):
        columns = pl.ds(pl.multiple_of(i * BLOCK + 128 * half, 128), 128)
        return pltpu.make_async_copy(
            self.wide.at[self.rows(number, half)], self.result.at[:, columns], self.sems.at[number, half]
        )

    def put(self, i, value):
        number = lax.rem(i, 2)

        @pl.when(i >= 2)
        def _():
            for half in range(2):
                self.copy(i, number, half).wait()

        for half in range(2):
            self.wide[self.rows(number, half), :] = value[:, 128 * half : 128 * (half + 1)]
            self.copy(i, number, half).start()

    def finish(self):
        for number in range(2):
            for half in range(2):
                self.copy(number, number, half).wait()


def feed_forward(R, gain, drain):
    w_o, w_g, w_u, w_d = R.nat_o, R.nat_g, R.nat_u, R.nat_d
    R.gain_two[...] = jnp.zeros_like(R.gain_two)

    def body(i, _):
        rows = block_rows(i)
        o = jnp.concatenate([R.o[t, rows, :] for t in range(TILES)], axis=1)
        x2 = R.tok[rows, :].astype(F32) + mm(o[:, 0:D], w_o[:, 0:D])
        r2 = row_scale(x2)
        n2 = x2 * r2
        h = (n2 * gain).astype(BF)
        c = R.cot[rows, :]
        gate = mm(h, w_g[...])
        upper = mm(h, w_u[...])
        grad = mm(c, w_d[:, 0:D], NT)
        sigma = 0.5 * jnp.tanh(0.5 * gate) + 0.5
        silu = gate * sigma
        z = (silu * upper).astype(BF)
        column = pl.ds(pl.multiple_of(lax.rem(i, 2) * FF, 128), FF)
        R.z_buf[i // 2, :, :, :, :, column] = z.reshape(2, 2, 4, 16, FF)
        dg = (grad * upper * (sigma + silu * (1.0 - sigma))).astype(BF)
        du = (grad * silu).astype(BF)
        drain.put(i, (x2 + mm(z, w_d[:, 0:D])).T)
        dh = mm(dg, w_g[...], NT) + mm(du, w_u[...], NT)
        for base, value in ((GATE_BASE, dg), (UP_BASE, du)):
            for k in range(3):
                part = mm(h, value[:, 512 * k : 512 * (k + 1)], TN)
                for t in range(4):
                    here = slice(base + (4 * k + t) * D, base + (4 * k + t + 1) * D)
                    R.wide[here, :] += part[:, 128 * t : 128 * (t + 1)]
        R.gain_two[...] += jnp.sum(dh * n2, axis=0, keepdims=True)
        scaled = dh * gain
        mean = jnp.sum(scaled * n2, axis=1, keepdims=True) * (1.0 / D)
        dx = c.astype(F32) + r2 * (scaled - n2 * mean)
        R.dx[rows, :] = dx
        do = mm(dx.astype(BF), w_o[:, 0:D], NT)
        pick = (lax.broadcasted_iota(jnp.int32, (8, 128), 0) == lane((8, 128)) // 64).astype(BF)
        for t in range(TILES):
            if t < TILES - 1:
                tile = do[:, 128 * t : 128 * (t + 1)]
            else:
                tile = jnp.concatenate([do[:, 512:576], jnp.zeros((BLOCK, 64), F32)], axis=1)
            tile = tile.astype(BF)
            R.do[t, rows, :] = tile
            product = tile.astype(F32) * o[:, 128 * t : 128 * (t + 1)].astype(F32)
            high = product.astype(BF)
            low = (product - high.astype(F32)).astype(BF)
            inner = mm(pick, high, NT) + mm(pick, low, NT)
            R.inner[2 * t, :, rows] = inner[0:1]
            if t < TILES - 1:
                R.inner[2 * t + 1, :, rows] = inner[1:2]
        return 0

    lax.fori_loop(0, SEQ // BLOCK, body, 0)
    drain.finish()


def down_gradient(R, dest):
    for k in range(3):
        dest[512 * k : 512 * (k + 1), 0:D] = mm(read_z(R.z_buf, 512 * k, 512), R.cot[...], TN).astype(BF)
    dest[:, D:] = jnp.zeros((FF, 640 - D), BF)


def out_gradient(R, dest):
    for t in range(TILES):
        part = mm(R.o[t], R.dx[...].astype(BF), TN).astype(BF)
        rows = min(128, D - 128 * t)
        dest[128 * t : 128 * t + rows, 0:D] = part[0:rows]
    dest[:, D:] = jnp.zeros((D, 640 - D), BF)


def attend_back_group(g, R):
    for h in range(HEADS // KV_HEADS):
        j = 3 * g + h
        t, parity = j // 2, lax.rem(j, 2)
        for i in range(SEQ // BLOCK):
            start = BLOCK * i
            rows = slice(start, start + BLOCK)
            key = own_lanes(R.k[g, rows, :], parity)
            value = own_lanes(R.v[g, rows, :], parity)
            query, grad = R.q[t, start:, :], R.do[t, start:, :]
            probs = jnp.exp2(mm(key, query, NT) * LOG2E - R.lse[j, :, start:])
            down = lax.broadcasted_iota(jnp.int32, (BLOCK, BLOCK), 0)
            across = lax.broadcasted_iota(jnp.int32, (BLOCK, BLOCK), 1)
            corner = jnp.where(across >= down, probs[:, :BLOCK], 0.0)
            probs = jnp.concatenate([corner, probs[:, BLOCK:]], axis=1) if start + BLOCK < SEQ else corner
            ds = (probs * (mm(value, grad, NT) - R.inner[j, :, start:])).astype(BF)
            place = (2 * g + parity) * SEQ + start
            R.wide[pl.ds(pl.multiple_of(DV_BASE + place, BLOCK), BLOCK), :] += mm(probs.astype(BF), grad)
            R.wide[pl.ds(pl.multiple_of(DK_BASE + place, BLOCK), BLOCK), :] += mm(ds, query)
            R.wide[pl.ds(pl.multiple_of(t * SEQ + start, BLOCK), SEQ - start), :] += mm(ds, key, TN)


def attend_back_all(R, between=()):
    R.wide[...] = jnp.zeros_like(R.wide)

    def body(g, _):
        attend_back_group(g, R)
        for number, action in enumerate(between):
            pl.when(g == number)(action)
        return 0

    lax.fori_loop(0, KV_HEADS, body, 0)


def heads_out(R):
    def body(i, _):
        rows = block_rows(i)
        cosine, sine = R.cos[rows, :], R.sin[rows, :]
        for t in range(TILES):
            tile = R.wide[pl.ds(pl.multiple_of(t * SEQ + i * BLOCK, BLOCK), BLOCK), :] * HEAD_DIM ** (-0.5)
            R.o[t, rows, :] = rotate_tile(tile, cosine, sine, True).astype(BF)
        low = lane((BLOCK, 128)) < 64
        for base, column, rotary in ((DK_BASE, 0, True), (DV_BASE, 256, False)):
            whole = []
            for g in range(KV_HEADS):
                parts = [
                    R.wide[pl.ds(pl.multiple_of(base + (2 * g + p) * SEQ + i * BLOCK, BLOCK), BLOCK), :]
                    for p in range(2)
                ]
                whole.append(parts[0] + turn(parts[1]))
            tiles = (jnp.where(low, whole[0], turn(whole[1])), jnp.where(low, whole[2], 0.0))
            for half in range(2):
                tile = rotate_tile(tiles[half], cosine, sine, True) if rotary else tiles[half]
                R.cot[rows, column + 128 * half : column + 128 * (half + 1)] = tile.astype(BF)
        return 0

    lax.fori_loop(0, SEQ // BLOCK, body, 0)


def first_gradients(R, dest_q, dest_kv):
    a = R.a[...]
    for t in range(TILES):
        dest_q[:, 128 * t : 128 * (t + 1)] = mm(a, R.o[t], TN).astype(BF)
    dest_kv[:, 0:512] = mm(a, R.cot[:, 0:512], TN).astype(BF)


def key_gain(R):
    R.gain_one[...] = jnp.zeros_like(R.gain_one)

    def body(i, _):
        rows = block_rows(i)
        dq = jnp.concatenate([R.o[t, rows, :] for t in range(TILES)], axis=1)
        da = mm(dq, R.nat_q[...], NT) + mm(R.cot[rows, 0:512], R.nat_kv[...], NT)
        x = R.tok[rows, :].astype(F32)
        R.gain_one[...] += jnp.sum(da * (x * row_scale(x)), axis=0, keepdims=True)
        R.wide[pl.ds(pl.multiple_of(i * BLOCK, BLOCK), BLOCK), :] = da[:, 0:128]
        for t in range(1, TILES):
            width = min(128, D - 128 * t)
            R.wide[pl.ds(pl.multiple_of(t * SEQ + i * BLOCK, BLOCK), BLOCK), 0:width] = da[:, 128 * t : 128 * t + width]
        return 0

    lax.fori_loop(0, SEQ // BLOCK, body, 0)


def input_gradient(R, gain, drain):
    def body(i, _):
        rows = block_rows(i)
        tiles = [R.wide[pl.ds(pl.multiple_of(t * SEQ + i * BLOCK, BLOCK), BLOCK), :] for t in range(TILES)]
        da = jnp.concatenate(tiles, axis=1)[:, 0:D]
        x = R.tok[rows, :].astype(F32)
        r1 = row_scale(x)
        n1 = x * r1
        scaled = da * gain
        mean = jnp.sum(scaled * n1, axis=1, keepdims=True) * (1.0 / D)
        drain.put(i, (R.dx[rows, :] + r1 * (scaled - n1 * mean)).T)
        return 0

    lax.fori_loop(0, SEQ // BLOCK, body, 0)
    drain.finish()


LAYER_SCRATCH = {
    "nat_q": ((D, 640), BF),
    "nat_kv": ((D, 512), BF),
    "nat_o": ((D, 640), BF),
    "nat_g": ((D, FF), BF),
    "nat_u": ((D, FF), BF),
    "nat_d": ((FF, 640), BF),
    "gains": ((1, 2 * D), F32),
    "tok": ((SEQ, D), BF),
    "cot": ((SEQ, D), BF),
    "a": ((SEQ, D), BF),
    "cos": ((SEQ, 128), F32),
    "sin": ((SEQ, 128), F32),
    "q": ((TILES, SEQ, 128), BF),
    "k": ((KV_HEADS, SEQ, 128), BF),
    "v": ((KV_HEADS, SEQ, 128), BF),
    "lse": ((HEADS, 1, SEQ), F32),
    "inner": ((HEADS, 1, SEQ), F32),
    "o": ((TILES, SEQ, 128), BF),
    "do": ((TILES, SEQ, 128), BF),
    "dx": ((SEQ, D), F32),
    "wide": ((WIDE_ROWS, 128), F32),
    "gain_one": ((1, D), F32),
    "gain_two": ((1, D), F32),
}


def layer_scratch():
    return [pltpu.VMEM(*s) for s in LAYER_SCRATCH.values()] + [
        pltpu.SemaphoreType.DMA((2,)),
        pltpu.SemaphoreType.DMA((2, 2)),
    ]


def layer_refs(refs, z_buf):
    names = list(LAYER_SCRATCH) + ["in_sems", "out_sems"]
    return types.SimpleNamespace(z_buf=z_buf, **dict(zip(names, refs)))


def nothing():
    return None


def run_layer(R, tok_t, positions, cot_t, freqs, out_t, grad_t, steps):
    copies = [
        pltpu.make_async_copy(tok_t, R.nat_g.at[:, 0:SEQ], R.in_sems.at[0]),
        pltpu.make_async_copy(cot_t, R.nat_u.at[:, 0:SEQ], R.in_sems.at[1]),
    ]
    for copy in copies:
        copy.start()
    steps.begin()
    make_tables(positions, freqs, R.cos, R.sin)
    copies[0].wait()
    turn_over(R.nat_g, R.tok)
    copies[1].wait()
    turn_over(R.nat_u, R.cot)
    R.wide[...] = jnp.zeros_like(R.wide)
    steps.first_weights()
    normalize_tokens(R.tok, R.gains[:, 0:D], R.a)
    heads_in(R.a, R.nat_q, R.nat_kv, R.cos, R.sin, R.q, R.k, R.v)
    attend_all(R.q, R.k, R.v, R.o, R.lse, steps.forward)
    steps.second_weights()
    feed_forward(R, R.gains[:, D : 2 * D], Drain(R.wide, R.out_sems, out_t))
    steps.after_feed_forward()
    attend_back_all(R, steps.backward)
    heads_out(R)
    steps.after_attention()
    input_gradient(R, R.gains[:, 0:D], Drain(R.wide, R.out_sems, grad_t))
    steps.end()


def local_kernel(tok_t, positions, cot_t, freqs, gains, w_q, w_kv, w_o, w_g, w_u, w_d, *refs):
    out_t, grad_t, g_q, g_kv, g_o, g_g, g_u, g_d, gain_one, gain_two = refs[:10]
    R = layer_refs(refs[11:], refs[10])

    def first_weights():
        R.nat_q[...] = w_q[...]
        R.nat_kv[...] = w_kv[...]
        R.gains[...] = gains[...]

    def second_weights():
        R.nat_o[...] = w_o[...]
        R.nat_g[...] = w_g[...]
        R.nat_u[...] = w_u[...]
        R.nat_d[...] = w_d[...]

    def after_feed_forward():
        down_gradient(R, g_d)
        out_gradient(R, g_o)
        for dest, base in ((g_g, GATE_BASE), (g_u, UP_BASE)):
            for t in range(12):
                dest[:, 128 * t : 128 * (t + 1)] = R.wide[base + t * D : base + (t + 1) * D, :].astype(BF)

    def after_attention():
        first_gradients(R, g_q, g_kv)
        key_gain(R)
        gain_one[...] = R.gain_one[...]
        gain_two[...] = R.gain_two[...]

    steps = types.SimpleNamespace(
        begin=nothing,
        first_weights=first_weights,
        forward=(),
        second_weights=second_weights,
        after_feed_forward=after_feed_forward,
        backward=(),
        after_attention=after_attention,
        end=nothing,
    )
    run_layer(R, tok_t, positions, cot_t, freqs, out_t, grad_t, steps)


def hbm():
    return pl.BlockSpec(memory_space=pl.ANY)


def layer_inputs(tokens, positions, cotangent):
    return tokens.T, positions.reshape(-1, 128), cotangent.T, jnp.asarray(frequencies())


def layer(tokens, positions, cotangent, gains, *natural):
    shape = jax.ShapeDtypeStruct
    args = (*layer_inputs(tokens, positions, cotangent), gains, *natural)
    grads = [shape(v.shape, BF) for v in natural]
    outs = pl.pallas_call(
        local_kernel,
        out_shape=(shape((D, SEQ), F32), shape((D, SEQ), F32), *grads, shape((1, D), F32), shape((1, D), F32)),
        in_specs=[hbm(), vmem(), hbm(), vmem()] + [vmem()] * 7,
        out_specs=(hbm(), hbm()) + (vmem(),) * 8,
        scratch_shapes=[pltpu.VMEM((2, 2, 2, 4) + group_shape(("g", "u")), BF)] + layer_scratch(),
        compiler_params=pltpu.CompilerParams(vmem_limit_bytes=VMEM_LIMIT),
        name="layer",
    )(*args)
    return outs[0].T, outs[1].T, outs[2:8], outs[8], outs[9]


def local_call(kernel, name, args, outs, scratch):
    return pl.pallas_call(
        kernel,
        out_shape=tuple(jax.ShapeDtypeStruct(*o) for o in outs),
        in_specs=[vmem()] * len(args),
        out_specs=(vmem(),) * len(outs),
        scratch_shapes=[pltpu.VMEM(*s) for s in scratch],
        compiler_params=pltpu.CompilerParams(vmem_limit_bytes=VMEM_LIMIT),
        name=name,
    )(*args)


OWNERS = {"q": 16, "kv": 18, "o": 12, "g": 8, "u": 22, "d": 14}
UNIT_NAMES = ("q", "kv", "o", "g", "u", "d")


class Reduce:
    def __init__(self, buf, r1, r2, r3, r4, send, recv, where):
        self.buf, self.r1, self.r2, self.r3, self.r4 = buf, r1, r2, r3, r4
        self.send, self.recv = send, recv
        self.me, (self.z, self.a, self.b, self.c), self.peer_a, self.peer_b, self.sibling, self.along = where

    def copy(self, k):
        if k < 2:
            half = 1 - self.b if k == 0 else self.b
            src, dst, target = self.buf.at[1 - self.c, half], self.r1.at[half], self.sibling
        elif k == 2:
            src, dst, target = self.buf.at[self.c, 1 - self.a], self.r2, self.peer_a
        elif k == 3:
            src, dst, target = self.buf.at[self.c, self.a, 1 - self.b], self.r3, self.peer_b
        else:
            step = k - 3
            src = self.buf.at[self.c, self.a, self.b, lax.rem(self.z + step, 4)]
            dst, target = self.r4.at[step - 1], self.along(step)
        return remote(src, dst, self.send.at[k], self.recv.at[k], target)

    def stage_one(self):
        self.copy(0).start()
        self.copy(1).start()

    def add(self, buf, index, got, count):
        def body(i, _):
            bb, zz = i // 4, lax.rem(i, 4)
            here = index + ((bb, zz) if len(index) == 2 else (zz,))
            there = got[1] + ((bb, zz) if len(index) == 2 else (zz,))
            buf[here] = (buf[here].astype(F32) + got[0][there].astype(F32)).astype(BF)
            return 0

        lax.fori_loop(0, count, body, 0)

    def stage_two(self):
        self.copy(0).wait_recv()
        self.add(self.buf, (self.c, 1 - self.a), (self.r1, (1 - self.a,)), 8)
        self.copy(2).start()
        self.copy(1).wait_recv()
        self.add(self.buf, (self.c, self.a), (self.r1, (self.a,)), 8)

    def stage_three(self):
        self.copy(2).wait_recv()
        self.add(self.buf, (self.c, self.a, 1 - self.b), (self.r2, (1 - self.b,)), 4)
        self.copy(3).start()
        self.add(self.buf, (self.c, self.a, self.b), (self.r2, (self.b,)), 4)

    def stage_four(self):
        self.copy(3).wait_recv()
        self.add(self.buf, (self.c, self.a, self.b), (self.r3, ()), 4)
        for step in (1, 3, 2):
            self.copy(3 + step).start()

    def result(self, total):
        for step in (1, 3, 2):
            self.copy(3 + step).wait_recv()
        own = self.buf[self.c, self.a, self.b, self.z].astype(F32)
        total[...] = (
            own + self.r4[0].astype(F32) + self.r4[1].astype(F32) + self.r4[2].astype(F32)
        )

    def finish(self):
        for k in range(7):
            self.copy(k).wait_send()


def diagonal(n):
    return lax.broadcasted_iota(jnp.int32, (n, n), 0) == lax.broadcasted_iota(jnp.int32, (n, n), 1)


OWN_WIDTH = 1920


def slab_width(name):
    return 640 if name == "d" else unit_width(name)


def own_width(name):
    return OWN_WIDTH if name == "d" else unit_width(name)


def own_slab_value(name, ref):
    value = ref[...]
    if name == "d":
        return jnp.concatenate([value[:, 640 * k : 640 * (k + 1)] for k in range(3)], axis=0)
    return value


def sum_squares(value):
    return jnp.sum(jnp.sum(value * value, axis=1, keepdims=True), axis=0, keepdims=True)


def on_diagonal(first, rows, n, value):
    row = lax.broadcasted_iota(jnp.int32, (rows, n), 0) + first
    return jnp.where(row == lane((rows, n)), value, 0.0)


def newton_schulz(wide, low, columns, e_ref, r_ref):
    first, last = columns
    rows = low.shape[0]
    tiles = (last - first + 127) // 128
    tall = rows > last - first
    n = last - first if tall else rows

    def here(t):
        return pl.ds(t * rows, rows)

    total = jnp.zeros((1, 1), F32)
    for t in range(tiles):
        value = low[:, first + 128 * t : first + 128 * (t + 1)].astype(F32)
        wide[here(t), :] = value
        total = total + sum_squares(value)
    scale = 1.0 / (jnp.sqrt(total) + 1e-07)
    for t in range(tiles):
        wide[here(t), :] = wide[here(t), :] * scale

    def step(_, squares):
        for t in range(tiles):
            low[:, first + 128 * t : first + 128 * (t + 1)] = wide[here(t), :].astype(BF)
        state = low[:, first:last]
        mean = squares * (1.0 / n)
        panel = 256 if tall else 288
        total = jnp.zeros((1, 1), F32)
        for top in range(0, n, panel):
            p = min(panel, n - top)
            gram = mm(state[:, top : top + p], state, TN) if tall else mm(state[top : top + p], state, NT)
            rest = gram - on_diagonal(top, p, n, mean)
            e_ref[top : top + p, 0:n] = rest.astype(BF)
            total = total + sum_squares(rest)
        more = total * (coef_three / n)
        slope = coef_two + 2.0 * coef_three * mean
        whole = e_ref[0:n, 0:n]
        for top in range(0, n, panel):
            p = min(panel, n - top)
            rest = e_ref[top : top + p, 0:n]
            poly = slope * rest.astype(F32) + coef_three * mm(rest, whole) - on_diagonal(top, p, n, more)
            r_ref[top : top + p, 0:n] = poly.astype(BF)
        keep = coef_one + coef_two * mean + coef_three * mean * mean + more
        poly = r_ref[0:n, 0:n]
        total = jnp.zeros((1, 1), F32)
        width = last - first
        for left in range(0, width, 256):
            w = min(256, width - left)
            if tall:
                change = mm(state, poly[:, left : left + w])
            else:
                change = mm(poly, state[:, left : left + w])
            for k in range((w + 127) // 128):
                t = left // 128 + k
                part = change[:, 128 * k : min(128 * (k + 1), w)]
                if part.shape[1] < 128:
                    part = jnp.concatenate([part, jnp.zeros((rows, 128 - part.shape[1]), F32)], axis=1)
                value = keep * wide[here(t), :] + part
                wide[here(t), :] = value
                total = total + sum_squares(value)
        return total

    lax.fori_loop(0, NS_ITERS, step, total * scale * scale)
    for t in range(tiles):
        low[:, first + 128 * t : first + 128 * (t + 1)] = wide[here(t), :].astype(BF)


def whole_kernel(*refs):
    tok_t, positions, cot_t, freqs = refs[0:4]
    w, gains_ref = refs[4:11], refs[11]
    m, m_gains = refs[12:19], refs[19]
    spread_ref, collect_ref, select_ref, lanes_ref, lanes_back, gain_put = refs[20:26]
    out_t, grad_t = refs[26:28]
    totals = refs[28:32]
    directions = dict(zip(UNIT_NAMES, refs[32:38]))
    k = 38
    bufs = refs[k : k + 4]
    r1, r2, r3, r4 = (refs[k + 4 + 4 * j : k + 8 + 4 * j] for j in range(4))
    k += 20
    scr, fold_scr, lane_scr = refs[k : k + 3]
    k += 3
    old = dict(zip(UNIT_NAMES, refs[k : k + 6]))
    mslab = dict(zip(UNIT_NAMES, refs[k + 6 : k + 12]))
    oslab = dict(zip(UNIT_NAMES, refs[k + 12 : k + 18]))
    k += 18
    held = refs[k]
    R = layer_refs(refs[k + 1 : k + 3 + len(LAYER_SCRATCH)], bufs[2])
    k += 3 + len(LAYER_SCRATCH)
    ag_send, ag_recv, rs_send, rs_recv, up_send, up_recv, down_send, down_recv = refs[k : k + 8]

    where = coords()
    me, (z, a, b, c), peer_a, peer_b, sibling, along = where
    own = (c, a, b, z)
    natural = {"q": R.nat_q, "kv": R.nat_kv, "o": R.nat_o, "g": R.nat_g, "u": R.nat_u}
    gathers = [Gather(buf, ag_send.at[n], ag_recv.at[n], where) for n, buf in enumerate(bufs)]
    late = gathers[1:]
    sums = [Reduce(bufs[g], r1[g], r2[g], r3[g], r4[g], rs_send.at[g], rs_recv.at[g], where) for g in range(4)]
    QKV, OUT, WIDE, DOWN = range(4)

    def pack_group(n):
        for name in GROUPS[n]:
            load_unit(name, w, scr)
            own_gains = None
            if name == "q":
                fold_scr[0:1, 0:128] = jnp.zeros((1, 128), F32)
                fold_scr[0:1, 0:36] = gains_ref[...]
                own_gains = fold_scr[0:1, 0:128]
            pack_slab(name, scr, fold_scr, bufs[n].at[own], unit_offset(name), own_gains)

    def begin():
        barrier = pltpu.get_barrier_semaphore()

        def hello(j, _):
            @pl.when(j != me)
            def _():
                pl.semaphore_signal(barrier, inc=1, device_id=(j,), device_id_type=MESH)

            return 0

        lax.fori_loop(0, 32, hello, 0)
        pack_group(QKV)
        pl.semaphore_wait(barrier, 31)
        gathers[QKV].phase_own()
        for n in (OUT, WIDE, DOWN):
            pack_group(n)
        lane_scr[0:1, :] = jnp.zeros((1, 128), F32)
        lane_scr[0:1, 0:36] = m_gains[...]
        for name in UNIT_NAMES:
            load_unit(name, m, scr)
            pack_slab(name, scr, fold_scr, old[name], 0, lane_scr[0:1, :] if name == "q" else None)

    def first_weights():
        gathers[QKV].phase_z()
        gathers[QKV].phase_b()
        gathers[QKV].phase_a()
        for move in late:
            move.phase_own()
        gathers[QKV].phase_sibling()
        for name in GROUPS[QKV]:
            spread(name, bufs[QKV], unit_offset(name), spread_ref, natural[name])
        read_gains(bufs[QKV], select_ref, lanes_ref, R.gains)

    def phase_z():
        for move in late:
            move.phase_z()

    def phase_b():
        for move in late:
            move.phase_b()

    def phase_a():
        for move in late:
            move.phase_a()

    def second_weights():
        for n in (OUT, WIDE):
            gathers[n].phase_sibling()
            for name in GROUPS[n]:
                spread(name, bufs[n], unit_offset(name), spread_ref, natural[name])
        gathers[DOWN].phase_sibling()
        spread_down(bufs[DOWN], R.nat_d)
        for move in gathers:
            move.finish()

    def after_feed_forward():
        down_gradient(R, R.nat_d)
        collect_down(R.nat_d, bufs[DOWN])
        sums[DOWN].stage_one()
        for name, base in (("g", GATE_BASE), ("u", UP_BASE)):
            def read(rows, q, fold, base=base):
                tiles = [
                    R.wide[pl.ds(pl.multiple_of(rows + base + (2 * q + s) * D, 16), 144), :] for s in range(2)
                ]
                return jnp.concatenate(tiles, axis=1).astype(BF)

            collect(name, read, bufs[WIDE], unit_offset(name), collect_ref)
        sums[WIDE].stage_one()
        sums[DOWN].stage_two()
        out_gradient(R, R.nat_o)
        collect("o", reader(R.nat_o), bufs[OUT], unit_offset("o"), collect_ref)
        sums[OUT].stage_one()
        sums[WIDE].stage_two()

    def to_owner(name):
        number, owner, width = UNIT_NAMES.index(name), OWNERS[name], own_width(name)
        target = held.at[c, a, b, z, :, pl.ds(0, width)]

        @pl.when(me != owner)
        def _():
            remote(mslab[name], target, up_send.at[number], up_recv.at[slot(*own)], owner).start()

        @pl.when(me == owner)
        def _():
            held[c, a, b, z, :, 0:width] = mslab[name][...]

    def settle(n):
        sums[n].result(totals[n])
        for name in GROUPS[n]:
            off = unit_offset(name)
            fresh = (momentum_decay * old[name][...] + totals[n][:, off : off + slab_width(name)]).astype(BF)
            if name == "d":
                for k3 in range(3):
                    mslab[name][:, 640 * k3 : 640 * (k3 + 1)] = fresh[16 * k3 : 16 * (k3 + 1), :]
            else:
                mslab[name][...] = fresh
            to_owner(name)

    def between_one():
        sums[DOWN].stage_three()
        sums[OUT].stage_two()

    def between_two():
        sums[WIDE].stage_three()
        sums[DOWN].stage_four()
        sums[OUT].stage_three()

    def between_three():
        settle(DOWN)
        sums[WIDE].stage_four()
        sums[OUT].stage_four()

    def after_attention():
        first_gradients(R, R.nat_o, R.nat_g)
        key_gain(R)
        row = lax.broadcasted_iota(jnp.int32, (32, 2 * D), 0) * 36
        col = lane((32, 2 * D))
        keep = jnp.logical_and(col >= row, col < row + 36)
        both_gains = jnp.concatenate([R.gain_one[...], R.gain_two[...]], axis=1)
        chosen = jnp.where(keep, jnp.broadcast_to(both_gains, (32, 2 * D)), 0.0).astype(BF)
        by_device = mm(chosen, lanes_back[...]).astype(BF)
        collect("kv", reader(R.nat_g), bufs[QKV], unit_offset("kv"), collect_ref)
        collect(
            "q", reader(R.nat_o), bufs[QKV], unit_offset("q"), collect_ref, lambda zz: mm(gain_put[zz], by_device)
        )
        sums[QKV].stage_one()
        settle(WIDE)
        sums[QKV].stage_two()
        settle(OUT)

    def arrived(width):
        def one(j, _):
            @pl.when(j != slot(*own))
            def _():
                ref = held.at[j // 16, lax.rem(j // 8, 2), lax.rem(j // 4, 2), lax.rem(j, 4), :, pl.ds(0, width)]
                remote(ref, ref, up_send.at[0], up_recv.at[j], sibling).wait_recv()

            return 0

        lax.fori_loop(0, 32, one, 0)

    def give_back(name):
        width = own_width(name)

        def one(j, wait):
            cc, aa, bb, zz = j // 16, lax.rem(j // 8, 2), lax.rem(j // 4, 2), lax.rem(j, 4)
            y = aa * (1 - cc) + bb * cc
            x = bb * (1 - cc) + aa * cc
            target = ((zz * 2 + y) * 2 + x) * 2 + cc
            ref = held.at[cc, aa, bb, zz, :, pl.ds(0, width)]

            @pl.when(j != slot(*own))
            def _():
                copy = remote(ref, oslab[name], down_send.at[j], down_recv.at[UNIT_NAMES.index(name)], target)
                if wait:
                    copy.wait_send()
                else:
                    copy.start()

        def start(j, _):
            one(j, False)
            return 0

        def finish(j, _):
            one(j, True)
            return 0

        lax.fori_loop(0, 32, start, 0)
        oslab[name][...] = held[c, a, b, z, :, 0:width]
        lax.fori_loop(0, 32, finish, 0)

    e_ref, r_ref = R.nat_u.at[:, 0:640], R.nat_u.at[:, 640:1280]

    def is_owner(*names):
        hit = me == OWNERS[names[0]]
        for name in names[1:]:
            hit = jnp.logical_or(hit, me == OWNERS[name])
        return hit

    def own_each(names):
        for name in names:
            pl.when(me == OWNERS[name])(lambda name=name: give_back(name))

    def end():
        sums[QKV].stage_three()
        sums[QKV].stage_four()
        settle(QKV)

        @pl.when(is_owner("g", "u"))
        def _():
            arrived(own_width("g"))
            spread("g", held, 0, spread_ref, R.nat_g)
            newton_schulz(R.wide, R.nat_g, (0, FF), e_ref, r_ref)
            collect("g", reader(R.nat_g), held, 0, collect_ref)
            own_each(("g", "u"))

        @pl.when(is_owner("d"))
        def _():
            arrived(own_width("d"))
            spread_own_down(held, R.nat_d)
            newton_schulz(R.wide, R.nat_d, (0, D), e_ref, r_ref)
            collect_own_down(R.nat_d, held)
            own_each(("d",))

        @pl.when(is_owner("q", "o"))
        def _():
            arrived(own_width("q"))
            spread("q", held, 0, spread_ref, R.nat_q)
            rows_of = gain_rows(held[:, :, :, :, :, 640:768].reshape(512, 128), select_ref)
            squares = jnp.sum(rows_of * rows_of, axis=1, keepdims=True)
            scales = [
                lax.rsqrt(jnp.sum(squares[16 * h : 16 * h + 16], axis=0, keepdims=True) * (1.0 / D) + 1e-06)
                for h in range(2)
            ]
            newton_schulz(R.wide, R.nat_q, (0, 640), e_ref, r_ref)

            def scale_extra(zz):
                scale = jnp.where(zz < 2, scales[0], scales[1])
                high = scale.astype(BF).astype(F32)
                row16 = lax.rem(lax.broadcasted_iota(jnp.int32, (128, 128), 0), 16)
                return jnp.where(row16 == 7, high, 0.0) + jnp.where(row16 == 15, scale - high, 0.0)

            collect("q", reader(R.nat_q), held, 0, collect_ref, scale_extra)
            own_each(("q", "o"))

        @pl.when(is_owner("kv"))
        def _():
            arrived(own_width("kv"))
            spread("kv", held, 0, spread_ref, R.nat_kv)
            newton_schulz(R.wide, R.nat_kv, (0, KVD), e_ref, r_ref)
            newton_schulz(R.wide, R.nat_kv, (256, 256 + KVD), e_ref, r_ref)
            collect("kv", reader(R.nat_kv), held, 0, collect_ref)
            own_each(("kv",))

        for name in ("d", "g", "u", "o", "kv", "q"):
            number = UNIT_NAMES.index(name)

            @pl.when(me != OWNERS[name])
            def _():
                remote(oslab[name], oslab[name], down_send.at[0], down_recv.at[number], sibling).wait_recv()

            directions[name][...] = oslab[name][...]

        for name in UNIT_NAMES:
            number = UNIT_NAMES.index(name)
            target = held.at[c, a, b, z, :, pl.ds(0, own_width(name))]

            @pl.when(me != OWNERS[name])
            def _():
                remote(mslab[name], target, up_send.at[number], up_recv.at[slot(*own)], OWNERS[name]).wait_send()

        for move in sums:
            move.finish()

    steps = types.SimpleNamespace(
        begin=begin,
        first_weights=first_weights,
        forward=(phase_z, phase_b, phase_a),
        second_weights=second_weights,
        after_feed_forward=after_feed_forward,
        backward=(between_one, between_two, between_three),
        after_attention=after_attention,
        end=end,
    )
    run_layer(R, tok_t, positions, cot_t, freqs, out_t, grad_t, steps)


def collect_constants():
    forward = spread_matrices()
    put = np.zeros((4, 128, 32), np.float32)
    for zz in range(4):
        for d in range(8):
            put[zz, 16 * place_of(d) + 7, 8 * zz + d] = 1
    low = ml_dtypes.bfloat16
    return (
        forward.astype(low),
        forward.transpose(0, 2, 1).astype(low),
        gain_select().astype(low),
        gain_lanes().astype(low),
        gain_lanes().T.astype(low),
        put.astype(low),
    )


def whole_call(tokens, positions, cotangent, w, gains, m, m_gains):
    shape = jax.ShapeDtypeStruct
    args = (*layer_inputs(tokens, positions, cotangent), *w, gains, *m, m_gains, *collect_constants())
    stages = []
    for lead in ((2, 2, 4), (2, 4), (4,), (3,)):
        stages += [pltpu.VMEM(lead + group_shape(group), BF) for group in GROUPS]
    travel = [pltpu.VMEM((16, own_width(n)), BF) for n in UNIT_NAMES]
    outs = (
        [shape((D, SEQ), F32)] * 2
        + [shape(group_shape(group), F32) for group in GROUPS]
        + [shape((16, own_width(n)), BF) for n in UNIT_NAMES]
    )
    return pl.pallas_call(
        whole_kernel,
        out_shape=tuple(outs),
        in_specs=[hbm(), vmem(), hbm()] + [vmem()] * (len(args) - 3),
        out_specs=(hbm(), hbm()) + (vmem(),) * 10,
        scratch_shapes=slab_buffers()
        + stages
        + [pltpu.VMEM((12, 48, 128), F32), pltpu.VMEM((16, 256), F32), pltpu.VMEM((8, 128), F32)]
        + [pltpu.VMEM((ROWS_D, 640) if n == "d" else (16, unit_width(n)), F32) for n in UNIT_NAMES]
        + travel
        + travel
        + [pltpu.VMEM((2, 2, 2, 4, 16, OWN_WIDTH), BF)]
        + layer_scratch()
        + [
            pltpu.SemaphoreType.DMA((4, 31)),
            pltpu.SemaphoreType.DMA((4, 32)),
            pltpu.SemaphoreType.DMA((4, 7)),
            pltpu.SemaphoreType.DMA((4, 7)),
            pltpu.SemaphoreType.DMA((6,)),
            pltpu.SemaphoreType.DMA((32,)),
            pltpu.SemaphoreType.DMA((32,)),
            pltpu.SemaphoreType.DMA((6,)),
        ],
        compiler_params=pltpu.CompilerParams(
            collective_id=0, has_side_effects=True, vmem_limit_bytes=VMEM_LIMIT
        ),
        name="layer_and_step",
    )(*args)


def finish_kernel(*refs):
    totals = refs[0:4]
    directions = dict(zip(UNIT_NAMES, refs[4:10]))
    w, gains = refs[10:17], refs[17]
    m, m_gains = refs[18:25], refs[25]
    grad_out, grad_gains = refs[26:33], refs[33]
    new_m, new_m_gains = refs[34:41], refs[41]
    new_w, new_gains = refs[42:49], refs[49]
    scr, fold_scr = refs[50:52]
    shapes = matrix_shapes()
    for group, total in zip(GROUPS, totals):
        for name in group:
            off = unit_offset(name)
            unpack_slab(name, total[:, off : off + slab_width(name)], scr, fold_scr)
            for index, tile, tiles2, rows in PARTS[name]:
                store_rows(scr, grad_out[index], rows, tiles2, tile)
                new_m[index][...] = momentum_decay * m[index][...] + grad_out[index][...]
            if name == "q":
                grad_gains[...] = fold_scr[7:8, 0:36]
                new_m_gains[...] = momentum_decay * m_gains[...] + grad_gains[...]
            unpack_slab(name, own_slab_value(name, directions[name]).astype(F32), scr, fold_scr)
            for index, tile, tiles2, rows in PARTS[name]:
                store_rows(scr, new_w[index], rows, tiles2, tile)
                rate = 0.2 * math.sqrt(max(shapes[index]))
                old = w[index][...]
                new_w[index][...] = old - matrix_rate * (weight_decay * old + rate * new_w[index][...])
            if name == "q":
                scale = fold_scr[7:8, 0:36] + fold_scr[15:16, 0:36]
                new_gains[...] = gains[...] - gain_rate * (new_m_gains[...] * scale)


def finish_call(slabs, w, gains, m, m_gains):
    outs = [(v.shape, F32) for v in (*w, gains)] * 3
    return local_call(
        finish_kernel, "finish", (*slabs, *w, gains, *m, m_gains), outs, (((12, 48, 128), F32), ((16, 256), F32))
    )


def orthogonal(matrix):
    rows, cols = matrix.shape
    wide = matrix.T if rows > cols else matrix
    state = wide / (jnp.sqrt(jnp.sum(wide * wide)) + 1e-07)
    for turn_number in range(NS_ITERS):
        gram = jnp.dot(state, state.T, precision=precise)
        poly = coef_two * gram + coef_three * jnp.dot(gram, gram, precision=precise)
        state = coef_one * state + jnp.dot(poly, state, precision=precise)
    return state.T if rows > cols else state


def direction_of(index, flat):
    if index < 7:
        return orthogonal(flat.reshape(matrix_shapes()[index])).reshape(-1)
    halves = flat.reshape(2, D)
    return (halves * lax.rsqrt(jnp.mean(halves * halves, axis=1, keepdims=True) + 1e-06)).reshape(-1)


def gather_all(flat):
    return lax.all_gather(flat.astype(BF), "dp", axis=0, tiled=True)


def scatter_sum(whole):
    return lax.psum_scatter(whole, "dp", scatter_dimension=0, tiled=True)


def pad_columns(matrix, width):
    return jnp.pad(matrix, ((0, 0), (0, width - matrix.shape[1])))


def per_device(tokens, positions, cotangent, *rest):
    w, gains, m, m_gains = rest[0:7], rest[7], rest[8:15], rest[15]
    shapes = matrix_shapes()
    whole = [gather_all(v).reshape(s) for v, s in zip(w, shapes)]
    padded = (
        pad_columns(whole[0], 640),
        jnp.concatenate([pad_columns(whole[1], 256), pad_columns(whole[2], 256)], axis=1),
        pad_columns(whole[3], 640),
        whole[4],
        whole[5],
        pad_columns(whole[6], 640),
    )
    block_out, input_grad, grads, *gain_grads = layer(
        tokens, positions, cotangent, gather_all(gains).astype(F32).reshape(1, -1), *padded
    )
    parts = (
        grads[0][:, :D],
        grads[1][:, :KVD],
        grads[1][:, 256 : 256 + KVD],
        grads[2][:, :D],
        grads[3],
        grads[4],
        grads[5][:, :D],
    )
    shares = [scatter_sum(g.astype(F32).reshape(-1)) for g in parts] + [scatter_sum(jnp.concatenate(gain_grads, axis=1).reshape(-1))]
    moments = [momentum_decay * old + share for old, share in zip((*m, m_gains), shares)]
    device = lax.axis_index("dp")
    stride = lax.axis_size("dp") // 8
    pieces = []
    for i in range(8):
        full = gather_all(moments[i]).astype(F32)
        found = lax.cond(
            device == i * stride, lambda v, i=i: direction_of(i, v), jnp.zeros_like, full
        )
        pieces.append(scatter_sum(found))
    updated = []
    for i in range(7):
        scale = 0.2 * math.sqrt(max(shapes[i]))
        updated.append(w[i] - matrix_rate * (weight_decay * w[i] + scale * pieces[i]))
    new_gains = gains - gain_rate * pieces[7]
    return (block_out, input_grad, *moments, *updated, new_gains, *shares)


def per_device_32(tokens, positions, cotangent, *rest):
    w, gains, m, m_gains = rest[0:7], rest[7], rest[8:15], rest[15]
    w = [v.reshape(-1, 128) for v in w]
    m = [v.reshape(-1, 128) for v in m]
    gains, m_gains = gains.reshape(1, -1), m_gains.reshape(1, -1)
    out_t, grad_t, *slabs = whole_call(tokens, positions, cotangent, w, gains, m, m_gains)
    flat = [v.reshape(-1) for v in finish_call(slabs, w, gains, m, m_gains)]
    return (out_t.T, grad_t.T, *flat[8:16], *flat[16:24], *flat[0:8])


def solution(mesh):
    placed = (P("dp", None), P("dp"), P("dp", None)) + (P("dp"),) * 16
    return jax.shard_map(
        per_device_32 if mesh.shape["dp"] == 32 else per_device,
        mesh=mesh,
        in_specs=placed,
        out_specs=(P("dp", None), P("dp", None)) + (P("dp"),) * 24,
        check_vma=False,
    )
```

```python
import math
import types

import jax
import jax.numpy as jnp
import ml_dtypes
import numpy as np
from jax import lax
from jax.experimental import pallas as pl
from jax.experimental.pallas import tpu as pltpu
from jax.sharding import PartitionSpec as P

HEADS = 9
KV_HEADS = 3
HEAD_DIM = 64
D = 576
KVD = 192
FF = 1536
SEQ = 1024
NS_ITERS = 5


eps_norm = 1e-05
rope_base = 100000.0
momentum_decay = 0.95
matrix_rate = 0.1
weight_decay = 0.1
gain_rate = 0.25
coef_one = 3.4445
coef_two = -4.775
coef_three = 2.0315
precise = lax.Precision.HIGHEST
BF = jnp.bfloat16
F32 = jnp.float32
MESH = pl.DeviceIdType.MESH
VMEM_LIMIT = 63 * 2**20


def matrix_shapes():
    return ((D, D), (D, KVD), (D, KVD), (D, D), (D, FF), (D, FF), (FF, D))


UNITS = {
    "q": (640, 128, 5),
    "kv": (512, 128, 4),
    "o": (640, 128, 5),
    "g": (1536, 256, 6),
    "u": (1536, 256, 6),
}
GROUPS = (("q", "kv"), ("o",), ("g",), ("u",), ("d",))
ROWS_D = 48


def unit_width(name):
    return UNITS[name][0] + UNITS[name][1]


def group_shape(group):
    if group == ("d",):
        return (ROWS_D, 640)
    return (16, sum(unit_width(u) for u in group))


def unit_offset(name):
    for group in GROUPS:
        off = 0
        for u in group:
            if u == name:
                return off
            off += unit_width(u)
    raise KeyError(name)


def place_of(d):
    y, x, c = d // 4, (d // 2) % 2, d % 2
    return c * 4 + (y * 2 + x if c == 0 else x * 2 + y)


def spread_matrices():
    out = np.zeros((6, 144, 256), np.float32)
    for q in range(6):
        for d in range(8):
            p = place_of(d)
            for r in range(16):
                out[q, 18 * d + r, 16 * p + r] = 1
            for e in range(2):
                out[q, 18 * d + 16 + e, 128 + 16 * p + 8 * e + q] = 1
    return out


def gain_select():
    out = np.zeros((32, 512), np.float32)
    for i in range(32):
        z, d = i // 8, i % 8
        out[i, (place_of(d) * 4 + z) * 16 + 7] = 1
    return out


def gain_lanes():
    out = np.zeros((128, 2 * D), np.float32)
    for j in range(2 * D):
        out[j % 36, j] = 1
    return out


def coords():
    me = lax.axis_index("dp")
    z, y, x, c = me // 8, lax.rem(me // 4, 2), lax.rem(me // 2, 2), lax.rem(me, 2)
    a = y * (1 - c) + x * c
    b = x * (1 - c) + y * c

    def dev(zz, yy, xx, cc):
        return ((zz * 2 + yy) * 2 + xx) * 2 + cc

    peer_b = dev(z, y + (1 - 2 * y) * c, x + (1 - 2 * x) * (1 - c), c)
    peer_a = dev(z, y + (1 - 2 * y) * (1 - c), x + (1 - 2 * x) * c, c)
    sibling = dev(z, y, x, 1 - c)

    def along(step):
        return dev(lax.rem(z + step, 4), y, x, c)

    return me, (z, a, b, c), peer_a, peer_b, sibling, along


def remote(src, dst, send, recv, target):
    return pltpu.make_async_remote_copy(
        src_ref=src, dst_ref=dst, send_sem=send, recv_sem=recv, device_id=(target,), device_id_type=MESH
    )


def slot(c, a, b, z):
    return ((c * 2 + a) * 2 + b) * 4 + z


class Gather:
    def __init__(self, buf, send, recv, where):
        self.buf, self.send, self.recv = buf, send, recv
        self.me, (self.z, self.a, self.b, self.c), self.peer_a, self.peer_b, self.sibling, self.along = where
        self.count = 0

    def push(self, index, target):
        ref = self.buf.at[index]
        copy = remote(ref, ref, self.send.at[self.count], self.recv.at[slot(*index)], target)
        copy.start()
        self.count += 1

    def arrive(self, index):
        ref = self.buf.at[index]
        remote(ref, ref, self.send.at[0], self.recv.at[slot(*index)], self.sibling).wait_recv()

    def phase_own(self):
        own = (self.c, self.a, self.b, self.z)
        for step in (1, 3, 2):
            self.push(own, self.along(step))
        self.push(own, self.peer_b)
        self.push(own, self.peer_a)
        self.push(own, self.sibling)

    def from_z(self, *steps):
        for step in steps:
            index = (self.c, self.a, self.b, lax.rem(self.z + step, 4))
            self.arrive(index)
            self.push(index, self.peer_b)
            self.push(index, self.peer_a)
            self.push(index, self.sibling)

    def from_b(self, *steps):
        for step in steps:
            index = (self.c, self.a, 1 - self.b, lax.rem(self.z + step, 4))
            self.arrive(index)
            self.push(index, self.peer_a)
            self.push(index, self.sibling)

    def from_a(self, other, *steps):
        for step in steps:
            index = (self.c, 1 - self.a, 1 - self.b if other else self.b, lax.rem(self.z + step, 4))
            self.arrive(index)
            self.push(index, self.sibling)

    def phase_sibling(self):
        for aa in range(2):
            for bb in range(2):
                for zz in range(4):
                    self.arrive((1 - self.c, aa, bb, zz))

    def finish(self):
        own = (self.c, self.a, self.b, self.z)
        ref = self.buf.at[own]
        for n in range(self.count):
            remote(ref, ref, self.send.at[n], self.recv.at[slot(*own)], self.sibling).wait_send()


def low_lanes(rows):
    return lax.broadcasted_iota(jnp.int32, (rows, 128), 1) < 64


def turn(v):
    return pltpu.roll(v, 64, axis=1)


def load_rows(flat, scr, rows, tiles2):
    if tiles2 % 2 == 0:
        nt = tiles2 // 2
        for t in range(nt):
            scr[t, 0:rows, :] = flat[pl.ds(t, rows, stride=nt), :]
        return
    half, h = rows // 2, (tiles2 - 1) // 2
    low = low_lanes(half)
    pair = [flat[pl.ds(t, half, stride=tiles2), :] for t in range(tiles2)]
    turned = {t: turn(pair[t]) for t in range(h, tiles2)}
    for j in range(h + 1):
        even = pair[j] if j < h else jnp.where(low, pair[h], 0.0)
        odd = jnp.where(low, turned[h + j], turned[h + j + 1] if j < h else 0.0)
        scr[j, pl.ds(0, half, stride=2), :] = even
        scr[j, pl.ds(1, half, stride=2), :] = odd


def store_rows(scr, flat, rows, tiles2, base=0):
    if tiles2 % 2 == 0:
        nt = tiles2 // 2
        for t in range(nt):
            flat[pl.ds(t, rows, stride=nt), :] = scr[base + t, 0:rows, :]
        return
    half, h = rows // 2, (tiles2 - 1) // 2
    low = low_lanes(half)
    even = [scr[base + j, pl.ds(0, half, stride=2), :] for j in range(h + 1)]
    odd = [turn(scr[base + j, pl.ds(1, half, stride=2), :]) for j in range(h + 1)]
    for t in range(tiles2):
        if t < h:
            value = even[t]
        elif t == h:
            value = jnp.where(low, even[h], odd[0])
        else:
            value = jnp.where(low, odd[t - h - 1], odd[t - h])
        flat[pl.ds(t, half, stride=tiles2), :] = value


PARTS = {
    "q": ((0, 0, 9, 18),),
    "kv": ((1, 0, 3, 18), (2, 2, 3, 18)),
    "o": ((3, 0, 9, 18),),
    "g": ((4, 0, 24, 18),),
    "u": ((5, 0, 24, 18),),
    "d": ((6, 0, 9, 48),),
}


def pack_slab(name, scr, fold_scr, slab, off, gains=None):
    if name == "d":
        for t in range(5):
            slab[:, off + 128 * t : off + 128 * (t + 1)] = scr[t, 0:48, :].astype(slab.dtype)
        return
    padded, fold, chunks = UNITS[name]
    for t in range(padded // 128):
        slab[:, off + 128 * t : off + 128 * (t + 1)] = scr[t, 0:16, :].astype(slab.dtype)
    fold_scr[...] = jnp.zeros_like(fold_scr)
    per = fold // 128
    for q in range(chunks):
        for k in range(per):
            for e in range(2):
                fold_scr[e * 8 + q : e * 8 + q + 1, 128 * k : 128 * (k + 1)] = scr[q * per + k, 16 + e : 17 + e, :]
    if gains is not None:
        fold_scr[7:8, 0:128] = gains
    slab[:, off + padded : off + padded + fold] = fold_scr[:, 0:fold].astype(slab.dtype)


def unpack_slab(name, main, scr, fold_scr):
    if name == "d":
        for t in range(5):
            scr[t, 0:48, :] = main[:, 128 * t : 128 * (t + 1)]
        return
    padded, fold, chunks = UNITS[name]
    for t in range(padded // 128):
        scr[t, 0:16, :] = main[:, 128 * t : 128 * (t + 1)]
    fold_scr[:, 0:fold] = main[:, padded : padded + fold]
    per = fold // 128
    for q in range(chunks):
        for k in range(per):
            for e in range(2):
                scr[q * per + k, 16 + e : 17 + e, :] = fold_scr[e * 8 + q : e * 8 + q + 1, 128 * k : 128 * (k + 1)]


def spread(name, buf, off, spread_ref, dest):
    padded, fold, chunks = UNITS[name]

    def plane(z, _):
        folded = buf[:, :, :, z, :, off + padded : off + padded + fold].reshape(128, fold)
        for q in range(chunks):
            main = buf[:, :, :, z, :, off + q * fold : off + (q + 1) * fold].reshape(128, fold)
            both = jnp.concatenate([main, folded], axis=0)
            block = jnp.dot(spread_ref[q], both, preferred_element_type=F32)
            dest[pl.ds(pl.multiple_of(z * 144, 16), 144), q * fold : (q + 1) * fold] = block.astype(dest.dtype)
        return 0

    lax.fori_loop(0, 4, plane, 0)


def spread_down(buf, dest):
    for z in range(4):
        for d in range(8):
            y, x, c = d // 4, (d // 2) % 2, d % 2
            a, b = (y, x) if c == 0 else (x, y)
            dest[(z * 8 + d) * 48 : (z * 8 + d + 1) * 48, :] = buf[c, a, b, z].astype(dest.dtype)


def reader(source):
    return lambda first, q, fold: source[pl.ds(first, 144), q * fold : (q + 1) * fold].astype(BF)


def collect(name, read, buf, off, collect_ref, extra=None, after=None):
    padded, fold, chunks = UNITS[name]

    def plane(z, _):
        first = pl.multiple_of(z * 144, 16)
        total = jnp.zeros((128, fold), F32)
        for q in range(chunks):
            both = jnp.dot(collect_ref[q], read(first, q, fold), preferred_element_type=F32)
            buf[:, :, :, z, :, off + q * fold : off + (q + 1) * fold] = (
                both[0:128].astype(BF).reshape(2, 2, 2, 16, fold)
            )
            total = total + both[128:256]
        if extra is not None:
            total = total + extra(z)
        buf[:, :, :, z, :, off + padded : off + padded + fold] = total.astype(BF).reshape(2, 2, 2, 16, fold)
        if after is not None:
            after(z)
        return 0

    lax.fori_loop(0, 4, plane, 0)


def collect_down(source, buf):
    for z in range(4):
        for d in range(8):
            y, x, c = d // 4, (d // 2) % 2, d % 2
            a, b = (y, x) if c == 0 else (x, y)
            buf[c, a, b, z] = source[(z * 8 + d) * 48 : (z * 8 + d + 1) * 48, :].astype(BF)


def spread_own_down(buf, dest):
    for z in range(4):
        for d in range(8):
            y, x, c = d // 4, (d // 2) % 2, d % 2
            a, b = (y, x) if c == 0 else (x, y)
            for k in range(3):
                first = (z * 8 + d) * 48 + 16 * k
                dest[first : first + 16, :] = buf[c, a, b, z, :, 640 * k : 640 * (k + 1)]


def collect_own_down(source, buf):
    for z in range(4):
        for d in range(8):
            y, x, c = d // 4, (d // 2) % 2, d % 2
            a, b = (y, x) if c == 0 else (x, y)
            for k in range(3):
                first = (z * 8 + d) * 48 + 16 * k
                buf[c, a, b, z, :, 640 * k : 640 * (k + 1)] = source[first : first + 16, :]


def load_unit(name, flats, scr):
    for index, tile, tiles2, rows in PARTS[name]:
        view = scr if tile == 0 else scr.at[pl.ds(tile, (tiles2 + 1) // 2)]
        load_rows(flats[index], view, rows, tiles2)


def read_gains(buf, select_ref, lanes_ref, gains_out):
    rows = gain_rows(buf[:, :, :, :, :, 640:768].reshape(512, 128), select_ref)
    wide = jnp.dot(rows.astype(BF), lanes_ref[...], preferred_element_type=F32)
    device = lax.broadcasted_iota(jnp.int32, wide.shape, 0)
    column = lax.broadcasted_iota(jnp.int32, wide.shape, 1)
    low = device * 36
    keep = jnp.logical_and(column >= low, column < low + 36)
    gains_out[...] = jnp.sum(jnp.where(keep, wide, 0.0), axis=0, keepdims=True)


def gain_rows(folds, select_ref):
    return jnp.dot(select_ref[...], folds, preferred_element_type=F32)


def vmem():
    return pl.BlockSpec(memory_space=pltpu.VMEM)


def slab_buffers():
    lead = (2, 2, 2, 4)
    shapes = [lead + group_shape(group) for group in GROUPS]
    return [pltpu.VMEM(s, BF) for s in (shapes[0], shapes[1], (2,) + shapes[2], shapes[4])]


def group_buffers(refs):
    return (refs[0], refs[1], refs[2].at[0], refs[2].at[1], refs[3])


NN = (((1,), (0,)), ((), ()))
NT = (((1,), (1,)), ((), ()))
TN = (((0,), (0,)), ((), ()))
TILES = 5
BLOCK = 256
LOG2E = 1.4426950408889634


def mm(left, right, dims=NN):
    return lax.dot_general(left, right, dims, preferred_element_type=F32)


def block_rows(i, size=BLOCK):
    return pl.ds(pl.multiple_of(i * size, size), size)


def frequencies():
    half = HEAD_DIM // 2
    freqs = rope_base ** (-np.arange(half) * 2.0 / HEAD_DIM)
    return np.tile(freqs.astype(np.float32), 4).reshape(1, 128)


def lane(shape):
    return lax.broadcasted_iota(jnp.int32, shape, len(shape) - 1)


def cos_sin(angle):
    turns = jnp.floor(angle * 0.6366197723675814 + 0.5)
    rest = ((angle - turns * 1.5703125) - turns * 4.837512969970703e-4) - turns * 7.549789948768648e-8
    square = rest * rest
    sine = rest + rest * square * (
        -1.6666654611e-1 + square * (8.3321608736e-3 + square * -1.9515295891e-4)
    )
    cosine = (1.0 - 0.5 * square) + square * square * (
        4.166664568298827e-2 + square * (-1.388731625493765e-3 + square * 2.443315711809948e-5)
    )
    quarter = turns - 4.0 * jnp.floor(turns * 0.25)
    odd = jnp.logical_or(quarter == 1.0, quarter == 3.0)
    swapped_cos = jnp.where(odd, sine, cosine)
    swapped_sin = jnp.where(odd, cosine, sine)
    cos_sign = jnp.logical_or(quarter == 1.0, quarter == 2.0)
    return (
        jnp.where(cos_sign, -swapped_cos, swapped_cos),
        jnp.where(quarter >= 2.0, -swapped_sin, swapped_sin),
    )


def make_tables(positions, freqs, cos_ref, sin_ref):
    for r in range(SEQ // 128):
        row = jnp.broadcast_to(positions[r : r + 1, :].astype(F32), (128, 128))
        column = jnp.sum(jnp.where(diagonal(128), row, 0.0), axis=1, keepdims=True)
        cosine, sine = cos_sin(column * freqs[...])
        cos_ref[128 * r : 128 * (r + 1), :] = cosine
        sin_ref[128 * r : 128 * (r + 1), :] = jnp.where(lax.rem(lane((128, 128)), 64) < 32, -sine, sine)


def rotate_tile(value, cosine, sine, inverse=False):
    first = lax.rem(lane(value.shape), 64) < 32
    swapped = jnp.where(first, pltpu.roll(value, 96, axis=1), pltpu.roll(value, 32, axis=1))
    if inverse:
        return value * cosine - swapped * sine
    return value * cosine + swapped * sine


def row_scale(value):
    return lax.rsqrt(jnp.sum(value * value, axis=1, keepdims=True) * (1.0 / D) + eps_norm)


def turn_over(source, dest):
    def body(i, _):
        rows = block_rows(i)
        dest[rows, :] = source[:, rows].T
        return 0

    lax.fori_loop(0, SEQ // BLOCK, body, 0)


def normalize_tokens(tokens, gain, a_ref):
    def body(i, _):
        rows = block_rows(i)
        x = tokens[rows, :].astype(F32)
        a_ref[rows, :] = (x * row_scale(x) * gain).astype(BF)
        return 0

    lax.fori_loop(0, SEQ // BLOCK, body, 0)


def heads_in(a_ref, w_q, w_kv, cos_ref, sin_ref, q_ref, k_ref, v_ref, between=()):
    def body(i, _):
        rows = block_rows(i)
        a = a_ref[rows, :]
        cosine, sine = cos_ref[rows, :], sin_ref[rows, :]
        pq = mm(a, w_q[...])
        for t in range(TILES):
            turned = rotate_tile(pq[:, 128 * t : 128 * (t + 1)], cosine, sine).astype(BF)
            q_ref[t, rows, :] = turned * jnp.asarray(HEAD_DIM ** (-0.5), BF)
        pkv = mm(a, w_kv[...])
        low = lane((BLOCK, 128)) < 64
        for ref, base, rotary in ((k_ref, 0, True), (v_ref, 256, False)):
            for half in range(2):
                tile = pkv[:, base + 128 * half : base + 128 * (half + 1)]
                if rotary:
                    tile = rotate_tile(tile, cosine, sine)
                other = turn(tile)
                ref[2 * half, rows, :] = jnp.where(low, tile, other).astype(BF)
                if half == 0:
                    ref[1, rows, :] = jnp.where(low, other, tile).astype(BF)
        for number, action in enumerate(between):
            pl.when(i == number)(action)
        return 0

    lax.fori_loop(0, SEQ // BLOCK, body, 0)


def own_lanes(value, parity):
    here = lane(value.shape) // 64 == parity
    return jnp.where(here, value, jnp.zeros_like(value))


def attend_group(g, q_ref, k_ref, v_ref, o_ref, lse_ref):
    for h in range(HEADS // KV_HEADS):
        j = 3 * g + h
        t, parity = j // 2, lax.rem(j, 2)
        for i in range(SEQ // BLOCK):
            end = BLOCK * (i + 1)
            query = q_ref[t, BLOCK * i : end, :]
            s = mm(own_lanes(k_ref[g, 0:end, :], parity), query, NT)
            rows = lax.broadcasted_iota(jnp.int32, (BLOCK, BLOCK), 0)
            cols = lax.broadcasted_iota(jnp.int32, (BLOCK, BLOCK), 1)
            corner = jnp.where(cols >= rows, s[BLOCK * i :, :], -1e30)
            s = jnp.concatenate([s[: BLOCK * i, :], corner], axis=0) if i else corner
            top = jnp.max(s, axis=0, keepdims=True)
            weights = jnp.exp2((s - top) * LOG2E)
            total = jnp.sum(weights, axis=0, keepdims=True)
            probs = (weights * (1.0 / total)).astype(BF)
            out = mm(probs, own_lanes(v_ref[g, 0:end, :], parity), TN)
            o_ref[t, BLOCK * i : end, :] += out.astype(BF)
            lse_ref[j, :, BLOCK * i : end] = top * LOG2E + jnp.log2(total)


def attend_all(q_ref, k_ref, v_ref, o_ref, lse_ref, between=()):
    o_ref[...] = jnp.zeros_like(o_ref)

    def body(g, _):
        attend_group(g, q_ref, k_ref, v_ref, o_ref, lse_ref)
        for number, action in enumerate(between):
            pl.when(g == number)(action)
        return 0

    lax.fori_loop(0, KV_HEADS, body, 0)


DK_BASE = TILES * SEQ
DV_BASE = DK_BASE + 2 * KV_HEADS * SEQ
WIDE_ROWS = DV_BASE + 2 * KV_HEADS * SEQ
GATE_BASE = 0
UP_BASE = 12 * D


def read_z(z_buf, first, count):
    blocks = []
    for i in range(SEQ // BLOCK):
        blocks.append(z_buf[i // 2, i % 2, :, :, :, :, first : first + count].reshape(BLOCK, count))
    return jnp.concatenate(blocks, axis=0)


STAGE_BASE = UP_BASE + 12 * D


class Drain:
    def __init__(self, wide, sems, result):
        self.wide, self.sems, self.result = wide, sems, result

    def rows(self, number, half):
        return pl.ds(pl.multiple_of(STAGE_BASE + (2 * number + half) * D, 8), D)

    def copy(self, i, number, half):
        columns = pl.ds(pl.multiple_of(i * BLOCK + 128 * half, 128), 128)
        return pltpu.make_async_copy(
            self.wide.at[self.rows(number, half)], self.result.at[:, columns], self.sems.at[number, half]
        )

    def put(self, i, value):
        number = lax.rem(i, 2)

        @pl.when(i >= 2)
        def _():
            for half in range(2):
                self.copy(i, number, half).wait()

        for half in range(2):
            self.wide[self.rows(number, half), :] = value[:, 128 * half : 128 * (half + 1)]
            self.copy(i, number, half).start()

    def finish(self):
        for number in range(2):
            for half in range(2):
                self.copy(number, number, half).wait()


def feed_forward(R, gain, drain):
    w_o, w_g, w_u, w_d = R.nat_o, R.nat_g, R.nat_u, R.nat_d
    R.gain_two[...] = jnp.zeros_like(R.gain_two)

    def body(i, _):
        rows = block_rows(i)
        o = jnp.concatenate([R.o[t, rows, :] for t in range(TILES)], axis=1)
        x2 = R.tok[rows, :].astype(F32) + mm(o[:, 0:D], w_o[:, 0:D])
        r2 = row_scale(x2)
        n2 = x2 * r2
        h = (n2 * gain).astype(BF)
        c = R.cot[rows, :]
        gate = mm(h, w_g[...])
        upper = mm(h, w_u[...])
        grad = mm(c, w_d[:, 0:D], NT)
        sigma = 0.5 * jnp.tanh(0.5 * gate) + 0.5
        silu = gate * sigma
        z = (silu * upper).astype(BF)
        R.z_buf[i // 2, lax.rem(i, 2), :, :, :, :, 0:FF] = z.reshape(2, 2, 4, 16, FF)
        dg = (grad * upper * (sigma + silu * (1.0 - sigma))).astype(BF)
        du = (grad * silu).astype(BF)
        drain.put(i, (x2 + mm(z, w_d[:, 0:D])).T)
        dh = mm(dg, w_g[...], NT) + mm(du, w_u[...], NT)
        for base, value in ((GATE_BASE, dg), (UP_BASE, du)):
            for k in range(3):
                part = mm(h, value[:, 512 * k : 512 * (k + 1)], TN)
                for t in range(4):
                    here = slice(base + (4 * k + t) * D, base + (4 * k + t + 1) * D)
                    R.wide[here, :] += part[:, 128 * t : 128 * (t + 1)]
        R.gain_two[...] += jnp.sum(dh * n2, axis=0, keepdims=True)
        scaled = dh * gain
        mean = jnp.sum(scaled * n2, axis=1, keepdims=True) * (1.0 / D)
        dx = c.astype(F32) + r2 * (scaled - n2 * mean)
        R.dx[rows, :] = dx
        do = mm(dx.astype(BF), w_o[:, 0:D], NT)
        pick = (lax.broadcasted_iota(jnp.int32, (8, 128), 0) == lane((8, 128)) // 64).astype(BF)
        for t in range(TILES):
            if t < TILES - 1:
                tile = do[:, 128 * t : 128 * (t + 1)]
            else:
                tile = jnp.concatenate([do[:, 512:576], jnp.zeros((BLOCK, 64), F32)], axis=1)
            tile = tile.astype(BF)
            R.do[t, rows, :] = tile
            product = tile.astype(F32) * o[:, 128 * t : 128 * (t + 1)].astype(F32)
            high = product.astype(BF)
            low = (product - high.astype(F32)).astype(BF)
            inner = mm(pick, high, NT) + mm(pick, low, NT)
            R.inner[2 * t, :, rows] = inner[0:1]
            if t < TILES - 1:
                R.inner[2 * t + 1, :, rows] = inner[1:2]
        return 0

    lax.fori_loop(0, SEQ // BLOCK, body, 0)
    drain.finish()


def down_gradient(R, dest):
    for k in range(3):
        dest[512 * k : 512 * (k + 1), 0:D] = mm(read_z(R.z_buf, 512 * k, 512), R.cot[...], TN).astype(BF)
    dest[:, D:] = jnp.zeros((FF, 640 - D), BF)


def out_gradient(R, dest):
    for t in range(TILES):
        part = mm(R.o[t], R.dx[...].astype(BF), TN).astype(BF)
        rows = min(128, D - 128 * t)
        dest[128 * t : 128 * t + rows, 0:D] = part[0:rows]
    dest[:, D:] = jnp.zeros((D, 640 - D), BF)


def attend_back_group(g, R, between):
    for h in range(HEADS // KV_HEADS):
        j = 3 * g + h
        t, parity = j // 2, lax.rem(j, 2)
        for i in range(SEQ // BLOCK):
            start = BLOCK * i
            rows = slice(start, start + BLOCK)
            key = own_lanes(R.k[g, rows, :], parity)
            value = own_lanes(R.v[g, rows, :], parity)
            query, grad = R.q[t, start:, :], R.do[t, start:, :]
            probs = jnp.exp2(mm(key, query, NT) * LOG2E - R.lse[j, :, start:])
            down = lax.broadcasted_iota(jnp.int32, (BLOCK, BLOCK), 0)
            across = lax.broadcasted_iota(jnp.int32, (BLOCK, BLOCK), 1)
            corner = jnp.where(across >= down, probs[:, :BLOCK], 0.0)
            probs = jnp.concatenate([corner, probs[:, BLOCK:]], axis=1) if start + BLOCK < SEQ else corner
            ds = (probs * (mm(value, grad, NT) - R.inner[j, :, start:])).astype(BF)
            place = (2 * g + parity) * SEQ + start
            R.wide[pl.ds(pl.multiple_of(DV_BASE + place, BLOCK), BLOCK), :] += mm(probs.astype(BF), grad)
            R.wide[pl.ds(pl.multiple_of(DK_BASE + place, BLOCK), BLOCK), :] += mm(ds, query)
            R.wide[pl.ds(pl.multiple_of(t * SEQ + start, BLOCK), SEQ - start), :] += mm(ds, key, TN)
        for number in range(h, len(between), HEADS // KV_HEADS):
            if between[number] is not None:
                pl.when(j == number)(between[number])


def attend_back_all(R, between=()):
    R.wide[...] = jnp.zeros_like(R.wide)

    def body(g, _):
        attend_back_group(g, R, between)
        return 0

    lax.fori_loop(0, KV_HEADS, body, 0)


def heads_out(R):
    def body(i, _):
        rows = block_rows(i)
        cosine, sine = R.cos[rows, :], R.sin[rows, :]
        for t in range(TILES):
            tile = R.wide[pl.ds(pl.multiple_of(t * SEQ + i * BLOCK, BLOCK), BLOCK), :] * HEAD_DIM ** (-0.5)
            R.o[t, rows, :] = rotate_tile(tile, cosine, sine, True).astype(BF)
        low = lane((BLOCK, 128)) < 64
        for base, column, rotary in ((DK_BASE, 0, True), (DV_BASE, 256, False)):
            whole = []
            for g in range(KV_HEADS):
                parts = [
                    R.wide[pl.ds(pl.multiple_of(base + (2 * g + p) * SEQ + i * BLOCK, BLOCK), BLOCK), :]
                    for p in range(2)
                ]
                whole.append(parts[0] + turn(parts[1]))
            tiles = (jnp.where(low, whole[0], turn(whole[1])), jnp.where(low, whole[2], 0.0))
            for half in range(2):
                tile = rotate_tile(tiles[half], cosine, sine, True) if rotary else tiles[half]
                R.cot[rows, column + 128 * half : column + 128 * (half + 1)] = tile.astype(BF)
        return 0

    lax.fori_loop(0, SEQ // BLOCK, body, 0)


def first_gradients(R, dest_q, dest_kv):
    a = R.a[...]
    for t in range(TILES):
        dest_q[:, 128 * t : 128 * (t + 1)] = mm(a, R.o[t], TN).astype(BF)
    dest_kv[:, 0:512] = mm(a, R.cot[:, 0:512], TN).astype(BF)


def key_gain(R):
    R.gain_one[...] = jnp.zeros_like(R.gain_one)

    def body(i, _):
        rows = block_rows(i)
        dq = jnp.concatenate([R.o[t, rows, :] for t in range(TILES)], axis=1)
        da = mm(dq, R.nat_q[...], NT) + mm(R.cot[rows, 0:512], R.nat_kv[...], NT)
        x = R.tok[rows, :].astype(F32)
        R.gain_one[...] += jnp.sum(da * (x * row_scale(x)), axis=0, keepdims=True)
        R.wide[pl.ds(pl.multiple_of(i * BLOCK, BLOCK), BLOCK), :] = da[:, 0:128]
        for t in range(1, TILES):
            width = min(128, D - 128 * t)
            R.wide[pl.ds(pl.multiple_of(t * SEQ + i * BLOCK, BLOCK), BLOCK), 0:width] = da[:, 128 * t : 128 * t + width]
        return 0

    lax.fori_loop(0, SEQ // BLOCK, body, 0)


def input_gradient(R, gain, drain):
    def body(i, _):
        rows = block_rows(i)
        tiles = [R.wide[pl.ds(pl.multiple_of(t * SEQ + i * BLOCK, BLOCK), BLOCK), :] for t in range(TILES)]
        da = jnp.concatenate(tiles, axis=1)[:, 0:D]
        x = R.tok[rows, :].astype(F32)
        r1 = row_scale(x)
        n1 = x * r1
        scaled = da * gain
        mean = jnp.sum(scaled * n1, axis=1, keepdims=True) * (1.0 / D)
        drain.put(i, (R.dx[rows, :] + r1 * (scaled - n1 * mean)).T)
        return 0

    lax.fori_loop(0, SEQ // BLOCK, body, 0)
    drain.finish()


LAYER_SCRATCH = {
    "nat_q": ((D, 640), BF),
    "nat_kv": ((D, 512), BF),
    "nat_o": ((D, 640), BF),
    "nat_g": ((D, FF), BF),
    "nat_u": ((D, FF), BF),
    "nat_d": ((FF, 640), BF),
    "gains": ((1, 2 * D), F32),
    "tok": ((SEQ, D), BF),
    "cot": ((SEQ, D), BF),
    "a": ((SEQ, D), BF),
    "cos": ((SEQ, 128), F32),
    "sin": ((SEQ, 128), F32),
    "q": ((TILES, SEQ, 128), BF),
    "k": ((KV_HEADS, SEQ, 128), BF),
    "v": ((KV_HEADS, SEQ, 128), BF),
    "lse": ((HEADS, 1, SEQ), F32),
    "inner": ((HEADS, 1, SEQ), F32),
    "o": ((TILES, SEQ, 128), BF),
    "do": ((TILES, SEQ, 128), BF),
    "dx": ((SEQ, D), F32),
    "wide": ((WIDE_ROWS, 128), F32),
    "gain_one": ((1, D), F32),
    "gain_two": ((1, D), F32),
}


def layer_scratch():
    return [pltpu.VMEM(*s) for s in LAYER_SCRATCH.values()] + [
        pltpu.SemaphoreType.DMA((2,)),
        pltpu.SemaphoreType.DMA((2, 2)),
    ]


def layer_refs(refs, z_buf):
    names = list(LAYER_SCRATCH) + ["in_sems", "out_sems"]
    return types.SimpleNamespace(z_buf=z_buf, **dict(zip(names, refs)))


def nothing():
    return None


def run_layer(R, tok_t, positions, cot_t, freqs, out_t, grad_t, steps):
    copies = [
        pltpu.make_async_copy(tok_t, R.nat_g.at[:, 0:SEQ], R.in_sems.at[0]),
        pltpu.make_async_copy(cot_t, R.nat_u.at[:, 0:SEQ], R.in_sems.at[1]),
    ]
    for copy in copies:
        copy.start()
    steps.begin()
    make_tables(positions, freqs, R.cos, R.sin)
    copies[0].wait()
    turn_over(R.nat_g, R.tok)
    copies[1].wait()
    turn_over(R.nat_u, R.cot)
    R.wide[...] = jnp.zeros_like(R.wide)
    steps.first_weights()
    normalize_tokens(R.tok, R.gains[:, 0:D], R.a)
    heads_in(R.a, R.nat_q, R.nat_kv, R.cos, R.sin, R.q, R.k, R.v, steps.heads)
    attend_all(R.q, R.k, R.v, R.o, R.lse, steps.forward)
    steps.second_weights()
    feed_forward(R, R.gains[:, D : 2 * D], Drain(R.wide, R.out_sems, out_t))
    steps.after_feed_forward()
    attend_back_all(R, steps.backward)
    heads_out(R)
    steps.after_attention()
    steps.end(lambda: input_gradient(R, R.gains[:, 0:D], Drain(R.wide, R.out_sems, grad_t)))


def local_kernel(tok_t, positions, cot_t, freqs, gains, w_q, w_kv, w_o, w_g, w_u, w_d, *refs):
    out_t, grad_t, g_q, g_kv, g_o, g_g, g_u, g_d, gain_one, gain_two = refs[:10]
    R = layer_refs(refs[11:], refs[10])

    def first_weights():
        R.nat_q[...] = w_q[...]
        R.nat_kv[...] = w_kv[...]
        R.gains[...] = gains[...]

    def second_weights():
        R.nat_o[...] = w_o[...]
        R.nat_g[...] = w_g[...]
        R.nat_u[...] = w_u[...]
        R.nat_d[...] = w_d[...]

    def after_feed_forward():
        down_gradient(R, g_d)
        out_gradient(R, g_o)
        for dest, base in ((g_g, GATE_BASE), (g_u, UP_BASE)):
            for t in range(12):
                dest[:, 128 * t : 128 * (t + 1)] = R.wide[base + t * D : base + (t + 1) * D, :].astype(BF)

    def after_attention():
        first_gradients(R, g_q, g_kv)
        key_gain(R)
        gain_one[...] = R.gain_one[...]
        gain_two[...] = R.gain_two[...]

    steps = types.SimpleNamespace(
        begin=nothing,
        first_weights=first_weights,
        heads=(),
        forward=(),
        second_weights=second_weights,
        after_feed_forward=after_feed_forward,
        backward=(),
        after_attention=after_attention,
        end=lambda last: last(),
    )
    run_layer(R, tok_t, positions, cot_t, freqs, out_t, grad_t, steps)


def hbm():
    return pl.BlockSpec(memory_space=pl.ANY)


def layer_inputs(tokens, positions, cotangent):
    return tokens.T, positions.reshape(-1, 128), cotangent.T, jnp.asarray(frequencies())


def layer(tokens, positions, cotangent, gains, *natural):
    shape = jax.ShapeDtypeStruct
    args = (*layer_inputs(tokens, positions, cotangent), gains, *natural)
    grads = [shape(v.shape, BF) for v in natural]
    outs = pl.pallas_call(
        local_kernel,
        out_shape=(shape((D, SEQ), F32), shape((D, SEQ), F32), *grads, shape((1, D), F32), shape((1, D), F32)),
        in_specs=[hbm(), vmem(), hbm(), vmem()] + [vmem()] * 7,
        out_specs=(hbm(), hbm()) + (vmem(),) * 8,
        scratch_shapes=[pltpu.VMEM((2, 2, 2, 2, 4) + group_shape(("g",)), BF)] + layer_scratch(),
        compiler_params=pltpu.CompilerParams(vmem_limit_bytes=VMEM_LIMIT),
        name="layer",
    )(*args)
    return outs[0].T, outs[1].T, outs[2:8], outs[8], outs[9]


OWNERS = {"q": 20, "kv": 12, "o": 16, "g": 8, "u": 18, "d": 14}
UNIT_NAMES = ("q", "kv", "o", "g", "u", "d")


class Reduce:
    def __init__(self, buf, r1, r2, r3, r4, send, recv, where):
        self.buf, self.r1, self.r2, self.r3, self.r4 = buf, r1, r2, r3, r4
        self.send, self.recv = send, recv
        self.me, (self.z, self.a, self.b, self.c), self.peer_a, self.peer_b, self.sibling, self.along = where

    def copy(self, k):
        if k < 2:
            half = 1 - self.b if k == 0 else self.b
            src, dst, target = self.buf.at[1 - self.c, half], self.r1.at[half], self.sibling
        elif k == 2:
            src, dst, target = self.buf.at[self.c, 1 - self.a], self.r2, self.peer_a
        elif k == 3:
            src, dst, target = self.buf.at[self.c, self.a, 1 - self.b], self.r3, self.peer_b
        else:
            step = k - 3
            src = self.buf.at[self.c, self.a, self.b, lax.rem(self.z + step, 4)]
            dst, target = self.r4.at[step - 1], self.along(step)
        return remote(src, dst, self.send.at[k], self.recv.at[k], target)

    def stage_one(self):
        self.copy(0).start()
        self.copy(1).start()

    def add(self, buf, index, got, count):
        def body(i, _):
            bb, zz = i // 4, lax.rem(i, 4)
            here = index + ((bb, zz) if len(index) == 2 else (zz,))
            there = got[1] + ((bb, zz) if len(index) == 2 else (zz,))
            buf[here] = (buf[here].astype(F32) + got[0][there].astype(F32)).astype(BF)
            return 0

        lax.fori_loop(0, count, body, 0)

    def stage_two(self):
        self.copy(0).wait_recv()
        self.add(self.buf, (self.c, 1 - self.a), (self.r1, (1 - self.a,)), 8)
        self.copy(2).start()
        self.copy(1).wait_recv()
        self.add(self.buf, (self.c, self.a), (self.r1, (self.a,)), 8)

    def stage_three(self):
        self.copy(2).wait_recv()
        self.add(self.buf, (self.c, self.a, 1 - self.b), (self.r2, (1 - self.b,)), 4)
        self.copy(3).start()
        self.add(self.buf, (self.c, self.a, self.b), (self.r2, (self.b,)), 4)

    def stage_four(self):
        self.copy(3).wait_recv()
        self.add(self.buf, (self.c, self.a, self.b), (self.r3, ()), 4)
        for step in (1, 3, 2):
            self.copy(3 + step).start()

    def result(self, total):
        for step in (1, 3, 2):
            self.copy(3 + step).wait_recv()
        own = self.buf[self.c, self.a, self.b, self.z].astype(F32)
        total[...] = (
            own + self.r4[0].astype(F32) + self.r4[1].astype(F32) + self.r4[2].astype(F32)
        )

    def finish(self):
        for k in range(7):
            self.copy(k).wait_send()


def diagonal(n):
    return lax.broadcasted_iota(jnp.int32, (n, n), 0) == lax.broadcasted_iota(jnp.int32, (n, n), 1)


OWN_WIDTH = 1920
NS_BASE = TILES * SEQ


def slab_width(name):
    return 640 if name == "d" else unit_width(name)


def own_width(name):
    return OWN_WIDTH if name == "d" else unit_width(name)


def own_slab_value(name, ref):
    value = ref[...]
    if name == "d":
        return jnp.concatenate([value[:, 640 * k : 640 * (k + 1)] for k in range(3)], axis=0)
    return value


def sum_squares(value):
    return jnp.sum(jnp.sum(value * value, axis=1, keepdims=True), axis=0, keepdims=True)


def on_diagonal(first, rows, n, value):
    row = lax.broadcasted_iota(jnp.int32, (rows, n), 0) + first
    return jnp.where(row == lane((rows, n)), value, 0.0)


def newton_schulz(wide, low, columns, e_ref, r_ref, between=()):
    first, last = columns
    rows = low.shape[0]
    width = last - first
    tiles = (width + 127) // 128
    tall = rows > width
    n = width if tall else rows
    cuts = [(top, min(256, n - top)) for top in range(0, n, 256)]

    def here(t):
        return pl.ds(NS_BASE + t * rows, rows)

    def put(ref, top, p, corner, value):
        ref[top : top + p, top : top + p] = (value[:, 0:p] - jnp.where(diagonal(p), corner, 0.0)).astype(BF)
        if top + p < n:
            beside = value[:, p:].astype(BF)
            ref[top : top + p, top + p : n] = beside
            ref[top + p : n, top : top + p] = beside.T

    total = jnp.zeros((1, 1), F32)
    for t in range(tiles):
        value = low[:, first + 128 * t : first + 128 * (t + 1)].astype(F32)
        wide[here(t), :] = value
        total = total + sum_squares(value)
    scale = 1.0 / (jnp.sqrt(total) + 1e-07)
    for t in range(tiles):
        wide[here(t), :] = wide[here(t), :] * scale

    def step(number, squares):
        for t in range(tiles):
            low[:, first + 128 * t : first + 128 * (t + 1)] = wide[here(t), :].astype(BF)
        state = low[:, first:last]
        mean = squares * (1.0 / n)
        total = jnp.zeros((1, 1), F32)
        for top, p in cuts:
            if tall:
                gram = mm(state[:, top : top + p], state[:, top:], TN)
            else:
                gram = mm(state[top : top + p], state[top:], NT)
            put(e_ref, top, p, mean, gram)
            total = total + sum_squares(gram[:, 0:p] - jnp.where(diagonal(p), mean, 0.0))
            if top + p < n:
                total = total + 2.0 * sum_squares(gram[:, p:])
        more = total * (coef_three / n)
        slope = coef_two + 2.0 * coef_three * mean
        whole = e_ref[0:n, 0:n]
        for top, p in cuts:
            rest = e_ref[top : top + p, 0:n]
            put(r_ref, top, p, more, slope * rest[:, top:].astype(F32) + coef_three * mm(rest, whole[:, top:]))
        keep = coef_one + coef_two * mean + coef_three * mean * mean + more
        poly = r_ref[0:n, 0:n]
        total = jnp.zeros((1, 1), F32)
        for left in range(0, width, 256):
            w = min(256, width - left)
            if tall:
                change = mm(state, poly[:, left : left + w])
            else:
                change = mm(poly, state[:, left : left + w])
            for k in range((w + 127) // 128):
                t = left // 128 + k
                part = change[:, 128 * k : min(128 * (k + 1), w)]
                if part.shape[1] < 128:
                    part = jnp.concatenate([part, jnp.zeros((rows, 128 - part.shape[1]), F32)], axis=1)
                value = keep * wide[here(t), :] + part
                wide[here(t), :] = value
                total = total + sum_squares(value)
        for when, action in enumerate(between):
            pl.when(number == when)(action)
        return total

    lax.fori_loop(0, NS_ITERS, step, total * scale * scale)
    for t in range(tiles):
        low[:, first + 128 * t : first + 128 * (t + 1)] = wide[here(t), :].astype(BF)


def whole_kernel(*refs):
    tok_t, positions, cot_t, freqs = refs[0:4]
    w, gains_ref = refs[4:11], refs[11]
    m, m_gains = refs[12:19], refs[19]
    spread_ref, collect_ref, select_ref, lanes_ref, lanes_back, gain_put = refs[20:26]
    out_t, grad_t = refs[26:28]
    totals = refs[28:33]
    directions = dict(zip(UNIT_NAMES, refs[33:39]))
    k = 39
    bufs, z_buf = group_buffers(refs[k : k + 4]), refs[k + 2]
    r1, r2, r3, r4 = (refs[k + 4 + 5 * j : k + 9 + 5 * j] for j in range(4))
    k += 24
    scr, fold_scr, lane_scr = refs[k : k + 3]
    k += 3
    old = dict(zip(UNIT_NAMES, refs[k : k + 6]))
    mslab = dict(zip(UNIT_NAMES, refs[k + 6 : k + 12]))
    oslab = dict(zip(UNIT_NAMES, refs[k + 12 : k + 18]))
    k += 18
    held = refs[k]
    R = layer_refs(refs[k + 1 : k + 3 + len(LAYER_SCRATCH)], z_buf)
    k += 3 + len(LAYER_SCRATCH)
    ag_send, ag_recv, rs_send, rs_recv, up_send, up_recv, down_send, down_recv = refs[k : k + 8]

    where = coords()
    me, (z, a, b, c), peer_a, peer_b, sibling, along = where
    own = (c, a, b, z)
    natural = {"q": R.nat_q, "kv": R.nat_kv, "o": R.nat_o, "g": R.nat_g, "u": R.nat_u}
    gathers = [Gather(buf, ag_send.at[n], ag_recv.at[n], where) for n, buf in enumerate(bufs)]
    late = gathers[1:]
    sums = [Reduce(bufs[g], r1[g], r2[g], r3[g], r4[g], rs_send.at[g], rs_recv.at[g], where) for g in range(5)]
    QKV, OUT, GATE, UP, DOWN = range(5)

    def pack_group(n):
        for name in GROUPS[n]:
            load_unit(name, w, scr)
            own_gains = None
            if name == "q":
                fold_scr[0:1, 0:128] = jnp.zeros((1, 128), F32)
                fold_scr[0:1, 0:36] = gains_ref[...]
                own_gains = fold_scr[0:1, 0:128]
            pack_slab(name, scr, fold_scr, bufs[n].at[own], unit_offset(name), own_gains)

    def begin():
        barrier = pltpu.get_barrier_semaphore()

        def hello(j, _):
            @pl.when(j != me)
            def _():
                pl.semaphore_signal(barrier, inc=1, device_id=(j,), device_id_type=MESH)

            return 0

        lax.fori_loop(0, 32, hello, 0)
        pack_group(QKV)
        pl.semaphore_wait(barrier, 31)
        gathers[QKV].phase_own()
        for n in (OUT, GATE, UP, DOWN):
            pack_group(n)
            gathers[n].phase_own()
        lane_scr[0:1, :] = jnp.zeros((1, 128), F32)
        lane_scr[0:1, 0:36] = m_gains[...]
        for name in UNIT_NAMES:
            load_unit(name, m, scr)
            pack_slab(name, scr, fold_scr, old[name], 0, lane_scr[0:1, :] if name == "q" else None)

    def first_weights():
        qkv = gathers[QKV]
        qkv.from_z(1, 3, 2)
        qkv.from_b(0, 1, 3, 2)
        qkv.from_a(False, 0, 1, 3, 2)
        qkv.from_a(True, 0, 1, 3, 2)
        for move in late:
            move.from_z(1, 3)
        qkv.phase_sibling()
        for name in GROUPS[QKV]:
            spread(name, bufs[QKV], unit_offset(name), spread_ref, natural[name])
        read_gains(bufs[QKV], select_ref, lanes_ref, R.gains)

    def hook_in():
        for move in late:
            move.from_b(0, 1, 3)

    def hook_one():
        for move in late:
            move.from_z(2)
            move.from_a(False, 0, 1, 3)

    def hook_two():
        for move in late:
            move.from_b(2)
            move.from_a(True, 0, 1, 3)

    def hook_three():
        for move in late:
            move.from_a(False, 2)
            move.from_a(True, 2)

    def second_weights():
        for n in (OUT, GATE, UP):
            gathers[n].phase_sibling()
            for name in GROUPS[n]:
                spread(name, bufs[n], unit_offset(name), spread_ref, natural[name])
        gathers[DOWN].phase_sibling()
        spread_down(bufs[DOWN], R.nat_d)
        for move in gathers:
            move.finish()

    def collect_wide(n, base):
        def read(rows, q, fold):
            tiles = [R.wide[pl.ds(pl.multiple_of(rows + base + (2 * q + s) * D, 16), 144), :] for s in range(2)]
            return jnp.concatenate(tiles, axis=1).astype(BF)

        collect(GROUPS[n][0], read, bufs[n], 0, collect_ref)

    def after_feed_forward():
        down_gradient(R, R.nat_d)
        collect_wide(GATE, GATE_BASE)
        sums[GATE].stage_one()
        collect_wide(UP, UP_BASE)
        sums[UP].stage_one()
        collect_down(R.nat_d, bufs[DOWN])
        sums[GATE].stage_two()
        sums[DOWN].stage_one()
        out_gradient(R, R.nat_o)
        sums[UP].stage_two()
        collect("o", reader(R.nat_o), bufs[OUT], 0, collect_ref)
        sums[OUT].stage_one()
        sums[DOWN].stage_two()

    def to_owner(name):
        number, owner, width = UNIT_NAMES.index(name), OWNERS[name], own_width(name)
        target = held.at[c, a, b, z, :, pl.ds(0, width)]

        @pl.when(me != owner)
        def _():
            remote(mslab[name], target, up_send.at[number], up_recv.at[slot(*own)], owner).start()

        @pl.when(me == owner)
        def _():
            held[c, a, b, z, :, 0:width] = mslab[name][...]

    def settle(n):
        sums[n].result(totals[n])
        for name in GROUPS[n]:
            off = unit_offset(name)
            fresh = (momentum_decay * old[name][...] + totals[n][:, off : off + slab_width(name)]).astype(BF)
            if name == "d":
                for k3 in range(3):
                    mslab[name][:, 640 * k3 : 640 * (k3 + 1)] = fresh[16 * k3 : 16 * (k3 + 1), :]
            else:
                mslab[name][...] = fresh
            to_owner(name)

    def both(one, other):
        def run():
            one()
            other()

        return run

    def after_attention():
        settle(DOWN)
        first_gradients(R, R.nat_o, R.nat_g)
        key_gain(R)
        row = lax.broadcasted_iota(jnp.int32, (32, 2 * D), 0) * 36
        col = lane((32, 2 * D))
        keep = jnp.logical_and(col >= row, col < row + 36)
        both_gains = jnp.concatenate([R.gain_one[...], R.gain_two[...]], axis=1)
        chosen = jnp.where(keep, jnp.broadcast_to(both_gains, (32, 2 * D)), 0.0).astype(BF)
        by_device = mm(chosen, lanes_back[...]).astype(BF)
        collect("kv", reader(R.nat_g), bufs[QKV], unit_offset("kv"), collect_ref)
        collect(
            "q", reader(R.nat_o), bufs[QKV], unit_offset("q"), collect_ref, lambda zz: mm(gain_put[zz], by_device)
        )
        sums[QKV].stage_one()
        settle(OUT)
        sums[QKV].stage_two()

    def arrived(width):
        def one(j, _):
            @pl.when(j != slot(*own))
            def _():
                ref = held.at[j // 16, lax.rem(j // 8, 2), lax.rem(j // 4, 2), lax.rem(j, 4), :, pl.ds(0, width)]
                remote(ref, ref, up_send.at[0], up_recv.at[j], sibling).wait_recv()

            return 0

        lax.fori_loop(0, 32, one, 0)

    def give_plane(name, zz, wait):
        width = own_width(name)

        def one(p, _):
            cc, aa, bb = p // 4, lax.rem(p // 2, 2), lax.rem(p, 2)
            y = aa * (1 - cc) + bb * cc
            x = bb * (1 - cc) + aa * cc
            target = ((zz * 2 + y) * 2 + x) * 2 + cc
            ref = held.at[cc, aa, bb, zz, :, pl.ds(0, width)]
            j = slot(cc, aa, bb, zz)

            @pl.when(j != slot(*own))
            def _():
                copy = remote(ref, oslab[name], down_send.at[j], down_recv.at[UNIT_NAMES.index(name)], target)
                if wait:
                    copy.wait_send()
                else:
                    copy.start()

            return 0

        lax.fori_loop(0, 8, one, 0)

    def give(names):
        def after(zz):
            for name in names:
                pl.when(me == OWNERS[name])(lambda name=name: give_plane(name, zz, False))

        return after

    def give_rest(names):
        for name in names:
            @pl.when(me == OWNERS[name])
            def _(name=name):
                oslab[name][...] = held[c, a, b, z, :, 0 : own_width(name)]

                def plane(zz, _):
                    give_plane(name, zz, True)
                    return 0

                lax.fori_loop(0, 4, plane, 0)

    e_ref, r_ref = R.nat_u.at[:, 0:640], R.nat_u.at[:, 640:1280]

    def is_owner(*names):
        hit = me == OWNERS[names[0]]
        for name in names[1:]:
            hit = jnp.logical_or(hit, me == OWNERS[name])
        return hit

    def end(input_gradients):
        large = is_owner("g", "u", "d")

        def settle_last():
            settle(QKV)

        meanwhile = (sums[QKV].stage_four, settle_last)
        sums[QKV].stage_three()

        @pl.when(jnp.logical_not(large))
        def _():
            sums[QKV].stage_four()
            input_gradients()
            settle_last()

        @pl.when(is_owner("g", "u"))
        def _():
            arrived(own_width("g"))
            spread("g", held, 0, spread_ref, R.nat_g)
            newton_schulz(R.wide, R.nat_g, (0, FF), e_ref, r_ref, meanwhile)
            collect("g", reader(R.nat_g), held, 0, collect_ref, None, give(("g", "u")))

        @pl.when(is_owner("d"))
        def _():
            arrived(own_width("d"))
            spread_own_down(held, R.nat_d)
            newton_schulz(R.wide, R.nat_d, (0, D), e_ref, r_ref, meanwhile)
            collect_own_down(R.nat_d, held)
            for zz in range(4):
                give_plane("d", zz, False)

        @pl.when(large)
        def _():
            input_gradients()
            give_rest(("g", "u", "d"))

        @pl.when(is_owner("q", "o"))
        def _():
            arrived(own_width("q"))
            spread("q", held, 0, spread_ref, R.nat_q)
            rows_of = gain_rows(held[:, :, :, :, :, 640:768].reshape(512, 128), select_ref)
            squares = jnp.sum(rows_of * rows_of, axis=1, keepdims=True)
            scales = [
                lax.rsqrt(jnp.sum(squares[16 * h : 16 * h + 16], axis=0, keepdims=True) * (1.0 / D) + 1e-06)
                for h in range(2)
            ]
            newton_schulz(R.wide, R.nat_q, (0, 640), e_ref, r_ref)

            def scale_extra(zz):
                scale = jnp.where(zz < 2, scales[0], scales[1])
                high = scale.astype(BF).astype(F32)
                row16 = lax.rem(lax.broadcasted_iota(jnp.int32, (128, 128), 0), 16)
                return jnp.where(row16 == 7, high, 0.0) + jnp.where(row16 == 15, scale - high, 0.0)

            collect("q", reader(R.nat_q), held, 0, collect_ref, scale_extra, give(("q", "o")))
            give_rest(("q", "o"))

        @pl.when(is_owner("kv"))
        def _():
            arrived(own_width("kv"))
            spread("kv", held, 0, spread_ref, R.nat_kv)
            newton_schulz(R.wide, R.nat_kv, (0, KVD), e_ref, r_ref)
            newton_schulz(R.wide, R.nat_kv, (256, 256 + KVD), e_ref, r_ref)
            collect("kv", reader(R.nat_kv), held, 0, collect_ref, None, give(("kv",)))
            give_rest(("kv",))

        for name in ("d", "g", "u", "o", "kv", "q"):
            number = UNIT_NAMES.index(name)

            @pl.when(me != OWNERS[name])
            def _():
                remote(oslab[name], oslab[name], down_send.at[0], down_recv.at[number], sibling).wait_recv()

            directions[name][...] = oslab[name][...]

        for name in UNIT_NAMES:
            number = UNIT_NAMES.index(name)
            target = held.at[c, a, b, z, :, pl.ds(0, own_width(name))]

            @pl.when(me != OWNERS[name])
            def _():
                remote(mslab[name], target, up_send.at[number], up_recv.at[slot(*own)], OWNERS[name]).wait_send()

        for move in sums:
            move.finish()

    steps = types.SimpleNamespace(
        begin=begin,
        first_weights=first_weights,
        heads=(nothing, nothing, nothing, hook_in),
        forward=(hook_one, hook_two, hook_three),
        second_weights=second_weights,
        after_feed_forward=after_feed_forward,
        backward=(
            both(sums[OUT].stage_two, sums[GATE].stage_three),
            None,
            sums[UP].stage_three,
            sums[GATE].stage_four,
            sums[DOWN].stage_three,
            both(sums[UP].stage_four, sums[OUT].stage_three),
            lambda: settle(GATE),
            sums[DOWN].stage_four,
            both(lambda: settle(UP), sums[OUT].stage_four),
        ),
        after_attention=after_attention,
        end=end,
    )
    run_layer(R, tok_t, positions, cot_t, freqs, out_t, grad_t, steps)


def collect_constants():
    forward = spread_matrices()
    put = np.zeros((4, 128, 32), np.float32)
    for zz in range(4):
        for d in range(8):
            put[zz, 16 * place_of(d) + 7, 8 * zz + d] = 1
    low = ml_dtypes.bfloat16
    return (
        forward.astype(low),
        forward.transpose(0, 2, 1).astype(low),
        gain_select().astype(low),
        gain_lanes().astype(low),
        gain_lanes().T.astype(low),
        put.astype(low),
    )


def whole_call(tokens, positions, cotangent, w, gains, m, m_gains):
    shape = jax.ShapeDtypeStruct
    args = (*layer_inputs(tokens, positions, cotangent), *w, gains, *m, m_gains, *collect_constants())
    stages = []
    for lead in ((2, 2, 4), (2, 4), (4,), (3,)):
        stages += [pltpu.VMEM(lead + group_shape(group), BF) for group in GROUPS]
    travel = [pltpu.VMEM((16, own_width(n)), BF) for n in UNIT_NAMES]
    outs = (
        [shape((D, SEQ), F32)] * 2
        + [shape(group_shape(group), F32) for group in GROUPS]
        + [shape((16, own_width(n)), BF) for n in UNIT_NAMES]
    )
    return pl.pallas_call(
        whole_kernel,
        out_shape=tuple(outs),
        in_specs=[hbm(), vmem(), hbm()] + [vmem()] * (len(args) - 3),
        out_specs=(hbm(), hbm()) + (vmem(),) * 11,
        scratch_shapes=slab_buffers()
        + stages
        + [pltpu.VMEM((12, 48, 128), F32), pltpu.VMEM((16, 256), F32), pltpu.VMEM((8, 128), F32)]
        + [pltpu.VMEM((ROWS_D, 640) if n == "d" else (16, unit_width(n)), F32) for n in UNIT_NAMES]
        + travel
        + travel
        + [pltpu.VMEM((2, 2, 2, 4, 16, OWN_WIDTH), BF)]
        + layer_scratch()
        + [
            pltpu.SemaphoreType.DMA((5, 31)),
            pltpu.SemaphoreType.DMA((5, 32)),
            pltpu.SemaphoreType.DMA((5, 7)),
            pltpu.SemaphoreType.DMA((5, 7)),
            pltpu.SemaphoreType.DMA((6,)),
            pltpu.SemaphoreType.DMA((32,)),
            pltpu.SemaphoreType.DMA((32,)),
            pltpu.SemaphoreType.DMA((6,)),
        ],
        compiler_params=pltpu.CompilerParams(
            collective_id=0, has_side_effects=True, vmem_limit_bytes=VMEM_LIMIT
        ),
        name="layer_and_step",
    )(*args)


def finish_kernel(*refs):
    large = refs[0:2]
    totals = refs[2:7]
    directions = dict(zip(UNIT_NAMES, refs[7:13]))
    w, gains = refs[13:20], refs[20]
    m, m_gains = refs[21:28], refs[28]
    large_out = refs[29:31]
    grad_out, grad_gains = refs[31:38], refs[38]
    new_m, new_m_gains = refs[39:46], refs[46]
    new_w, new_gains = refs[47:54], refs[54]
    scr, fold_scr, through, sems = refs[55:59]
    shapes = matrix_shapes()
    arrivals = [pltpu.make_async_copy(large[k], through.at[k], sems.at[0, k]) for k in range(2)]
    departures = [pltpu.make_async_copy(through.at[k], large_out[k], sems.at[1, k]) for k in range(2)]
    for copy in arrivals:
        copy.start()
    for n, (group, total) in enumerate(zip(GROUPS, totals)):
        if n == 3:
            for arrival, departure in zip(arrivals, departures):
                arrival.wait()
                departure.start()
        for name in group:
            off = unit_offset(name)
            unpack_slab(name, total[:, off : off + slab_width(name)], scr, fold_scr)
            for index, tile, tiles2, rows in PARTS[name]:
                store_rows(scr, grad_out[index], rows, tiles2, tile)
                new_m[index][...] = momentum_decay * m[index][...] + grad_out[index][...]
            if name == "q":
                grad_gains[...] = fold_scr[7:8, 0:36]
                new_m_gains[...] = momentum_decay * m_gains[...] + grad_gains[...]
            unpack_slab(name, own_slab_value(name, directions[name]).astype(F32), scr, fold_scr)
            for index, tile, tiles2, rows in PARTS[name]:
                store_rows(scr, new_w[index], rows, tiles2, tile)
                rate = 0.2 * math.sqrt(max(shapes[index]))
                old = w[index][...]
                new_w[index][...] = old - matrix_rate * (weight_decay * old + rate * new_w[index][...])
            if name == "q":
                scale = fold_scr[7:8, 0:36] + fold_scr[15:16, 0:36]
                new_gains[...] = gains[...] - gain_rate * (new_m_gains[...] * scale)
    for copy in departures:
        copy.wait()


def finish_call(large, slabs, w, gains, m, m_gains):
    shape = jax.ShapeDtypeStruct
    outs = [shape(v.shape, F32) for v in large] + [shape(v.shape, F32) for v in (*w, gains)] * 3
    args = (*large, *slabs, *w, gains, *m, m_gains)
    return pl.pallas_call(
        finish_kernel,
        out_shape=tuple(outs),
        in_specs=[hbm()] * 2 + [vmem()] * (len(args) - 2),
        out_specs=(hbm(), hbm()) + (vmem(),) * 24,
        scratch_shapes=[
            pltpu.VMEM((12, 48, 128), F32),
            pltpu.VMEM((16, 256), F32),
            pltpu.VMEM((2, D, SEQ), F32),
            pltpu.SemaphoreType.DMA((2, 2)),
        ],
        compiler_params=pltpu.CompilerParams(vmem_limit_bytes=VMEM_LIMIT),
        name="finish",
    )(*args)


def orthogonal(matrix):
    rows, cols = matrix.shape
    wide = matrix.T if rows > cols else matrix
    state = wide / (jnp.sqrt(jnp.sum(wide * wide)) + 1e-07)
    for turn_number in range(NS_ITERS):
        gram = jnp.dot(state, state.T, precision=precise)
        poly = coef_two * gram + coef_three * jnp.dot(gram, gram, precision=precise)
        state = coef_one * state + jnp.dot(poly, state, precision=precise)
    return state.T if rows > cols else state


def direction_of(index, flat):
    if index < 7:
        return orthogonal(flat.reshape(matrix_shapes()[index])).reshape(-1)
    halves = flat.reshape(2, D)
    return (halves * lax.rsqrt(jnp.mean(halves * halves, axis=1, keepdims=True) + 1e-06)).reshape(-1)


def gather_all(flat):
    return lax.all_gather(flat.astype(BF), "dp", axis=0, tiled=True)


def scatter_sum(whole):
    return lax.psum_scatter(whole, "dp", scatter_dimension=0, tiled=True)


def pad_columns(matrix, width):
    return jnp.pad(matrix, ((0, 0), (0, width - matrix.shape[1])))


def per_device(tokens, positions, cotangent, *rest):
    w, gains, m, m_gains = rest[0:7], rest[7], rest[8:15], rest[15]
    shapes = matrix_shapes()
    whole = [gather_all(v).reshape(s) for v, s in zip(w, shapes)]
    padded = (
        pad_columns(whole[0], 640),
        jnp.concatenate([pad_columns(whole[1], 256), pad_columns(whole[2], 256)], axis=1),
        pad_columns(whole[3], 640),
        whole[4],
        whole[5],
        pad_columns(whole[6], 640),
    )
    block_out, input_grad, grads, *gain_grads = layer(
        tokens, positions, cotangent, gather_all(gains).astype(F32).reshape(1, -1), *padded
    )
    parts = (
        grads[0][:, :D],
        grads[1][:, :KVD],
        grads[1][:, 256 : 256 + KVD],
        grads[2][:, :D],
        grads[3],
        grads[4],
        grads[5][:, :D],
    )
    shares = [scatter_sum(g.astype(F32).reshape(-1)) for g in parts] + [scatter_sum(jnp.concatenate(gain_grads, axis=1).reshape(-1))]
    moments = [momentum_decay * old + share for old, share in zip((*m, m_gains), shares)]
    device = lax.axis_index("dp")
    stride = lax.axis_size("dp") // 8
    pieces = []
    for i in range(8):
        full = gather_all(moments[i]).astype(F32)
        found = lax.cond(
            device == i * stride, lambda v, i=i: direction_of(i, v), jnp.zeros_like, full
        )
        pieces.append(scatter_sum(found))
    updated = []
    for i in range(7):
        scale = 0.2 * math.sqrt(max(shapes[i]))
        updated.append(w[i] - matrix_rate * (weight_decay * w[i] + scale * pieces[i]))
    new_gains = gains - gain_rate * pieces[7]
    return (block_out, input_grad, *moments, *updated, new_gains, *shares)


def per_device_32(tokens, positions, cotangent, *rest):
    w, gains, m, m_gains = rest[0:7], rest[7], rest[8:15], rest[15]
    w = [v.reshape(-1, 128) for v in w]
    m = [v.reshape(-1, 128) for v in m]
    gains, m_gains = gains.reshape(1, -1), m_gains.reshape(1, -1)
    out_t, grad_t, *slabs = whole_call(tokens, positions, cotangent, w, gains, m, m_gains)
    out_t, grad_t, *flat = finish_call((out_t, grad_t), slabs, w, gains, m, m_gains)
    flat = [v.reshape(-1) for v in flat]
    return (out_t.T, grad_t.T, *flat[8:16], *flat[16:24], *flat[0:8])


def solution(mesh):
    placed = (P("dp", None), P("dp"), P("dp", None)) + (P("dp"),) * 16
    return jax.shard_map(
        per_device_32 if mesh.shape["dp"] == 32 else per_device,
        mesh=mesh,
        in_specs=placed,
        out_specs=(P("dp", None), P("dp", None)) + (P("dp"),) * 24,
        check_vma=False,
    )
```

```python
import math
import types

import jax
import jax.numpy as jnp
import ml_dtypes
import numpy as np
from jax import lax
from jax.experimental import pallas as pl
from jax.experimental.pallas import tpu as pltpu
from jax.sharding import PartitionSpec as P

HEADS = 9
KV_HEADS = 3
HEAD_DIM = 64
D = 576
KVD = 192
FF = 1536
SEQ = 1024
NS_ITERS = 5


eps_norm = 1e-05
rope_base = 100000.0
momentum_decay = 0.95
matrix_rate = 0.1
weight_decay = 0.1
gain_rate = 0.25
coef_one = 3.4445
coef_two = -4.775
coef_three = 2.0315
precise = lax.Precision.HIGHEST
BF = jnp.bfloat16
F32 = jnp.float32
MESH = pl.DeviceIdType.MESH
VMEM_LIMIT = 63 * 2**20


def matrix_shapes():
    return ((D, D), (D, KVD), (D, KVD), (D, D), (D, FF), (D, FF), (FF, D))


UNITS = {
    "q": (640, 128, 5),
    "kv": (512, 128, 4),
    "o": (640, 128, 5),
    "g": (1536, 256, 6),
    "u": (1536, 256, 6),
}
GROUPS = (("q", "kv"), ("o",), ("g",), ("u",), ("d",))
ROWS_D = 48


def unit_width(name):
    return UNITS[name][0] + UNITS[name][1]


def group_shape(group):
    if group == ("d",):
        return (ROWS_D, 640)
    return (16, sum(unit_width(u) for u in group))


def unit_offset(name):
    for group in GROUPS:
        off = 0
        for u in group:
            if u == name:
                return off
            off += unit_width(u)
    raise KeyError(name)


def place_of(d):
    y, x, c = d // 4, (d // 2) % 2, d % 2
    return c * 4 + (y * 2 + x if c == 0 else x * 2 + y)


def spread_matrices():
    out = np.zeros((6, 144, 256), np.float32)
    for q in range(6):
        for d in range(8):
            p = place_of(d)
            for r in range(16):
                out[q, 18 * d + r, 16 * p + r] = 1
            for e in range(2):
                out[q, 18 * d + 16 + e, 128 + 16 * p + 8 * e + q] = 1
    return out


def gain_select():
    out = np.zeros((32, 512), np.float32)
    for i in range(32):
        z, d = i // 8, i % 8
        out[i, (place_of(d) * 4 + z) * 16 + 7] = 1
    return out


def gain_lanes():
    out = np.zeros((128, 2 * D), np.float32)
    for j in range(2 * D):
        out[j % 36, j] = 1
    return out


def coords():
    me = lax.axis_index("dp")
    z, y, x, c = me // 8, lax.rem(me // 4, 2), lax.rem(me // 2, 2), lax.rem(me, 2)
    a = y * (1 - c) + x * c
    b = x * (1 - c) + y * c

    def dev(zz, yy, xx, cc):
        return ((zz * 2 + yy) * 2 + xx) * 2 + cc

    peer_b = dev(z, y + (1 - 2 * y) * c, x + (1 - 2 * x) * (1 - c), c)
    peer_a = dev(z, y + (1 - 2 * y) * (1 - c), x + (1 - 2 * x) * c, c)
    sibling = dev(z, y, x, 1 - c)

    def along(step):
        return dev(lax.rem(z + step, 4), y, x, c)

    return me, (z, a, b, c), peer_a, peer_b, sibling, along


def remote(src, dst, send, recv, target):
    return pltpu.make_async_remote_copy(
        src_ref=src, dst_ref=dst, send_sem=send, recv_sem=recv, device_id=(target,), device_id_type=MESH
    )


def slot(c, a, b, z):
    return ((c * 2 + a) * 2 + b) * 4 + z


class Gather:
    def __init__(self, buf, send, recv, where):
        self.buf, self.send, self.recv = buf, send, recv
        self.me, (self.z, self.a, self.b, self.c), self.peer_a, self.peer_b, self.sibling, self.along = where
        self.count = 0

    def push(self, index, target):
        ref = self.buf.at[index]
        copy = remote(ref, ref, self.send.at[self.count], self.recv.at[slot(*index)], target)
        copy.start()
        self.count += 1

    def arrive(self, index):
        ref = self.buf.at[index]
        remote(ref, ref, self.send.at[0], self.recv.at[slot(*index)], self.sibling).wait_recv()

    def phase_own(self):
        own = (self.c, self.a, self.b, self.z)
        for step in (1, 3, 2):
            self.push(own, self.along(step))
        self.push(own, self.peer_b)
        self.push(own, self.peer_a)
        self.push(own, self.sibling)

    def from_z(self, *steps):
        for step in steps:
            index = (self.c, self.a, self.b, lax.rem(self.z + step, 4))
            self.arrive(index)
            self.push(index, self.peer_b)
            self.push(index, self.peer_a)
            self.push(index, self.sibling)

    def from_b(self, *steps):
        for step in steps:
            index = (self.c, self.a, 1 - self.b, lax.rem(self.z + step, 4))
            self.arrive(index)
            self.push(index, self.peer_a)
            self.push(index, self.sibling)

    def from_a(self, other, *steps):
        for step in steps:
            index = (self.c, 1 - self.a, 1 - self.b if other else self.b, lax.rem(self.z + step, 4))
            self.arrive(index)
            self.push(index, self.sibling)

    def phase_sibling(self):
        for aa in range(2):
            for bb in range(2):
                for zz in range(4):
                    self.arrive((1 - self.c, aa, bb, zz))

    def finish(self):
        own = (self.c, self.a, self.b, self.z)
        ref = self.buf.at[own]
        for n in range(self.count):
            remote(ref, ref, self.send.at[n], self.recv.at[slot(*own)], self.sibling).wait_send()


def low_lanes(rows):
    return lax.broadcasted_iota(jnp.int32, (rows, 128), 1) < 64


def turn(v):
    return pltpu.roll(v, 64, axis=1)


def load_rows(flat, scr, rows, tiles2):
    if tiles2 % 2 == 0:
        nt = tiles2 // 2
        for t in range(nt):
            scr[t, 0:rows, :] = flat[pl.ds(t, rows, stride=nt), :]
        return
    half, h = rows // 2, (tiles2 - 1) // 2
    low = low_lanes(half)
    pair = [flat[pl.ds(t, half, stride=tiles2), :] for t in range(tiles2)]
    turned = {t: turn(pair[t]) for t in range(h, tiles2)}
    for j in range(h + 1):
        even = pair[j] if j < h else jnp.where(low, pair[h], 0.0)
        odd = jnp.where(low, turned[h + j], turned[h + j + 1] if j < h else 0.0)
        scr[j, pl.ds(0, half, stride=2), :] = even
        scr[j, pl.ds(1, half, stride=2), :] = odd


def store_rows(scr, flat, rows, tiles2, base=0):
    if tiles2 % 2 == 0:
        nt = tiles2 // 2
        for t in range(nt):
            flat[pl.ds(t, rows, stride=nt), :] = scr[base + t, 0:rows, :]
        return
    half, h = rows // 2, (tiles2 - 1) // 2
    low = low_lanes(half)
    even = [scr[base + j, pl.ds(0, half, stride=2), :] for j in range(h + 1)]
    odd = [turn(scr[base + j, pl.ds(1, half, stride=2), :]) for j in range(h + 1)]
    for t in range(tiles2):
        if t < h:
            value = even[t]
        elif t == h:
            value = jnp.where(low, even[h], odd[0])
        else:
            value = jnp.where(low, odd[t - h - 1], odd[t - h])
        flat[pl.ds(t, half, stride=tiles2), :] = value


PARTS = {
    "q": ((0, 0, 9, 18),),
    "kv": ((1, 0, 3, 18), (2, 2, 3, 18)),
    "o": ((3, 0, 9, 18),),
    "g": ((4, 0, 24, 18),),
    "u": ((5, 0, 24, 18),),
    "d": ((6, 0, 9, 48),),
}


def pack_slab(name, scr, fold_scr, slab, off, gains=None):
    if name == "d":
        for t in range(5):
            slab[:, off + 128 * t : off + 128 * (t + 1)] = scr[t, 0:48, :].astype(slab.dtype)
        return
    padded, fold, chunks = UNITS[name]
    for t in range(padded // 128):
        slab[:, off + 128 * t : off + 128 * (t + 1)] = scr[t, 0:16, :].astype(slab.dtype)
    fold_scr[...] = jnp.zeros_like(fold_scr)
    per = fold // 128
    for q in range(chunks):
        for k in range(per):
            for e in range(2):
                fold_scr[e * 8 + q : e * 8 + q + 1, 128 * k : 128 * (k + 1)] = scr[q * per + k, 16 + e : 17 + e, :]
    if gains is not None:
        fold_scr[7:8, 0:128] = gains
    slab[:, off + padded : off + padded + fold] = fold_scr[:, 0:fold].astype(slab.dtype)


def unpack_slab(name, main, scr, fold_scr):
    if name == "d":
        for t in range(5):
            scr[t, 0:48, :] = main[:, 128 * t : 128 * (t + 1)]
        return
    padded, fold, chunks = UNITS[name]
    for t in range(padded // 128):
        scr[t, 0:16, :] = main[:, 128 * t : 128 * (t + 1)]
    fold_scr[:, 0:fold] = main[:, padded : padded + fold]
    per = fold // 128
    for q in range(chunks):
        for k in range(per):
            for e in range(2):
                scr[q * per + k, 16 + e : 17 + e, :] = fold_scr[e * 8 + q : e * 8 + q + 1, 128 * k : 128 * (k + 1)]


def spread(name, buf, off, spread_ref, dest):
    padded, fold, chunks = UNITS[name]

    def plane(z, _):
        folded = buf[:, :, :, z, :, off + padded : off + padded + fold].reshape(128, fold)
        for q in range(chunks):
            main = buf[:, :, :, z, :, off + q * fold : off + (q + 1) * fold].reshape(128, fold)
            both = jnp.concatenate([main, folded], axis=0)
            block = jnp.dot(spread_ref[q], both, preferred_element_type=F32)
            dest[pl.ds(pl.multiple_of(z * 144, 16), 144), q * fold : (q + 1) * fold] = block.astype(dest.dtype)
        return 0

    lax.fori_loop(0, 4, plane, 0)


def spread_down(buf, dest):
    for z in range(4):
        for d in range(8):
            y, x, c = d // 4, (d // 2) % 2, d % 2
            a, b = (y, x) if c == 0 else (x, y)
            dest[(z * 8 + d) * 48 : (z * 8 + d + 1) * 48, :] = buf[c, a, b, z].astype(dest.dtype)


def reader(source):
    return lambda first, q, fold: source[pl.ds(first, 144), q * fold : (q + 1) * fold].astype(BF)


def collect(name, read, buf, off, collect_ref, extra=None, after=None, order=None):
    padded, fold, chunks = UNITS[name]

    def plane(z, _):
        if order is not None:
            z = order(z)
        first = pl.multiple_of(z * 144, 16)
        total = jnp.zeros((128, fold), F32)
        for q in range(chunks):
            both = jnp.dot(collect_ref[q], read(first, q, fold), preferred_element_type=F32)
            buf[:, :, :, z, :, off + q * fold : off + (q + 1) * fold] = (
                both[0:128].astype(BF).reshape(2, 2, 2, 16, fold)
            )
            total = total + both[128:256]
        if extra is not None:
            total = total + extra(z)
        buf[:, :, :, z, :, off + padded : off + padded + fold] = total.astype(BF).reshape(2, 2, 2, 16, fold)
        if after is not None:
            after(z)
        return 0

    lax.fori_loop(0, 4, plane, 0)


def collect_down(source, buf):
    for z in range(4):
        for d in range(8):
            y, x, c = d // 4, (d // 2) % 2, d % 2
            a, b = (y, x) if c == 0 else (x, y)
            buf[c, a, b, z] = source[(z * 8 + d) * 48 : (z * 8 + d + 1) * 48, :].astype(BF)


def spread_own_down(buf, dest):
    for z in range(4):
        for d in range(8):
            y, x, c = d // 4, (d // 2) % 2, d % 2
            a, b = (y, x) if c == 0 else (x, y)
            for k in range(3):
                first = (z * 8 + d) * 48 + 16 * k
                dest[first : first + 16, :] = buf[c, a, b, z, :, 640 * k : 640 * (k + 1)]


def collect_own_down(source, buf):
    for z in range(4):
        for d in range(8):
            y, x, c = d // 4, (d // 2) % 2, d % 2
            a, b = (y, x) if c == 0 else (x, y)
            for k in range(3):
                first = (z * 8 + d) * 48 + 16 * k
                buf[c, a, b, z, :, 640 * k : 640 * (k + 1)] = source[first : first + 16, :]


def load_unit(name, flats, scr):
    for index, tile, tiles2, rows in PARTS[name]:
        view = scr if tile == 0 else scr.at[pl.ds(tile, (tiles2 + 1) // 2)]
        load_rows(flats[index], view, rows, tiles2)


def read_gains(buf, select_ref, lanes_ref, gains_out):
    rows = gain_rows(buf[:, :, :, :, :, 640:768].reshape(512, 128), select_ref)
    wide = jnp.dot(rows.astype(BF), lanes_ref[...], preferred_element_type=F32)
    device = lax.broadcasted_iota(jnp.int32, wide.shape, 0)
    column = lax.broadcasted_iota(jnp.int32, wide.shape, 1)
    low = device * 36
    keep = jnp.logical_and(column >= low, column < low + 36)
    gains_out[...] = jnp.sum(jnp.where(keep, wide, 0.0), axis=0, keepdims=True)


def gain_rows(folds, select_ref):
    return jnp.dot(select_ref[...], folds, preferred_element_type=F32)


def vmem():
    return pl.BlockSpec(memory_space=pltpu.VMEM)


def slab_buffers():
    lead = (2, 2, 2, 4)
    shapes = [lead + group_shape(group) for group in GROUPS]
    return [pltpu.VMEM(s, BF) for s in (shapes[0], shapes[1], (2,) + shapes[2], shapes[4])]


def group_buffers(refs):
    return (refs[0], refs[1], refs[2].at[0], refs[2].at[1], refs[3])


NN = (((1,), (0,)), ((), ()))
NT = (((1,), (1,)), ((), ()))
TN = (((0,), (0,)), ((), ()))
TILES = 5
BLOCK = 256
LOG2E = 1.4426950408889634


def mm(left, right, dims=NN):
    return lax.dot_general(left, right, dims, preferred_element_type=F32)


def block_rows(i, size=BLOCK):
    return pl.ds(pl.multiple_of(i * size, size), size)


def frequencies():
    half = HEAD_DIM // 2
    freqs = rope_base ** (-np.arange(half) * 2.0 / HEAD_DIM)
    return np.tile(freqs.astype(np.float32), 4).reshape(1, 128)


def lane(shape):
    return lax.broadcasted_iota(jnp.int32, shape, len(shape) - 1)


def cos_sin(angle):
    turns = jnp.floor(angle * 0.6366197723675814 + 0.5)
    rest = ((angle - turns * 1.5703125) - turns * 4.837512969970703e-4) - turns * 7.549789948768648e-8
    square = rest * rest
    sine = rest + rest * square * (
        -1.6666654611e-1 + square * (8.3321608736e-3 + square * -1.9515295891e-4)
    )
    cosine = (1.0 - 0.5 * square) + square * square * (
        4.166664568298827e-2 + square * (-1.388731625493765e-3 + square * 2.443315711809948e-5)
    )
    quarter = turns - 4.0 * jnp.floor(turns * 0.25)
    odd = jnp.logical_or(quarter == 1.0, quarter == 3.0)
    swapped_cos = jnp.where(odd, sine, cosine)
    swapped_sin = jnp.where(odd, cosine, sine)
    cos_sign = jnp.logical_or(quarter == 1.0, quarter == 2.0)
    return (
        jnp.where(cos_sign, -swapped_cos, swapped_cos),
        jnp.where(quarter >= 2.0, -swapped_sin, swapped_sin),
    )


def make_tables(positions, freqs, cos_ref, sin_ref):
    for r in range(SEQ // 128):
        row = jnp.broadcast_to(positions[r : r + 1, :].astype(F32), (128, 128))
        column = jnp.sum(jnp.where(diagonal(128), row, 0.0), axis=1, keepdims=True)
        cosine, sine = cos_sin(column * freqs[...])
        cos_ref[128 * r : 128 * (r + 1), :] = cosine
        sin_ref[128 * r : 128 * (r + 1), :] = jnp.where(lax.rem(lane((128, 128)), 64) < 32, -sine, sine)


def rotate_tile(value, cosine, sine, inverse=False):
    first = lax.rem(lane(value.shape), 64) < 32
    swapped = jnp.where(first, pltpu.roll(value, 96, axis=1), pltpu.roll(value, 32, axis=1))
    if inverse:
        return value * cosine - swapped * sine
    return value * cosine + swapped * sine


def row_scale(value):
    return lax.rsqrt(jnp.sum(value * value, axis=1, keepdims=True) * (1.0 / D) + eps_norm)


def turn_over(source, dest):
    def body(i, _):
        rows = block_rows(i)
        dest[rows, :] = source[:, rows].T
        return 0

    lax.fori_loop(0, SEQ // BLOCK, body, 0)


def normalize_tokens(tokens, gain, a_ref):
    def body(i, _):
        rows = block_rows(i)
        x = tokens[rows, :].astype(F32)
        a_ref[rows, :] = (x * row_scale(x) * gain).astype(BF)
        return 0

    lax.fori_loop(0, SEQ // BLOCK, body, 0)


def heads_in(a_ref, w_q, w_kv, cos_ref, sin_ref, q_ref, k_ref, v_ref, between=()):
    def body(i, _):
        rows = block_rows(i)
        a = a_ref[rows, :]
        cosine, sine = cos_ref[rows, :], sin_ref[rows, :]
        pq = mm(a, w_q[...])
        for t in range(TILES):
            turned = rotate_tile(pq[:, 128 * t : 128 * (t + 1)], cosine, sine).astype(BF)
            q_ref[t, rows, :] = turned * jnp.asarray(HEAD_DIM ** (-0.5), BF)
        pkv = mm(a, w_kv[...])
        low = lane((BLOCK, 128)) < 64
        for ref, base, rotary in ((k_ref, 0, True), (v_ref, 256, False)):
            for half in range(2):
                tile = pkv[:, base + 128 * half : base + 128 * (half + 1)]
                if rotary:
                    tile = rotate_tile(tile, cosine, sine)
                other = turn(tile)
                ref[2 * half, rows, :] = jnp.where(low, tile, other).astype(BF)
                if half == 0:
                    ref[1, rows, :] = jnp.where(low, other, tile).astype(BF)
        for number, action in enumerate(between):
            pl.when(i == number)(action)
        return 0

    lax.fori_loop(0, SEQ // BLOCK, body, 0)


def own_lanes(value, parity):
    here = lane(value.shape) // 64 == parity
    return jnp.where(here, value, jnp.zeros_like(value))


def attend_group(g, q_ref, k_ref, v_ref, o_ref, lse_ref):
    for h in range(HEADS // KV_HEADS):
        j = 3 * g + h
        t, parity = j // 2, lax.rem(j, 2)
        for i in range(SEQ // BLOCK):
            end = BLOCK * (i + 1)
            query = q_ref[t, BLOCK * i : end, :]
            s = mm(own_lanes(k_ref[g, 0:end, :], parity), query, NT)
            rows = lax.broadcasted_iota(jnp.int32, (BLOCK, BLOCK), 0)
            cols = lax.broadcasted_iota(jnp.int32, (BLOCK, BLOCK), 1)
            corner = jnp.where(cols >= rows, s[BLOCK * i :, :], -1e30)
            s = jnp.concatenate([s[: BLOCK * i, :], corner], axis=0) if i else corner
            top = jnp.max(s, axis=0, keepdims=True)
            weights = jnp.exp2((s - top) * LOG2E)
            total = jnp.sum(weights, axis=0, keepdims=True)
            probs = (weights * (1.0 / total)).astype(BF)
            out = mm(probs, own_lanes(v_ref[g, 0:end, :], parity), TN)
            o_ref[t, BLOCK * i : end, :] += out.astype(BF)
            lse_ref[j, :, BLOCK * i : end] = top * LOG2E + jnp.log2(total)


def attend_all(q_ref, k_ref, v_ref, o_ref, lse_ref, between=()):
    o_ref[...] = jnp.zeros_like(o_ref)

    def body(g, _):
        attend_group(g, q_ref, k_ref, v_ref, o_ref, lse_ref)
        for number, action in enumerate(between):
            pl.when(g == number)(action)
        return 0

    lax.fori_loop(0, KV_HEADS, body, 0)


DK_BASE = TILES * SEQ
DV_BASE = DK_BASE + 2 * KV_HEADS * SEQ
WIDE_ROWS = DV_BASE + 2 * KV_HEADS * SEQ
GATE_BASE = 0
UP_BASE = 12 * D


def read_z(z_buf, first, count):
    blocks = []
    for i in range(SEQ // BLOCK):
        blocks.append(z_buf[i // 2, i % 2, :, :, :, :, first : first + count].reshape(BLOCK, count))
    return jnp.concatenate(blocks, axis=0)


STAGE_BASE = UP_BASE + 12 * D


class Drain:
    def __init__(self, wide, sems, result):
        self.wide, self.sems, self.result = wide, sems, result

    def rows(self, number, half):
        return pl.ds(pl.multiple_of(STAGE_BASE + (2 * number + half) * D, 8), D)

    def copy(self, i, number, half):
        columns = pl.ds(pl.multiple_of(i * BLOCK + 128 * half, 128), 128)
        return pltpu.make_async_copy(
            self.wide.at[self.rows(number, half)], self.result.at[:, columns], self.sems.at[number, half]
        )

    def put(self, i, value):
        number = lax.rem(i, 2)

        @pl.when(i >= 2)
        def _():
            for half in range(2):
                self.copy(i, number, half).wait()

        for half in range(2):
            self.wide[self.rows(number, half), :] = value[:, 128 * half : 128 * (half + 1)]
            self.copy(i, number, half).start()

    def finish(self):
        for number in range(2):
            for half in range(2):
                self.copy(number, number, half).wait()


def feed_forward(R, gain, drain):
    w_o, w_g, w_u, w_d = R.nat_o, R.nat_g, R.nat_u, R.nat_d
    R.gain_two[...] = jnp.zeros_like(R.gain_two)

    def body(i, _):
        rows = block_rows(i)
        o = jnp.concatenate([R.o[t, rows, :] for t in range(TILES)], axis=1)
        x2 = R.tok[rows, :].astype(F32) + mm(o[:, 0:D], w_o[:, 0:D])
        r2 = row_scale(x2)
        n2 = x2 * r2
        h = (n2 * gain).astype(BF)
        c = R.cot[rows, :]
        gate = mm(h, w_g[...])
        upper = mm(h, w_u[...])
        grad = mm(c, w_d[:, 0:D], NT)
        sigma = 0.5 * jnp.tanh(0.5 * gate) + 0.5
        silu = gate * sigma
        z = (silu * upper).astype(BF)
        R.z_buf[i // 2, lax.rem(i, 2), :, :, :, :, 0:FF] = z.reshape(2, 2, 4, 16, FF)
        dg = (grad * upper * (sigma + silu * (1.0 - sigma))).astype(BF)
        du = (grad * silu).astype(BF)
        drain.put(i, (x2 + mm(z, w_d[:, 0:D])).T)
        dh = mm(dg, w_g[...], NT) + mm(du, w_u[...], NT)
        for base, value in ((GATE_BASE, dg), (UP_BASE, du)):
            for k in range(3):
                part = mm(h, value[:, 512 * k : 512 * (k + 1)], TN)
                for t in range(4):
                    here = slice(base + (4 * k + t) * D, base + (4 * k + t + 1) * D)
                    R.wide[here, :] += part[:, 128 * t : 128 * (t + 1)]
        R.gain_two[...] += jnp.sum(dh * n2, axis=0, keepdims=True)
        scaled = dh * gain
        mean = jnp.sum(scaled * n2, axis=1, keepdims=True) * (1.0 / D)
        dx = c.astype(F32) + r2 * (scaled - n2 * mean)
        R.dx[rows, :] = dx
        do = mm(dx.astype(BF), w_o[:, 0:D], NT)
        pick = (lax.broadcasted_iota(jnp.int32, (8, 128), 0) == lane((8, 128)) // 64).astype(BF)
        for t in range(TILES):
            if t < TILES - 1:
                tile = do[:, 128 * t : 128 * (t + 1)]
            else:
                tile = jnp.concatenate([do[:, 512:576], jnp.zeros((BLOCK, 64), F32)], axis=1)
            tile = tile.astype(BF)
            R.do[t, rows, :] = tile
            product = tile.astype(F32) * o[:, 128 * t : 128 * (t + 1)].astype(F32)
            high = product.astype(BF)
            low = (product - high.astype(F32)).astype(BF)
            inner = mm(pick, high, NT) + mm(pick, low, NT)
            R.inner[2 * t, :, rows] = inner[0:1]
            if t < TILES - 1:
                R.inner[2 * t + 1, :, rows] = inner[1:2]
        return 0

    lax.fori_loop(0, SEQ // BLOCK, body, 0)
    drain.finish()


def down_gradient(R, dest):
    for k in range(3):
        dest[512 * k : 512 * (k + 1), 0:D] = mm(read_z(R.z_buf, 512 * k, 512), R.cot[...], TN).astype(BF)
    dest[:, D:] = jnp.zeros((FF, 640 - D), BF)


def out_gradient(R, dest):
    for t in range(TILES):
        part = mm(R.o[t], R.dx[...].astype(BF), TN).astype(BF)
        rows = min(128, D - 128 * t)
        dest[128 * t : 128 * t + rows, 0:D] = part[0:rows]
    dest[:, D:] = jnp.zeros((D, 640 - D), BF)


def attend_back_group(g, R, between):
    for h in range(HEADS // KV_HEADS):
        j = 3 * g + h
        t, parity = j // 2, lax.rem(j, 2)
        for i in range(SEQ // BLOCK):
            start = BLOCK * i
            rows = slice(start, start + BLOCK)
            key = own_lanes(R.k[g, rows, :], parity)
            value = own_lanes(R.v[g, rows, :], parity)
            query, grad = R.q[t, start:, :], R.do[t, start:, :]
            probs = jnp.exp2(mm(key, query, NT) * LOG2E - R.lse[j, :, start:])
            down = lax.broadcasted_iota(jnp.int32, (BLOCK, BLOCK), 0)
            across = lax.broadcasted_iota(jnp.int32, (BLOCK, BLOCK), 1)
            corner = jnp.where(across >= down, probs[:, :BLOCK], 0.0)
            probs = jnp.concatenate([corner, probs[:, BLOCK:]], axis=1) if start + BLOCK < SEQ else corner
            ds = (probs * (mm(value, grad, NT) - R.inner[j, :, start:])).astype(BF)
            place = (2 * g + parity) * SEQ + start
            R.wide[pl.ds(pl.multiple_of(DV_BASE + place, BLOCK), BLOCK), :] += mm(probs.astype(BF), grad)
            R.wide[pl.ds(pl.multiple_of(DK_BASE + place, BLOCK), BLOCK), :] += mm(ds, query)
            R.wide[pl.ds(pl.multiple_of(t * SEQ + start, BLOCK), SEQ - start), :] += mm(ds, key, TN)
        for number in range(h, len(between), HEADS // KV_HEADS):
            if between[number] is not None:
                pl.when(j == number)(between[number])


def attend_back_all(R, between=()):
    R.wide[...] = jnp.zeros_like(R.wide)

    def body(g, _):
        attend_back_group(g, R, between)
        return 0

    lax.fori_loop(0, KV_HEADS, body, 0)


def heads_out(R):
    def body(i, _):
        rows = block_rows(i)
        cosine, sine = R.cos[rows, :], R.sin[rows, :]
        for t in range(TILES):
            tile = R.wide[pl.ds(pl.multiple_of(t * SEQ + i * BLOCK, BLOCK), BLOCK), :] * HEAD_DIM ** (-0.5)
            R.do[t, rows, :] = rotate_tile(tile, cosine, sine, True).astype(BF)
        low = lane((BLOCK, 128)) < 64
        for base, column, rotary in ((DK_BASE, 0, True), (DV_BASE, 256, False)):
            whole = []
            for g in range(KV_HEADS):
                parts = [
                    R.wide[pl.ds(pl.multiple_of(base + (2 * g + p) * SEQ + i * BLOCK, BLOCK), BLOCK), :]
                    for p in range(2)
                ]
                whole.append(parts[0] + turn(parts[1]))
            tiles = (jnp.where(low, whole[0], turn(whole[1])), jnp.where(low, whole[2], 0.0))
            for half in range(2):
                tile = rotate_tile(tiles[half], cosine, sine, True) if rotary else tiles[half]
                R.cot[rows, column + 128 * half : column + 128 * (half + 1)] = tile.astype(BF)
        return 0

    lax.fori_loop(0, SEQ // BLOCK, body, 0)


def first_gradients(R, gain, dest_q, dest_kv):
    a = R.a[...]
    products = jnp.zeros((D, 128), F32)
    for t in range(TILES):
        columns = slice(128 * t, 128 * (t + 1))
        part = mm(a, R.do[t], TN)
        products = products + part * R.nat_q[:, columns].astype(F32)
        dest_q[:, columns] = part.astype(BF)
    for t in range(4):
        columns = slice(128 * t, 128 * (t + 1))
        part = mm(a, R.cot[:, columns], TN)
        products = products + part * R.nat_kv[:, columns].astype(F32)
        dest_kv[:, columns] = part.astype(BF)
    ones = jnp.ones((8, 128), BF)
    high = products.astype(BF)
    low = (products - high.astype(F32)).astype(BF)
    R.gain_one[...] = (mm(ones, high, NT) + mm(ones, low, NT))[0:1, :] / gain


def input_gradient(R, gain, drain):
    def body(i, _):
        rows = block_rows(i)
        dq = jnp.concatenate([R.do[t, rows, :] for t in range(TILES)], axis=1)
        da = mm(dq, R.nat_q[...], NT) + mm(R.cot[rows, 0:512], R.nat_kv[...], NT)
        x = R.tok[rows, :].astype(F32)
        r1 = row_scale(x)
        n1 = x * r1
        scaled = da * gain
        mean = jnp.sum(scaled * n1, axis=1, keepdims=True) * (1.0 / D)
        drain.put(i, (R.dx[rows, :] + r1 * (scaled - n1 * mean)).T)
        return 0

    lax.fori_loop(0, SEQ // BLOCK, body, 0)
    drain.finish()


LAYER_SCRATCH = {
    "nat_q": ((D, 640), BF),
    "nat_kv": ((D, 512), BF),
    "nat_o": ((D, 640), BF),
    "nat_g": ((D, FF), BF),
    "nat_u": ((D, FF), BF),
    "nat_d": ((FF, 640), BF),
    "gains": ((1, 2 * D), F32),
    "tok": ((SEQ, D), BF),
    "cot": ((SEQ, D), BF),
    "a": ((SEQ, D), BF),
    "cos": ((SEQ, 128), F32),
    "sin": ((SEQ, 128), F32),
    "q": ((TILES, SEQ, 128), BF),
    "k": ((KV_HEADS, SEQ, 128), BF),
    "v": ((KV_HEADS, SEQ, 128), BF),
    "lse": ((HEADS, 1, SEQ), F32),
    "inner": ((HEADS, 1, SEQ), F32),
    "o": ((TILES, SEQ, 128), BF),
    "do": ((TILES, SEQ, 128), BF),
    "dx": ((SEQ, D), F32),
    "wide": ((WIDE_ROWS, 128), F32),
    "gain_one": ((1, D), F32),
    "gain_two": ((1, D), F32),
}


def layer_scratch():
    return [pltpu.VMEM(*s) for s in LAYER_SCRATCH.values()] + [
        pltpu.SemaphoreType.DMA((2,)),
        pltpu.SemaphoreType.DMA((2, 2)),
    ]


def layer_refs(refs, z_buf):
    names = list(LAYER_SCRATCH) + ["in_sems", "out_sems"]
    return types.SimpleNamespace(z_buf=z_buf, **dict(zip(names, refs)))


def nothing():
    return None


def run_layer(R, tok_t, positions, cot_t, freqs, out_t, grad_t, steps):
    copies = [
        pltpu.make_async_copy(tok_t, R.nat_g.at[:, 0:SEQ], R.in_sems.at[0]),
        pltpu.make_async_copy(cot_t, R.nat_u.at[:, 0:SEQ], R.in_sems.at[1]),
    ]
    for copy in copies:
        copy.start()
    steps.begin()
    make_tables(positions, freqs, R.cos, R.sin)
    copies[0].wait()
    turn_over(R.nat_g, R.tok)
    copies[1].wait()
    turn_over(R.nat_u, R.cot)
    R.wide[...] = jnp.zeros_like(R.wide)
    steps.first_weights()
    normalize_tokens(R.tok, R.gains[:, 0:D], R.a)
    heads_in(R.a, R.nat_q, R.nat_kv, R.cos, R.sin, R.q, R.k, R.v, steps.heads)
    attend_all(R.q, R.k, R.v, R.o, R.lse, steps.forward)
    steps.second_weights()
    feed_forward(R, R.gains[:, D : 2 * D], Drain(R.wide, R.out_sems, out_t))
    steps.after_feed_forward()
    attend_back_all(R, steps.backward)
    heads_out(R)
    steps.after_attention()
    steps.end(lambda: input_gradient(R, R.gains[:, 0:D], Drain(R.wide, R.out_sems, grad_t)))


def local_kernel(tok_t, positions, cot_t, freqs, gains, w_q, w_kv, w_o, w_g, w_u, w_d, *refs):
    out_t, grad_t, g_q, g_kv, g_o, g_g, g_u, g_d, gain_one, gain_two = refs[:10]
    R = layer_refs(refs[11:], refs[10])

    def first_weights():
        R.nat_q[...] = w_q[...]
        R.nat_kv[...] = w_kv[...]
        R.gains[...] = gains[...]

    def second_weights():
        R.nat_o[...] = w_o[...]
        R.nat_g[...] = w_g[...]
        R.nat_u[...] = w_u[...]
        R.nat_d[...] = w_d[...]

    def after_feed_forward():
        down_gradient(R, g_d)
        out_gradient(R, g_o)
        for dest, base in ((g_g, GATE_BASE), (g_u, UP_BASE)):
            for t in range(12):
                dest[:, 128 * t : 128 * (t + 1)] = R.wide[base + t * D : base + (t + 1) * D, :].astype(BF)

    def after_attention():
        first_gradients(R, R.gains[:, 0:D], g_q, g_kv)
        gain_one[...] = R.gain_one[...]
        gain_two[...] = R.gain_two[...]

    steps = types.SimpleNamespace(
        begin=nothing,
        first_weights=first_weights,
        heads=(),
        forward=(),
        second_weights=second_weights,
        after_feed_forward=after_feed_forward,
        backward=(),
        after_attention=after_attention,
        end=lambda last: last(),
    )
    run_layer(R, tok_t, positions, cot_t, freqs, out_t, grad_t, steps)


def hbm():
    return pl.BlockSpec(memory_space=pl.ANY)


def layer_inputs(tokens, positions, cotangent):
    return tokens.T, positions.reshape(-1, 128), cotangent.T, jnp.asarray(frequencies())


def layer(tokens, positions, cotangent, gains, *natural):
    shape = jax.ShapeDtypeStruct
    args = (*layer_inputs(tokens, positions, cotangent), gains, *natural)
    grads = [shape(v.shape, BF) for v in natural]
    outs = pl.pallas_call(
        local_kernel,
        out_shape=(shape((D, SEQ), F32), shape((D, SEQ), F32), *grads, shape((1, D), F32), shape((1, D), F32)),
        in_specs=[hbm(), vmem(), hbm(), vmem()] + [vmem()] * 7,
        out_specs=(hbm(), hbm()) + (vmem(),) * 8,
        scratch_shapes=[pltpu.VMEM((2, 2, 2, 2, 4) + group_shape(("g",)), BF)] + layer_scratch(),
        compiler_params=pltpu.CompilerParams(vmem_limit_bytes=VMEM_LIMIT),
        name="layer",
    )(*args)
    return outs[0].T, outs[1].T, outs[2:8], outs[8], outs[9]


OWNERS = {"q": 20, "kv": 12, "o": 16, "g": 8, "u": 18, "d": 14}
UNIT_NAMES = ("q", "kv", "o", "g", "u", "d")


class Reduce:
    def __init__(self, buf, r1, r2, r3, r4, send, recv, where):
        self.buf, self.r1, self.r2, self.r3, self.r4 = buf, r1, r2, r3, r4
        self.send, self.recv = send, recv
        self.me, (self.z, self.a, self.b, self.c), self.peer_a, self.peer_b, self.sibling, self.along = where

    def copy(self, k):
        if k < 2:
            half = 1 - self.b if k == 0 else self.b
            src, dst, target = self.buf.at[1 - self.c, half], self.r1.at[half], self.sibling
        elif k == 2:
            src, dst, target = self.buf.at[self.c, 1 - self.a], self.r2, self.peer_a
        elif k == 3:
            src, dst, target = self.buf.at[self.c, self.a, 1 - self.b], self.r3, self.peer_b
        else:
            step = k - 3
            src = self.buf.at[self.c, self.a, self.b, lax.rem(self.z + step, 4)]
            dst, target = self.r4.at[step - 1], self.along(step)
        return remote(src, dst, self.send.at[k], self.recv.at[k], target)

    def stage_one(self):
        self.copy(0).start()
        self.copy(1).start()

    def add(self, index, got):
        self.buf[index] = self.buf[index] + got

    def stage_two(self):
        self.copy(0).wait_recv()
        self.add((self.c, 1 - self.a), self.r1[1 - self.a])
        self.copy(2).start()
        self.copy(1).wait_recv()
        self.add((self.c, self.a), self.r1[self.a])

    def stage_three(self):
        self.copy(2).wait_recv()
        self.add((self.c, self.a, 1 - self.b), self.r2[1 - self.b])
        self.copy(3).start()
        self.add((self.c, self.a, self.b), self.r2[self.b])

    def stage_four(self):
        self.copy(3).wait_recv()
        self.add((self.c, self.a, self.b), self.r3[...])
        for step in (1, 3, 2):
            self.copy(3 + step).start()

    def result(self, total):
        for step in (1, 3, 2):
            self.copy(3 + step).wait_recv()
        own = self.buf[self.c, self.a, self.b, self.z].astype(F32)
        total[...] = (
            own + self.r4[0].astype(F32) + self.r4[1].astype(F32) + self.r4[2].astype(F32)
        )

    def finish(self):
        for k in range(7):
            self.copy(k).wait_send()


def diagonal(n):
    return lax.broadcasted_iota(jnp.int32, (n, n), 0) == lax.broadcasted_iota(jnp.int32, (n, n), 1)


OWN_WIDTH = 1920
NS_BASE = TILES * SEQ


def slab_width(name):
    return 640 if name == "d" else unit_width(name)


def own_width(name):
    return OWN_WIDTH if name == "d" else unit_width(name)


def own_slab_value(name, ref):
    value = ref[...]
    if name == "d":
        return jnp.concatenate([value[:, 640 * k : 640 * (k + 1)] for k in range(3)], axis=0)
    return value


def sum_squares(value):
    return jnp.sum(jnp.sum(value * value, axis=1, keepdims=True), axis=0, keepdims=True)


def on_diagonal(first, rows, n, value):
    row = lax.broadcasted_iota(jnp.int32, (rows, n), 0) + first
    return jnp.where(row == lane((rows, n)), value, 0.0)


def newton_schulz(wide, low, columns, e_ref, r_ref, between=()):
    first, last = columns
    rows = low.shape[0]
    width = last - first
    tiles = (width + 127) // 128
    tall = rows > width
    n = width if tall else rows
    cuts = [(top, min(256, n - top)) for top in range(0, n, 256)]

    def here(t):
        return pl.ds(NS_BASE + t * rows, rows)

    def put(ref, top, p, corner, value):
        ref[top : top + p, top : top + p] = (value[:, 0:p] - jnp.where(diagonal(p), corner, 0.0)).astype(BF)
        if top + p < n:
            beside = value[:, p:].astype(BF)
            ref[top : top + p, top + p : n] = beside
            ref[top + p : n, top : top + p] = beside.T

    total = jnp.zeros((1, 1), F32)
    for t in range(tiles):
        value = low[:, first + 128 * t : first + 128 * (t + 1)].astype(F32)
        wide[here(t), :] = value
        total = total + sum_squares(value)
    scale = 1.0 / (jnp.sqrt(total) + 1e-07)
    for t in range(tiles):
        wide[here(t), :] = wide[here(t), :] * scale

    def step(number, squares):
        for t in range(tiles):
            low[:, first + 128 * t : first + 128 * (t + 1)] = wide[here(t), :].astype(BF)
        state = low[:, first:last]
        mean = squares * (1.0 / n)
        total = jnp.zeros((1, 1), F32)
        for top, p in cuts:
            if tall:
                gram = mm(state[:, top : top + p], state[:, top:], TN)
            else:
                gram = mm(state[top : top + p], state[top:], NT)
            put(e_ref, top, p, mean, gram)
            total = total + sum_squares(gram[:, 0:p] - jnp.where(diagonal(p), mean, 0.0))
            if top + p < n:
                total = total + 2.0 * sum_squares(gram[:, p:])
        more = total * (coef_three / n)
        slope = coef_two + 2.0 * coef_three * mean
        whole = e_ref[0:n, 0:n]
        for top, p in cuts:
            rest = e_ref[top : top + p, 0:n]
            put(r_ref, top, p, more, slope * rest[:, top:].astype(F32) + coef_three * mm(rest, whole[:, top:]))
        keep = coef_one + coef_two * mean + coef_three * mean * mean + more
        poly = r_ref[0:n, 0:n]
        total = jnp.zeros((1, 1), F32)
        for left in range(0, width, 256):
            w = min(256, width - left)
            if tall:
                change = mm(state, poly[:, left : left + w])
            else:
                change = mm(poly, state[:, left : left + w])
            for k in range((w + 127) // 128):
                t = left // 128 + k
                part = change[:, 128 * k : min(128 * (k + 1), w)]
                if part.shape[1] < 128:
                    part = jnp.concatenate([part, jnp.zeros((rows, 128 - part.shape[1]), F32)], axis=1)
                value = keep * wide[here(t), :] + part
                wide[here(t), :] = value
                total = total + sum_squares(value)
        for when, action in enumerate(between):
            pl.when(number == when)(action)
        return total

    lax.fori_loop(0, NS_ITERS, step, total * scale * scale)
    for t in range(tiles):
        low[:, first + 128 * t : first + 128 * (t + 1)] = wide[here(t), :].astype(BF)


def whole_kernel(*refs):
    tok_t, positions, cot_t, freqs = refs[0:4]
    w, gains_ref = refs[4:11], refs[11]
    m, m_gains = refs[12:19], refs[19]
    spread_ref, collect_ref, select_ref, lanes_ref, lanes_back, gain_put = refs[20:26]
    out_t, grad_t = refs[26:28]
    totals = refs[28:33]
    directions = dict(zip(UNIT_NAMES, refs[33:39]))
    k = 39
    bufs, z_buf = group_buffers(refs[k : k + 4]), refs[k + 2]
    r1, r2, r3, r4 = (refs[k + 4 + 5 * j : k + 9 + 5 * j] for j in range(4))
    k += 24
    scr, fold_scr, lane_scr = refs[k : k + 3]
    k += 3
    old = dict(zip(UNIT_NAMES, refs[k : k + 6]))
    mslab = dict(zip(UNIT_NAMES, refs[k + 6 : k + 12]))
    oslab = dict(zip(UNIT_NAMES, refs[k + 12 : k + 18]))
    k += 18
    held = refs[k]
    R = layer_refs(refs[k + 1 : k + 3 + len(LAYER_SCRATCH)], z_buf)
    k += 3 + len(LAYER_SCRATCH)
    ag_send, ag_recv, rs_send, rs_recv, up_send, up_recv, down_send, down_recv = refs[k : k + 8]

    where = coords()
    me, (z, a, b, c), peer_a, peer_b, sibling, along = where
    own = (c, a, b, z)
    natural = {"q": R.nat_q, "kv": R.nat_kv, "o": R.nat_o, "g": R.nat_g, "u": R.nat_u}
    gathers = [Gather(buf, ag_send.at[n], ag_recv.at[n], where) for n, buf in enumerate(bufs)]
    late = gathers[1:]
    sums = [Reduce(bufs[g], r1[g], r2[g], r3[g], r4[g], rs_send.at[g], rs_recv.at[g], where) for g in range(5)]
    QKV, OUT, GATE, UP, DOWN = range(5)

    def pack_group(n):
        for name in GROUPS[n]:
            load_unit(name, w, scr)
            own_gains = None
            if name == "q":
                fold_scr[0:1, 0:128] = jnp.zeros((1, 128), F32)
                fold_scr[0:1, 0:36] = gains_ref[...]
                own_gains = fold_scr[0:1, 0:128]
            pack_slab(name, scr, fold_scr, bufs[n].at[own], unit_offset(name), own_gains)

    def begin():
        barrier = pltpu.get_barrier_semaphore()

        def hello(j, _):
            @pl.when(j != me)
            def _():
                pl.semaphore_signal(barrier, inc=1, device_id=(j,), device_id_type=MESH)

            return 0

        lax.fori_loop(0, 32, hello, 0)
        pack_group(QKV)
        pl.semaphore_wait(barrier, 31)
        gathers[QKV].phase_own()
        for n in (OUT, GATE, UP, DOWN):
            pack_group(n)
            gathers[n].phase_own()
        lane_scr[0:1, :] = jnp.zeros((1, 128), F32)
        lane_scr[0:1, 0:36] = m_gains[...]
        for name in UNIT_NAMES:
            load_unit(name, m, scr)
            pack_slab(name, scr, fold_scr, old[name], 0, lane_scr[0:1, :] if name == "q" else None)

    o_in, g_in, u_in, d_in = late

    def in_turn(*actions):
        def run():
            for action in actions:
                action()

        return run

    def first_weights():
        qkv = gathers[QKV]
        qkv.from_z(1, 3, 2)
        qkv.from_b(0, 1, 3, 2)
        o_in.from_z(1, 3)
        qkv.from_a(False, 0, 1, 3, 2)
        qkv.from_a(True, 0, 1, 3, 2)
        o_in.from_z(2)
        o_in.from_b(0)
        g_in.from_z(1, 3, 2)
        g_in.from_b(0)
        u_in.from_z(1, 3)
        qkv.phase_sibling()
        for name in GROUPS[QKV]:
            spread(name, bufs[QKV], unit_offset(name), spread_ref, natural[name])
        read_gains(bufs[QKV], select_ref, lanes_ref, R.gains)

    def in_block_0():
        u_in.from_z(2)
        u_in.from_b(0)
        d_in.from_z(1, 3)
        o_in.from_b(1, 3, 2)

    def in_block_1():
        g_in.from_b(1, 3)
        d_in.from_b(0)

    def in_block_2():
        d_in.from_z(2)
        o_in.from_a(False, 0, 1, 3, 2)

    def in_block_3():
        g_in.from_b(2)
        u_in.from_b(1, 3)

    def in_head_0():
        g_in.from_a(False, 0, 1, 3)
        o_in.from_a(True, 0, 1, 3, 2)

    def in_head_1():
        u_in.from_b(2)
        d_in.from_b(1, 3)

    def in_head_2():
        g_in.from_a(False, 2)
        g_in.from_a(True, 0, 1)

    def in_head_3():
        d_in.from_b(2)
        u_in.from_a(False, 0, 1, 3)

    def in_head_4():
        g_in.from_a(True, 3, 2)

    def in_head_5():
        u_in.from_a(False, 2)
        u_in.from_a(True, 0, 1)

    def in_head_6():
        d_in.from_a(False, 0, 1, 3)

    def in_head_7():
        u_in.from_a(True, 3, 2)

    def in_head_8():
        d_in.from_a(False, 2)
        d_in.from_a(True, 0, 1, 3, 2)

    def second_weights():
        for n in (OUT, GATE, UP):
            gathers[n].phase_sibling()
            for name in GROUPS[n]:
                spread(name, bufs[n], unit_offset(name), spread_ref, natural[name])
        gathers[DOWN].phase_sibling()
        spread_down(bufs[DOWN], R.nat_d)
        for move in gathers:
            move.finish()

    def collect_wide(n, base):
        def read(rows, q, fold):
            tiles = [R.wide[pl.ds(pl.multiple_of(rows + base + (2 * q + s) * D, 16), 144), :] for s in range(2)]
            return jnp.concatenate(tiles, axis=1).astype(BF)

        collect(GROUPS[n][0], read, bufs[n], 0, collect_ref)

    def after_feed_forward():
        down_gradient(R, R.nat_d)
        collect_down(R.nat_d, bufs[DOWN])
        sums[DOWN].stage_one()
        collect_wide(GATE, GATE_BASE)
        sums[GATE].stage_one()
        sums[DOWN].stage_two()
        collect_wide(UP, UP_BASE)
        sums[UP].stage_one()
        sums[GATE].stage_two()
        out_gradient(R, R.nat_o)
        sums[UP].stage_two()
        collect("o", reader(R.nat_o), bufs[OUT], 0, collect_ref)
        sums[OUT].stage_one()

    def to_owner(name):
        number, owner, width = UNIT_NAMES.index(name), OWNERS[name], own_width(name)
        target = held.at[c, a, b, z, :, pl.ds(0, width)]

        @pl.when(me != owner)
        def _():
            remote(mslab[name], target, up_send.at[number], up_recv.at[slot(*own)], owner).start()

        @pl.when(me == owner)
        def _():
            held[c, a, b, z, :, 0:width] = mslab[name][...]

    def settle(n):
        sums[n].result(totals[n])
        for name in GROUPS[n]:
            off = unit_offset(name)
            fresh = (momentum_decay * old[name][...] + totals[n][:, off : off + slab_width(name)]).astype(BF)
            if name == "d":
                for k3 in range(3):
                    mslab[name][:, 640 * k3 : 640 * (k3 + 1)] = fresh[16 * k3 : 16 * (k3 + 1), :]
            else:
                mslab[name][...] = fresh
            to_owner(name)

    def both(one, other):
        def run():
            one()
            other()

        return run

    def after_attention():
        grad_q, grad_kv = R.nat_u.at[:, 0:640], R.nat_g.at[:, 0:512]
        first_gradients(R, R.gains[:, 0:D], grad_q, grad_kv)
        settle(UP)
        row = lax.broadcasted_iota(jnp.int32, (32, 2 * D), 0) * 36
        col = lane((32, 2 * D))
        keep = jnp.logical_and(col >= row, col < row + 36)
        both_gains = jnp.concatenate([R.gain_one[...], R.gain_two[...]], axis=1)
        chosen = jnp.where(keep, jnp.broadcast_to(both_gains, (32, 2 * D)), 0.0).astype(BF)
        by_device = mm(chosen, lanes_back[...]).astype(BF)
        collect("kv", reader(grad_kv), bufs[QKV], unit_offset("kv"), collect_ref)
        collect("q", reader(grad_q), bufs[QKV], unit_offset("q"), collect_ref, lambda zz: mm(gain_put[zz], by_device))
        sums[QKV].stage_one()
        settle(OUT)
        sums[QKV].stage_two()
        sums[QKV].stage_three()

    def arrived(width):
        def one(j, _):
            @pl.when(j != slot(*own))
            def _():
                ref = held.at[j // 16, lax.rem(j // 8, 2), lax.rem(j // 4, 2), lax.rem(j, 4), :, pl.ds(0, width)]
                remote(ref, ref, up_send.at[0], up_recv.at[j], sibling).wait_recv()

            return 0

        lax.fori_loop(0, 32, one, 0)

    def give_plane(name, zz, wait):
        width = own_width(name)

        def one(p, _):
            cc, aa, bb = p // 4, lax.rem(p // 2, 2), lax.rem(p, 2)
            y = aa * (1 - cc) + bb * cc
            x = bb * (1 - cc) + aa * cc
            target = ((zz * 2 + y) * 2 + x) * 2 + cc
            ref = held.at[cc, aa, bb, zz, :, pl.ds(0, width)]
            j = slot(cc, aa, bb, zz)

            @pl.when(j != slot(*own))
            def _():
                copy = remote(ref, oslab[name], down_send.at[j], down_recv.at[UNIT_NAMES.index(name)], target)
                if wait:
                    copy.wait_send()
                else:
                    copy.start()

            return 0

        lax.fori_loop(0, 8, one, 0)

    def far_first(number):
        return lax.rem(number + 2 * (1 - z // 2), 4)

    def give(names):
        def after(zz):
            for name in names:
                pl.when(me == OWNERS[name])(lambda name=name: give_plane(name, zz, False))

        return after

    def give_rest(names):
        for name in names:
            @pl.when(me == OWNERS[name])
            def _(name=name):
                oslab[name][...] = held[c, a, b, z, :, 0 : own_width(name)]

                def plane(zz, _):
                    give_plane(name, zz, True)
                    return 0

                lax.fori_loop(0, 4, plane, 0)

    e_ref, r_ref = R.nat_u.at[:, 0:640], R.nat_u.at[:, 640:1280]

    def is_owner(*names):
        hit = me == OWNERS[names[0]]
        for name in names[1:]:
            hit = jnp.logical_or(hit, me == OWNERS[name])
        return hit

    def end(input_gradients):
        large = is_owner("g", "u", "d")

        meanwhile = (lambda: settle(QKV),)
        sums[QKV].stage_four()

        @pl.when(jnp.logical_not(large))
        def _():
            input_gradients()
            settle(QKV)

        @pl.when(is_owner("g", "u"))
        def _():
            arrived(own_width("g"))
            spread("g", held, 0, spread_ref, R.nat_g)
            newton_schulz(R.wide, R.nat_g, (0, FF), e_ref, r_ref, meanwhile)
            collect("g", reader(R.nat_g), held, 0, collect_ref, None, give(("g", "u")), far_first)

        @pl.when(is_owner("d"))
        def _():
            arrived(own_width("d"))
            spread_own_down(held, R.nat_d)
            newton_schulz(R.wide, R.nat_d, (0, D), e_ref, r_ref, meanwhile)
            collect_own_down(R.nat_d, held)
            for number in range(4):
                give_plane("d", far_first(number), False)

        @pl.when(large)
        def _():
            input_gradients()
            give_rest(("g", "u", "d"))

        @pl.when(is_owner("q", "o"))
        def _():
            arrived(own_width("q"))
            spread("q", held, 0, spread_ref, R.nat_q)
            rows_of = gain_rows(held[:, :, :, :, :, 640:768].reshape(512, 128), select_ref)
            squares = jnp.sum(rows_of * rows_of, axis=1, keepdims=True)
            scales = [
                lax.rsqrt(jnp.sum(squares[16 * h : 16 * h + 16], axis=0, keepdims=True) * (1.0 / D) + 1e-06)
                for h in range(2)
            ]
            newton_schulz(R.wide, R.nat_q, (0, 640), e_ref, r_ref)

            def scale_extra(zz):
                scale = jnp.where(zz < 2, scales[0], scales[1])
                high = scale.astype(BF).astype(F32)
                row16 = lax.rem(lax.broadcasted_iota(jnp.int32, (128, 128), 0), 16)
                return jnp.where(row16 == 7, high, 0.0) + jnp.where(row16 == 15, scale - high, 0.0)

            collect("q", reader(R.nat_q), held, 0, collect_ref, scale_extra, give(("q", "o")))
            give_rest(("q", "o"))

        @pl.when(is_owner("kv"))
        def _():
            arrived(own_width("kv"))
            spread("kv", held, 0, spread_ref, R.nat_kv)
            newton_schulz(R.wide, R.nat_kv, (0, KVD), e_ref, r_ref)
            newton_schulz(R.wide, R.nat_kv, (256, 256 + KVD), e_ref, r_ref)
            collect("kv", reader(R.nat_kv), held, 0, collect_ref, None, give(("kv",)))
            give_rest(("kv",))

        for name in ("d", "g", "u", "o", "kv", "q"):
            number = UNIT_NAMES.index(name)

            @pl.when(me != OWNERS[name])
            def _():
                remote(oslab[name], oslab[name], down_send.at[0], down_recv.at[number], sibling).wait_recv()

            directions[name][...] = oslab[name][...]

        for name in UNIT_NAMES:
            number = UNIT_NAMES.index(name)
            target = held.at[c, a, b, z, :, pl.ds(0, own_width(name))]

            @pl.when(me != OWNERS[name])
            def _():
                remote(mslab[name], target, up_send.at[number], up_recv.at[slot(*own)], OWNERS[name]).wait_send()

        for move in sums:
            move.finish()

    steps = types.SimpleNamespace(
        begin=begin,
        first_weights=first_weights,
        heads=(in_block_0, in_block_1, in_block_2, in_block_3),
        forward=(
            in_turn(in_head_0, in_head_1, in_head_2),
            in_turn(in_head_3, in_head_4, in_head_5),
            in_turn(in_head_6, in_head_7, in_head_8),
        ),
        second_weights=second_weights,
        after_feed_forward=after_feed_forward,
        backward=(
            sums[DOWN].stage_three,
            sums[OUT].stage_two,
            both(sums[DOWN].stage_four, sums[GATE].stage_three),
            None,
            both(sums[GATE].stage_four, sums[UP].stage_three),
            lambda: settle(DOWN),
            both(sums[UP].stage_four, sums[OUT].stage_three),
            lambda: settle(GATE),
            sums[OUT].stage_four,
        ),
        after_attention=after_attention,
        end=end,
    )
    run_layer(R, tok_t, positions, cot_t, freqs, out_t, grad_t, steps)


def collect_constants():
    forward = spread_matrices()
    put = np.zeros((4, 128, 32), np.float32)
    for zz in range(4):
        for d in range(8):
            put[zz, 16 * place_of(d) + 7, 8 * zz + d] = 1
    low = ml_dtypes.bfloat16
    return (
        forward.astype(low),
        forward.transpose(0, 2, 1).astype(low),
        gain_select().astype(low),
        gain_lanes().astype(low),
        gain_lanes().T.astype(low),
        put.astype(low),
    )


def whole_call(tokens, positions, cotangent, w, gains, m, m_gains):
    shape = jax.ShapeDtypeStruct
    args = (*layer_inputs(tokens, positions, cotangent), *w, gains, *m, m_gains, *collect_constants())
    stages = []
    for lead in ((2, 2, 4), (2, 4), (4,), (3,)):
        stages += [pltpu.VMEM(lead + group_shape(group), BF) for group in GROUPS]
    travel = [pltpu.VMEM((16, own_width(n)), BF) for n in UNIT_NAMES]
    outs = (
        [shape((D, SEQ), F32)] * 2
        + [shape(group_shape(group), F32) for group in GROUPS]
        + [shape((16, own_width(n)), BF) for n in UNIT_NAMES]
    )
    return pl.pallas_call(
        whole_kernel,
        out_shape=tuple(outs),
        in_specs=[hbm(), vmem(), hbm()] + [vmem()] * (len(args) - 3),
        out_specs=(hbm(), hbm()) + (vmem(),) * 11,
        scratch_shapes=slab_buffers()
        + stages
        + [pltpu.VMEM((12, 48, 128), F32), pltpu.VMEM((16, 256), F32), pltpu.VMEM((8, 128), F32)]
        + [pltpu.VMEM((ROWS_D, 640) if n == "d" else (16, unit_width(n)), F32) for n in UNIT_NAMES]
        + travel
        + travel
        + [pltpu.VMEM((2, 2, 2, 4, 16, OWN_WIDTH), BF)]
        + layer_scratch()
        + [
            pltpu.SemaphoreType.DMA((5, 31)),
            pltpu.SemaphoreType.DMA((5, 32)),
            pltpu.SemaphoreType.DMA((5, 7)),
            pltpu.SemaphoreType.DMA((5, 7)),
            pltpu.SemaphoreType.DMA((6,)),
            pltpu.SemaphoreType.DMA((32,)),
            pltpu.SemaphoreType.DMA((32,)),
            pltpu.SemaphoreType.DMA((6,)),
        ],
        compiler_params=pltpu.CompilerParams(
            collective_id=0, has_side_effects=True, vmem_limit_bytes=VMEM_LIMIT
        ),
        name="layer_and_step",
    )(*args)


PIECES = 4


def finish_kernel(*refs):
    large = refs[0:2]
    totals = refs[2:7]
    directions = dict(zip(UNIT_NAMES, refs[7:13]))
    w, gains = refs[13:20], refs[20]
    m, m_gains = refs[21:28], refs[28]
    large_out = refs[29:31]
    grad_out, grad_gains = refs[31:38], refs[38]
    new_m, new_m_gains = refs[39:46], refs[46]
    new_w, new_gains = refs[47:54], refs[54]
    scr, fold_scr, through, sems = refs[55:59]
    shapes = matrix_shapes()
    arrivals, departures = [], []
    for k in range(2):
        for n in range(PIECES):
            rows = pl.ds(n * (D // PIECES), D // PIECES)
            arrivals.append(pltpu.make_async_copy(large[k].at[rows], through.at[k, rows], sems.at[0, k, n]))
            departures.append(pltpu.make_async_copy(through.at[k, rows], large_out[k].at[rows], sems.at[1, k, n]))
    for copy in arrivals:
        copy.start()
    for n, (group, total) in enumerate(zip(GROUPS, totals)):
        for k in range(2 * PIECES * n // len(GROUPS), 2 * PIECES * (n + 1) // len(GROUPS)):
            arrivals[k].wait()
            departures[k].start()
        for name in group:
            off = unit_offset(name)
            unpack_slab(name, total[:, off : off + slab_width(name)], scr, fold_scr)
            for index, tile, tiles2, rows in PARTS[name]:
                store_rows(scr, grad_out[index], rows, tiles2, tile)
                new_m[index][...] = momentum_decay * m[index][...] + grad_out[index][...]
            if name == "q":
                grad_gains[...] = fold_scr[7:8, 0:36]
                new_m_gains[...] = momentum_decay * m_gains[...] + grad_gains[...]
            unpack_slab(name, own_slab_value(name, directions[name]).astype(F32), scr, fold_scr)
            for index, tile, tiles2, rows in PARTS[name]:
                store_rows(scr, new_w[index], rows, tiles2, tile)
                rate = 0.2 * math.sqrt(max(shapes[index]))
                old = w[index][...]
                new_w[index][...] = old - matrix_rate * (weight_decay * old + rate * new_w[index][...])
            if name == "q":
                scale = fold_scr[7:8, 0:36] + fold_scr[15:16, 0:36]
                new_gains[...] = gains[...] - gain_rate * (new_m_gains[...] * scale)
    for copy in departures:
        copy.wait()


def finish_call(large, slabs, w, gains, m, m_gains):
    shape = jax.ShapeDtypeStruct
    outs = [shape(v.shape, F32) for v in large] + [shape(v.shape, F32) for v in (*w, gains)] * 3
    args = (*large, *slabs, *w, gains, *m, m_gains)
    return pl.pallas_call(
        finish_kernel,
        out_shape=tuple(outs),
        in_specs=[hbm()] * 2 + [vmem()] * (len(args) - 2),
        out_specs=(hbm(), hbm()) + (vmem(),) * 24,
        scratch_shapes=[
            pltpu.VMEM((12, 48, 128), F32),
            pltpu.VMEM((16, 256), F32),
            pltpu.VMEM((2, D, SEQ), F32),
            pltpu.SemaphoreType.DMA((2, 2, PIECES)),
        ],
        compiler_params=pltpu.CompilerParams(vmem_limit_bytes=VMEM_LIMIT),
        name="finish",
    )(*args)


def orthogonal(matrix):
    rows, cols = matrix.shape
    wide = matrix.T if rows > cols else matrix
    state = wide / (jnp.sqrt(jnp.sum(wide * wide)) + 1e-07)
    for turn_number in range(NS_ITERS):
        gram = jnp.dot(state, state.T, precision=precise)
        poly = coef_two * gram + coef_three * jnp.dot(gram, gram, precision=precise)
        state = coef_one * state + jnp.dot(poly, state, precision=precise)
    return state.T if rows > cols else state


def direction_of(index, flat):
    if index < 7:
        return orthogonal(flat.reshape(matrix_shapes()[index])).reshape(-1)
    halves = flat.reshape(2, D)
    return (halves * lax.rsqrt(jnp.mean(halves * halves, axis=1, keepdims=True) + 1e-06)).reshape(-1)


def gather_all(flat):
    return lax.all_gather(flat.astype(BF), "dp", axis=0, tiled=True)


def scatter_sum(whole):
    return lax.psum_scatter(whole, "dp", scatter_dimension=0, tiled=True)


def pad_columns(matrix, width):
    return jnp.pad(matrix, ((0, 0), (0, width - matrix.shape[1])))


def per_device(tokens, positions, cotangent, *rest):
    w, gains, m, m_gains = rest[0:7], rest[7], rest[8:15], rest[15]
    shapes = matrix_shapes()
    whole = [gather_all(v).reshape(s) for v, s in zip(w, shapes)]
    padded = (
        pad_columns(whole[0], 640),
        jnp.concatenate([pad_columns(whole[1], 256), pad_columns(whole[2], 256)], axis=1),
        pad_columns(whole[3], 640),
        whole[4],
        whole[5],
        pad_columns(whole[6], 640),
    )
    block_out, input_grad, grads, *gain_grads = layer(
        tokens, positions, cotangent, gather_all(gains).astype(F32).reshape(1, -1), *padded
    )
    parts = (
        grads[0][:, :D],
        grads[1][:, :KVD],
        grads[1][:, 256 : 256 + KVD],
        grads[2][:, :D],
        grads[3],
        grads[4],
        grads[5][:, :D],
    )
    shares = [scatter_sum(g.astype(F32).reshape(-1)) for g in parts] + [scatter_sum(jnp.concatenate(gain_grads, axis=1).reshape(-1))]
    moments = [momentum_decay * old + share for old, share in zip((*m, m_gains), shares)]
    device = lax.axis_index("dp")
    stride = lax.axis_size("dp") // 8
    pieces = []
    for i in range(8):
        full = gather_all(moments[i]).astype(F32)
        found = lax.cond(
            device == i * stride, lambda v, i=i: direction_of(i, v), jnp.zeros_like, full
        )
        pieces.append(scatter_sum(found))
    updated = []
    for i in range(7):
        scale = 0.2 * math.sqrt(max(shapes[i]))
        updated.append(w[i] - matrix_rate * (weight_decay * w[i] + scale * pieces[i]))
    new_gains = gains - gain_rate * pieces[7]
    return (block_out, input_grad, *moments, *updated, new_gains, *shares)


def per_device_32(tokens, positions, cotangent, *rest):
    w, gains, m, m_gains = rest[0:7], rest[7], rest[8:15], rest[15]
    w = [v.reshape(-1, 128) for v in w]
    m = [v.reshape(-1, 128) for v in m]
    gains, m_gains = gains.reshape(1, -1), m_gains.reshape(1, -1)
    out_t, grad_t, *slabs = whole_call(tokens, positions, cotangent, w, gains, m, m_gains)
    out_t, grad_t, *flat = finish_call((out_t, grad_t), slabs, w, gains, m, m_gains)
    flat = [v.reshape(-1) for v in flat]
    return (out_t.T, grad_t.T, *flat[8:16], *flat[16:24], *flat[0:8])


def solution(mesh):
    placed = (P("dp", None), P("dp"), P("dp", None)) + (P("dp"),) * 16
    return jax.shard_map(
        per_device_32 if mesh.shape["dp"] == 32 else per_device,
        mesh=mesh,
        in_specs=placed,
        out_specs=(P("dp", None), P("dp", None)) + (P("dp"),) * 24,
        check_vma=False,
    )
```
